32 devices in a mesh: ctx: 8 (over z, x), head: 4 (over y, core).
Axes of the slice: x: 2, y: 2, z: 4, core: 2. Of those that a mesh axis runs over, the one named last changes fastest.
Arguments:
- queries: bfloat16 [8192, 4096], P('ctx', 'head'), may hold values from -30 to 30
- keys: bfloat16 [8192, 4096], P('ctx', 'head'), may hold values from -30 to 30
- values: bfloat16 [8192, 4096], P('ctx', 'head'), may hold values from -14 to 14
- selection: int32 [32, 8], P('ctx'), may hold values from 0 to 31, as said below
- norm_gain: bfloat16 [4096], P('head'), may hold values from 0.099609375 to 1.8984375
Outputs:
- normed: bfloat16 [8192, 4096], P('ctx', 'head')
The draws below stay inside these ranges and needn't reach their ends.
Inputs may be any that keep to these rules, and one draw needn't show every extreme that they name: `selection`: row c lists span c's blocks: the first entry is c; every other entry is a distinct block earlier than c, or c again where no block is selected. Block b belongs to the device holding span b, which is b // 4. Among the entries after the first in the 4 rows of one device, at most 2 that differ from their row's span name blocks of any one device.
All inputs are finite; a program needn't handle non-finite values.
Results may differ from the reference program's by a relative error of at most 0.0052.
Values may be sent and summed in bfloat16 or wider, within the bound.
No kernel may reach another device: no remote copies, remote signals or barrier semaphores. Data moves between devices by JAX's collectives and lax.ppermute only.
A program may use at most 192 MiB of HBM per device.

```python
import jax
import jax.numpy as jnp
from jax import lax

HEADS = 32
HD = 128
BLOCK = 256
TOPK = 8
CAP = 2
BPD = 4
NBLK = 32
TOKENS = 8192


def draw_queries(key, part):
    key = jax.random.fold_in(key, 1)
    base = jnp.clip(jax.random.normal(key, (TOKENS, HEADS, HD), jnp.float32), -4.5, 4.5)
    return base.reshape(TOKENS, HEADS * HD).astype(jnp.bfloat16)


def draw_keys(key, part):
    key = jax.random.fold_in(key, 2)
    base = jnp.clip(jax.random.normal(key, (TOKENS, HEADS, HD), jnp.float32), -4.5, 4.5)
    return base.reshape(TOKENS, HEADS * HD).astype(jnp.bfloat16)


def draw_values(key, part):
    key = jax.random.fold_in(key, 3)
    head_scale = 0.3 * 10.0 ** (jnp.arange(HEADS, dtype=jnp.float32) / (HEADS - 1))
    base = jnp.clip(jax.random.normal(key, (TOKENS, HEADS, HD), jnp.float32), -4.5, 4.5)
    return (base * head_scale[None, :, None]).reshape(TOKENS, HEADS * HD).astype(jnp.bfloat16)


def draw_selection(key, part):
    key = jax.random.fold_in(key, 5)
    popularity = jax.random.randint(jax.random.fold_in(key, 1), (NBLK,), 0, 4).astype(jnp.int32)
    popularity = popularity.at[0].set(8)
    noise = jax.random.randint(jax.random.fold_in(key, 2), (NBLK, NBLK), 0, 1000).astype(jnp.int32)
    blocks = jnp.arange(NBLK, dtype=jnp.int32)
    ranking = (popularity[None, :] * 1000 + noise) * NBLK + blocks[None, :]
    device_count = NBLK // BPD

    def one_device(device):
        counts = jnp.zeros((device_count,), jnp.int32)
        row_list = []
        for inner in range(BPD):
            span = device * BPD + inner
            taken = jnp.zeros((NBLK,), jnp.bool_)
            entries = [span]
            for step in range(TOPK - 1):
                allowed = (blocks < span) & jnp.logical_not(taken) & (counts[blocks // BPD] < CAP)
                masked = jnp.where(allowed, ranking[span], -1)
                best_value, best_index = lax.top_k(masked, 1)
                best = best_index[0].astype(jnp.int32)
                usable = best_value[0] >= 0
                entries.append(jnp.where(usable, best, span).astype(jnp.int32))
                taken = taken.at[best].set(taken[best] | usable)
                counts = counts.at[best // BPD].add(usable.astype(jnp.int32))
            row_list.append(jnp.stack(entries))
        return jnp.stack(row_list)
    return jax.vmap(one_device)(jnp.arange(device_count, dtype=jnp.int32)).reshape(NBLK, TOPK).astype(jnp.int32)


def setup_inputs(seed: int = 0) -> dict:
    arg_keys = jax.random.split(jax.random.key(seed), 6)
    queries = draw_queries(jax.random.fold_in(arg_keys[5], 71), 0)
    keys = draw_keys(jax.random.fold_in(arg_keys[5], 71), 0)
    values = draw_values(jax.random.fold_in(arg_keys[5], 71), 0)
    selection = draw_selection(jax.random.fold_in(arg_keys[5], 71), 0)
    norm_gain = jnp.clip(1.0 + 0.18 * jax.random.normal(arg_keys[4], (HEADS * HD,), jnp.float32), 0.099609375, 1.8984375).astype(jnp.bfloat16)
    return dict(queries=queries, keys=keys, values=values, selection=selection, norm_gain=norm_gain)


def reference(queries, keys, values, selection, norm_gain):
    width = HEADS * HD
    query_blocks = queries.reshape(NBLK, BLOCK, HEADS, HD)
    key_blocks = keys.reshape(NBLK, BLOCK, HEADS, HD)
    value_blocks = values.reshape(NBLK, BLOCK, HEADS, HD)
    scale = HD ** (-0.5)
    positions = jnp.arange(BLOCK, dtype=jnp.int32)
    causal = positions[None, :] <= positions[:, None]
    is_first = jnp.arange(TOPK, dtype=jnp.int32) == 0

    def one_span(span):
        selected = selection[span]
        query_rows = query_blocks[span].astype(jnp.float32)
        key_rows = key_blocks[selected].astype(jnp.float32)
        value_rows = value_blocks[selected].astype(jnp.float32)
        scores = jnp.einsum('qhd,tkhd->thqk', query_rows, key_rows) * scale
        keep = causal[None, None] | jnp.logical_not(is_first)[:, None, None, None]
        scores = jnp.where(keep, scores, -1e+30)
        row_peak = lax.optimization_barrier(jnp.max(scores, axis=3))
        exponentials = jnp.exp(scores - row_peak[..., None])
        row_sum = lax.optimization_barrier(jnp.sum(exponentials, axis=3))
        weights = lax.optimization_barrier(exponentials.astype(jnp.bfloat16)).astype(jnp.float32)
        blended = jnp.einsum('thqk,tkhd->tqhd', weights, value_rows)
        blended = blended / jnp.transpose(row_sum, (0, 2, 1))[..., None]
        rounded = lax.optimization_barrier(blended.astype(jnp.bfloat16)).astype(jnp.float32)
        blended = jnp.where(is_first[:, None, None, None], blended, rounded)
        log_sums = row_peak + jnp.log(row_sum)
        is_live = is_first | (selected != span)
        log_sums = jnp.where(is_live[:, None, None], log_sums, -1e+30)
        highest = lax.optimization_barrier(jnp.max(log_sums, axis=0))
        factors = jnp.where(is_live[:, None, None], jnp.exp(log_sums - highest[None]), 0.0)
        factors = jnp.transpose(factors, (0, 2, 1))[..., None]
        output_rows = lax.optimization_barrier(jnp.sum(factors * blended, axis=0)) / lax.optimization_barrier(jnp.sum(factors, axis=0))
        return output_rows.reshape(BLOCK, width)
    attended = lax.map(one_span, jnp.arange(NBLK, dtype=jnp.int32)).reshape(TOKENS, width)
    mean_square = lax.optimization_barrier(jnp.sum(attended * attended, axis=1)) / width
    factor = lax.rsqrt(mean_square + 1e-06)
    return (attended * factor[:, None] * norm_gain.astype(jnp.float32)[None, :]).astype(jnp.bfloat16)
```

```python
from functools import partial
import math

import jax
import jax.numpy as jnp
from jax import lax
from jax.experimental import pallas as pl
from jax.experimental.pallas import tpu as pltpu
from jax.sharding import PartitionSpec as P

HEADS = 32
HD = 128
CAP = 2
LOG2E = math.log2(math.e)
EXP_SCALE = HD ** (-0.5) * LOG2E


def partial_state(query_rows, key_block, value_block, causal):
    scores = jnp.einsum(
        "sqhd,skhd->shqk", query_rows, key_block, preferred_element_type=jnp.float32
    ) * query_rows.shape[3] ** (-0.5)
    if causal:
        query_pos = lax.broadcasted_iota(jnp.int32, scores.shape, 2)
        key_pos = lax.broadcasted_iota(jnp.int32, scores.shape, 3)
        scores = jnp.where(key_pos <= query_pos, scores, -1e30)
    row_peak = jnp.max(scores, axis=3)
    exponentials = jnp.exp(scores - row_peak[..., None])
    row_sum = jnp.sum(exponentials, axis=3)
    weights = exponentials.astype(jnp.bfloat16)
    blended = jnp.einsum(
        "shqk,skhd->sqhd", weights, value_block, preferred_element_type=jnp.float32
    )
    blended = blended / jnp.transpose(row_sum, (0, 2, 1))[..., None]
    return (blended, row_peak + jnp.log(row_sum))


def slot_plan(selected, first_span, per_dev, capacity):
    own_span = first_span + lax.broadcasted_iota(jnp.int32, selected.shape, 0)
    is_live = (selected != own_span).reshape(-1)
    owner_dev = (selected // per_dev).reshape(-1)
    pair_count = owner_dev.shape[0]
    is_later = lax.broadcasted_iota(jnp.int32, (pair_count, pair_count), 0) > lax.broadcasted_iota(
        jnp.int32, (pair_count, pair_count), 1
    )
    earlier = is_later & (owner_dev[:, None] == owner_dev[None, :]) & is_live[None, :]
    slot_rank = jnp.sum(earlier.astype(jnp.int32), axis=1)
    slot_index = jnp.where(is_live, owner_dev * capacity + slot_rank, 0)
    return (slot_index, is_live, (selected % per_dev).reshape(-1))


def shards(queries, keys, values, selection, norm_gain):
    n_ctx = lax.axis_size("ctx")
    device = lax.axis_index("ctx")
    rows, width = queries.shape
    per_dev, topk_count = selection.shape
    block_rows = rows // per_dev
    heads_dev = width // HD
    slot_count = n_ctx * CAP
    group_size = math.gcd(slot_count, 4)
    query_blocks = queries.reshape(per_dev, block_rows, heads_dev, HD)
    key_blocks = keys.reshape(per_dev, block_rows, heads_dev, HD)
    value_blocks = values.reshape(per_dev, block_rows, heads_dev, HD)
    slot_index, is_live, local_block = slot_plan(selection[:, 1:], device * per_dev, per_dev, CAP)
    pair_count = slot_index.shape[0]
    pair_span = lax.broadcasted_iota(jnp.int32, (pair_count,), 0) // (topk_count - 1)
    slot_ids = lax.broadcasted_iota(jnp.int32, (slot_count, pair_count), 0)
    placed = (slot_ids == slot_index[None, :]) & is_live[None, :]
    slot_span = jnp.sum(jnp.where(placed, pair_span[None, :], 0), axis=1)
    everyone = lax.all_gather(selection, "ctx", axis=0, tiled=True)
    requests = everyone[:, 1:].reshape(n_ctx, per_dev, topk_count - 1)
    first_spans = lax.broadcasted_iota(jnp.int32, (n_ctx,), 0) * per_dev
    all_slots, all_live, all_local = jax.vmap(partial(slot_plan, per_dev=per_dev, capacity=CAP))(
        requests, first_spans
    )
    owner_devs = requests.reshape(n_ctx, -1) // per_dev
    served = all_live & (owner_devs == device)
    capacity_ids = lax.broadcasted_iota(jnp.int32, (1, CAP, 1), 1)
    matched = served[:, None, :] & (all_slots[:, None, :] == device * CAP + capacity_ids)
    send_block = jnp.sum(jnp.where(matched, all_local[:, None, :], 0), axis=2)
    key_out = key_blocks[send_block].reshape(n_ctx, CAP, block_rows, width)
    value_out = value_blocks[send_block].reshape(n_ctx, CAP, block_rows, width)
    key_in, value_in = (
        lax.all_to_all(key_out, "ctx", split_axis=0, concat_axis=0, tiled=True),
        lax.all_to_all(value_out, "ctx", split_axis=0, concat_axis=0, tiled=True),
    )

    def one_group(packed):
        group_keys, group_values, group_span = packed
        blended, log_sums = partial_state(query_blocks[group_span], group_keys, group_values, False)
        return (blended.astype(jnp.bfloat16), log_sums)

    slot_out, slot_lse = lax.map(
        one_group,
        (
            key_in.reshape(-1, group_size, block_rows, heads_dev, HD),
            value_in.reshape(-1, group_size, block_rows, heads_dev, HD),
            slot_span.reshape(-1, group_size),
        ),
    )
    slot_out = slot_out.reshape(slot_count, block_rows, heads_dev, HD)
    slot_lse = slot_lse.reshape(slot_count, heads_dev, block_rows)
    own_out, own_lse = partial_state(query_blocks, key_blocks, value_blocks, True)
    live_pairs = is_live.reshape(per_dev, topk_count - 1)
    pair_out = (
        slot_out[slot_index]
        .reshape(per_dev, topk_count - 1, block_rows, heads_dev, HD)
        .astype(jnp.float32)
    )
    pair_lse = jnp.where(
        live_pairs[:, :, None, None],
        slot_lse[slot_index].reshape(per_dev, topk_count - 1, heads_dev, block_rows),
        -1e30,
    )
    highest = jnp.maximum(own_lse, jnp.max(pair_lse, axis=1))
    own_weight = jnp.exp(own_lse - highest)
    pair_weight = jnp.where(live_pairs[:, :, None, None], jnp.exp(pair_lse - highest[:, None]), 0.0)
    numerator = jnp.transpose(own_weight, (0, 2, 1))[..., None] * own_out
    numerator = numerator + jnp.sum(
        jnp.transpose(pair_weight, (0, 1, 3, 2))[..., None] * pair_out, axis=1
    )
    denominator = own_weight + jnp.sum(pair_weight, axis=1)
    attended = (numerator / jnp.transpose(denominator, (0, 2, 1))[..., None]).reshape(rows, width)
    squares = jnp.sum(attended * attended, axis=1)
    summed = lax.psum(squares, "head")
    factor = lax.rsqrt(summed / (HEADS * HD) + 1e-06)
    return (attended * factor[:, None] * norm_gain.astype(jnp.float32)[None, :]).astype(
        jnp.bfloat16
    )


def attention_kernel(set_sizes, causal, per_dev, block_rows, *refs):
    n_q, n_kv = set_sizes
    lists = refs[0]
    q_refs = refs[1 : 1 + n_q]
    kv_refs = refs[1 + n_q : 1 + n_q + n_kv]
    out_ref, lse_ref, k_scr, vt_scr, q_scr, acc_ref, top_ref, sum_ref = refs[1 + n_q + n_kv :]
    spans = n_q * per_dev
    last = lists.shape[1] - 1
    for piece, ref in enumerate(q_refs):
        for b in range(per_dev):
            q_scr[piece * per_dev + b] = ref[b * block_rows : (b + 1) * block_rows, :]
    for piece, ref in enumerate(kv_refs):
        for b in range(per_dev):
            k_scr[piece * per_dev + b] = ref[0, b * block_rows : (b + 1) * block_rows, :]
            vt_scr[piece * per_dev + b] = ref[1, b * block_rows : (b + 1) * block_rows, :].T

    def absorb(q, blocks, mask=False):
        scores = [
            lax.dot_general(
                k_scr[b], q, (((1,), (1,)), ((), ())), preferred_element_type=jnp.float32
            )
            for b in blocks
        ]
        if mask:
            key_pos = lax.broadcasted_iota(jnp.int32, scores[0].shape, 0)
            query_pos = lax.broadcasted_iota(jnp.int32, scores[0].shape, 1)
            scores = [jnp.where(key_pos <= query_pos, s, -1e30) for s in scores]
        old = top_ref[...]
        top = old
        for s in scores:
            top = jnp.maximum(top, jnp.max(s, axis=0, keepdims=True))
        decay = jnp.exp2((old - top) * EXP_SCALE)
        total = sum_ref[...] * decay
        acc = acc_ref[...] * decay
        for s, b in zip(scores, blocks):
            p = jnp.exp2((s - top) * EXP_SCALE)
            total = total + jnp.sum(p, axis=0, keepdims=True)
            acc = acc + jnp.dot(
                vt_scr[b], p.astype(jnp.bfloat16), preferred_element_type=jnp.float32
            )
        top_ref[...] = top
        sum_ref[...] = total
        acc_ref[...] = acc

    def one_span(span, carry):
        count = lists[span, last]
        live = count >= 0 if causal else count > 0

        @pl.when(live)
        def _():
            top_ref[...] = jnp.full_like(top_ref, -1e30)
            sum_ref[...] = jnp.zeros_like(sum_ref)
            acc_ref[...] = jnp.zeros_like(acc_ref)
            q = q_scr[span]
            if causal:
                absorb(q, [span], mask=True)

            def pair(i, carry):
                absorb(q, [lists[span, 2 * i], lists[span, 2 * i + 1]])
                return carry

            lax.fori_loop(0, count // 2, pair, 0)

            @pl.when(count % 2 == 1)
            def _():
                absorb(q, [lists[span, count - 1]])

            total = sum_ref[...]
            out_ref[span] = (acc_ref[...] / total).astype(out_ref.dtype)
            lse_ref[pl.ds(span, 1), :] = top_ref[...] * EXP_SCALE + jnp.log(total) * LOG2E

        if not causal:

            @pl.when(jnp.logical_not(live))
            def _():
                out_ref[span] = jnp.zeros(out_ref.shape[1:], out_ref.dtype)
                lse_ref[pl.ds(span, 1), :] = jnp.full((1, block_rows), -1e30, jnp.float32)

        return carry

    lax.fori_loop(0, spans, one_span, 0)


def attention_call(lists, q_pieces, kv_pieces, causal, per_dev, block_rows):
    n_q, n_kv = len(q_pieces), len(kv_pieces)
    spans = n_q * per_dev
    vmem = pl.BlockSpec(memory_space=pltpu.VMEM)
    return pl.pallas_call(
        partial(attention_kernel, (n_q, n_kv), causal, per_dev, block_rows),
        out_shape=(
            jax.ShapeDtypeStruct(
                (spans, HD, block_rows), jnp.float32 if causal else jnp.bfloat16
            ),
            jax.ShapeDtypeStruct((spans, block_rows), jnp.float32),
        ),
        in_specs=[pl.BlockSpec(memory_space=pltpu.SMEM)] + [vmem] * (n_q + n_kv),
        out_specs=(vmem, vmem),
        scratch_shapes=[
            pltpu.VMEM((n_kv * per_dev, block_rows, HD), jnp.bfloat16),
            pltpu.VMEM((n_kv * per_dev, HD, block_rows), jnp.bfloat16),
            pltpu.VMEM((spans, block_rows, HD), jnp.bfloat16),
            pltpu.VMEM((HD, block_rows), jnp.float32),
            pltpu.VMEM((1, block_rows), jnp.float32),
            pltpu.VMEM((1, block_rows), jnp.float32),
        ],
        compiler_params=pltpu.CompilerParams(vmem_limit_bytes=32 * 1024 * 1024),
        cost_estimate=pl.CostEstimate(
            flops=32 * 4 * block_rows * block_rows * HD,
            bytes_accessed=4 * 1024 * 1024,
            transcendentals=32 * block_rows * block_rows,
        ),
        name="own_attention" if causal else "served_attention",
    )(lists, *q_pieces, *kv_pieces)


def merge_kernel(per_dev, valid, *refs):
    outs, lses = refs[0:3], refs[3:6]
    keep_ref, send_ref, squares_ref = refs[6:]
    for span in range(2 * per_dev):
        rows = slice(span, span + 1)
        lse = [lses[0][rows, :]]
        for i in (1, 2):
            lse.append(jnp.where(valid[i - 1] > 0, lses[i][rows, :], -1e30))
        top = jnp.maximum(jnp.maximum(lse[0], lse[1]), lse[2])
        weight = [jnp.exp2(v - top) for v in lse]
        mixed = weight[0] * outs[0][span]
        for i in (1, 2):
            mixed = mixed + weight[i] * outs[i][span].astype(jnp.float32)
        mixed = mixed / (weight[0] + weight[1] + weight[2])
        squares_ref[rows, :] = jnp.sum(mixed * mixed, axis=0, keepdims=True)
        target = keep_ref if span < per_dev else send_ref
        block_rows = mixed.shape[1]
        start = (span % per_dev) * block_rows
        target[start : start + block_rows, :] = mixed.T.astype(target.dtype)


def merge_call(valid, own, near, far, per_dev, block_rows):
    vmem = pl.BlockSpec(memory_space=pltpu.VMEM)
    half = jax.ShapeDtypeStruct((per_dev * block_rows, HD), jnp.bfloat16)

    def kernel(valid_ref, *refs):
        merge_kernel(per_dev, (valid_ref[0], valid_ref[1]), *refs)

    return pl.pallas_call(
        kernel,
        out_shape=(half, half, jax.ShapeDtypeStruct((2 * per_dev, block_rows), jnp.float32)),
        in_specs=[pl.BlockSpec(memory_space=pltpu.SMEM)] + [vmem] * 6,
        out_specs=(vmem, vmem, vmem),
        compiler_params=pltpu.CompilerParams(vmem_limit_bytes=32 * 1024 * 1024),
        name="merge",
    )(valid, own[0], near[0], far[0], own[1], near[1], far[1])


def finish_kernel(per_dev, half, place_ref, *refs):
    pieces = refs[: 2 * half]
    squares_ref, gain_ref, out_ref = refs[2 * half :]
    block_rows = squares_ref.shape[1]
    factor = lax.rsqrt(squares_ref[...] / (HEADS * HD) + 1e-06)
    for b in range(per_dev):
        column = jnp.broadcast_to(factor[b : b + 1, :], (HD, block_rows)).T
        rows = slice(b * block_rows, (b + 1) * block_rows)
        for side in range(2):
            for c in range(half):
                start = pl.multiple_of((place_ref[side] * half + c) * HD, HD)
                piece = pieces[side * half + c][rows, :].astype(jnp.float32)
                gain = gain_ref[:, pl.ds(start, HD)].astype(jnp.float32)
                out_ref[rows, pl.ds(start, HD)] = (piece * column * gain).astype(out_ref.dtype)


def finish_call(place, kept, returned, squares, gain, per_dev):
    vmem = pl.BlockSpec(memory_space=pltpu.VMEM)
    rows = kept[0].shape[0]
    width = gain.shape[0]
    return pl.pallas_call(
        partial(finish_kernel, per_dev, len(kept)),
        out_shape=jax.ShapeDtypeStruct((rows, width), jnp.bfloat16),
        in_specs=[pl.BlockSpec(memory_space=pltpu.SMEM)] + [vmem] * (2 * len(kept) + 2),
        out_specs=vmem,
        compiler_params=pltpu.CompilerParams(vmem_limit_bytes=32 * 1024 * 1024),
        name="finish",
    )(place, *kept, *returned, squares, gain.reshape(1, width))


def slot_lists(rows, span_ids, level, x, per_dev, allowed_level, include_self):
    owner = rows // per_dev
    block_level, block_x = owner // 2, owner % 2
    live = (rows != span_ids[:, None]) & allowed_level(block_level)
    slot = jnp.where(block_level == level, 0, 2 * per_dev)
    slot = slot + jnp.where(block_x == x, 0, per_dev) + rows % per_dev
    count = rows.shape[1]
    t = jnp.arange(count)
    rank = jnp.sum((t[None, :, None] > t[None, None, :]) & live[:, None, :], axis=2)
    hit = live[:, :, None] & (rank[:, :, None] == t[None, None, :])
    packed = jnp.sum(jnp.where(hit, slot[:, :, None], 0), axis=1)
    total = jnp.sum(live.astype(jnp.int32), axis=1, keepdims=True)
    return jnp.concatenate([packed, total], axis=1).astype(jnp.int32)


def level_shards(queries, keys, values, selection, norm_gain):
    device = lax.axis_index("ctx")
    level, x = device // 2, device % 2
    rows, width = queries.shape
    per_dev, topk = selection.shape
    block_rows = rows // per_dev
    half = width // HD // 2

    def to(array, pairs):
        return lax.ppermute(array, "ctx", pairs)

    swap = [(d, d ^ 1) for d in range(8)]
    lift = [(0, 2), (1, 3)]
    near_down, far_down = [(4, 2), (5, 3), (6, 4), (7, 5)], [(6, 2), (7, 3)]
    near_up, far_up = [(2, 4), (3, 5), (4, 6), (5, 7)], [(2, 6), (3, 7)]

    everyone = lax.all_gather(selection, "ctx", axis=0, tiled=True)

    def level_rows(at):
        at = jnp.clip(at, 0, 3)
        first = jnp.stack([(at * 2 + x) * per_dev, (at * 2 + 1 - x) * per_dev])
        ids = (first[:, None] + jnp.arange(per_dev)[None, :]).reshape(-1)
        return everyone[ids, 1:], ids

    own_rows, own_ids = level_rows(level)
    own_lists = slot_lists(
        own_rows, own_ids, level, x, per_dev,
        lambda b: (b == level) | ((level == 1) & (b == 0)), True,
    )
    near_rows, near_ids = level_rows(level + 1)
    near_lists = slot_lists(
        near_rows, near_ids, level, x, per_dev,
        lambda b: ((level == 2) & (b == 2)) | ((level == 1) & (b <= 1)), False,
    )
    far_rows, far_ids = level_rows(level + 2)
    far_lists = slot_lists(
        far_rows, far_ids, level, x, per_dev, lambda b: (level == 1) & (b <= 1), False
    )
    served_lists = jnp.concatenate([near_lists, far_lists], axis=0)
    valid = jnp.stack([level >= 2, level >= 3]).astype(jnp.int32)
    place = jnp.stack([x, 1 - x]).astype(jnp.int32)

    def columns(array, head):
        return lax.dynamic_slice(array, (0, head * HD), (rows, HD))

    kept, returned, squares = [], [], []
    for c in range(half):
        here, there = x * half + c, (1 - x) * half + c
        kv_keep = jnp.stack([columns(keys, here), columns(values, here)])
        kv_swap = to(jnp.stack([columns(keys, there), columns(values, there)]), swap)
        q_keep = columns(queries, here)
        q_swap = to(columns(queries, there), swap)
        low = [to(kv_keep, lift), to(kv_swap, lift)]
        near_q = [to(q_keep, near_down), to(q_swap, near_down)]
        far_q = [to(q_keep, far_down), to(q_swap, far_down)]
        kv = [kv_keep, kv_swap] + low
        served, served_lse = attention_call(
            served_lists, near_q + far_q, kv, False, per_dev, block_rows
        )
        spans = 2 * per_dev
        near = (to(served[:spans], near_up), to(served_lse[:spans], near_up))
        far = (to(served[spans:], far_up), to(served_lse[spans:], far_up))
        own = attention_call(own_lists, [q_keep, q_swap], kv, True, per_dev, block_rows)
        keep, send, square = merge_call(valid, own, near, far, per_dev, block_rows)
        kept.append(keep)
        returned.append(to(send, swap))
        squares.append(square)
    square = sum(squares[1:], squares[0])
    square = square[:per_dev] + to(square[per_dev:], swap)
    square = lax.psum(square, "head")
    return finish_call(place, kept, returned, square, norm_gain, per_dev)


def solution(mesh):
    placed = (P("ctx", "head"), P("ctx", "head"), P("ctx", "head"), P("ctx", None), P("head"))
    body = level_shards if mesh.shape["ctx"] == 8 else shards
    return jax.shard_map(
        body, mesh=mesh, in_specs=placed, out_specs=P("ctx", "head"), check_vma=False
    )
```

```python
from functools import partial
import math

import jax
import jax.numpy as jnp
from jax import lax
from jax.experimental import pallas as pl
from jax.experimental.pallas import tpu as pltpu
from jax.sharding import PartitionSpec as P

HEADS = 32
HD = 128
CAP = 2
LOG2E = math.log2(math.e)
EXP_SCALE = HD ** (-0.5) * LOG2E


def partial_state(query_rows, key_block, value_block, causal):
    scores = jnp.einsum(
        "sqhd,skhd->shqk", query_rows, key_block, preferred_element_type=jnp.float32
    ) * query_rows.shape[3] ** (-0.5)
    if causal:
        query_pos = lax.broadcasted_iota(jnp.int32, scores.shape, 2)
        key_pos = lax.broadcasted_iota(jnp.int32, scores.shape, 3)
        scores = jnp.where(key_pos <= query_pos, scores, -1e30)
    row_peak = jnp.max(scores, axis=3)
    exponentials = jnp.exp(scores - row_peak[..., None])
    row_sum = jnp.sum(exponentials, axis=3)
    weights = exponentials.astype(jnp.bfloat16)
    blended = jnp.einsum(
        "shqk,skhd->sqhd", weights, value_block, preferred_element_type=jnp.float32
    )
    blended = blended / jnp.transpose(row_sum, (0, 2, 1))[..., None]
    return (blended, row_peak + jnp.log(row_sum))


def slot_plan(selected, first_span, per_dev, capacity):
    own_span = first_span + lax.broadcasted_iota(jnp.int32, selected.shape, 0)
    is_live = (selected != own_span).reshape(-1)
    owner_dev = (selected // per_dev).reshape(-1)
    pair_count = owner_dev.shape[0]
    is_later = lax.broadcasted_iota(jnp.int32, (pair_count, pair_count), 0) > lax.broadcasted_iota(
        jnp.int32, (pair_count, pair_count), 1
    )
    earlier = is_later & (owner_dev[:, None] == owner_dev[None, :]) & is_live[None, :]
    slot_rank = jnp.sum(earlier.astype(jnp.int32), axis=1)
    slot_index = jnp.where(is_live, owner_dev * capacity + slot_rank, 0)
    return (slot_index, is_live, (selected % per_dev).reshape(-1))


def shards(queries, keys, values, selection, norm_gain):
    n_ctx = lax.axis_size("ctx")
    device = lax.axis_index("ctx")
    rows, width = queries.shape
    per_dev, topk_count = selection.shape
    block_rows = rows // per_dev
    heads_dev = width // HD
    slot_count = n_ctx * CAP
    group_size = math.gcd(slot_count, 4)
    query_blocks = queries.reshape(per_dev, block_rows, heads_dev, HD)
    key_blocks = keys.reshape(per_dev, block_rows, heads_dev, HD)
    value_blocks = values.reshape(per_dev, block_rows, heads_dev, HD)
    slot_index, is_live, local_block = slot_plan(selection[:, 1:], device * per_dev, per_dev, CAP)
    pair_count = slot_index.shape[0]
    pair_span = lax.broadcasted_iota(jnp.int32, (pair_count,), 0) // (topk_count - 1)
    slot_ids = lax.broadcasted_iota(jnp.int32, (slot_count, pair_count), 0)
    placed = (slot_ids == slot_index[None, :]) & is_live[None, :]
    slot_span = jnp.sum(jnp.where(placed, pair_span[None, :], 0), axis=1)
    everyone = lax.all_gather(selection, "ctx", axis=0, tiled=True)
    requests = everyone[:, 1:].reshape(n_ctx, per_dev, topk_count - 1)
    first_spans = lax.broadcasted_iota(jnp.int32, (n_ctx,), 0) * per_dev
    all_slots, all_live, all_local = jax.vmap(partial(slot_plan, per_dev=per_dev, capacity=CAP))(
        requests, first_spans
    )
    owner_devs = requests.reshape(n_ctx, -1) // per_dev
    served = all_live & (owner_devs == device)
    capacity_ids = lax.broadcasted_iota(jnp.int32, (1, CAP, 1), 1)
    matched = served[:, None, :] & (all_slots[:, None, :] == device * CAP + capacity_ids)
    send_block = jnp.sum(jnp.where(matched, all_local[:, None, :], 0), axis=2)
    key_out = key_blocks[send_block].reshape(n_ctx, CAP, block_rows, width)
    value_out = value_blocks[send_block].reshape(n_ctx, CAP, block_rows, width)
    key_in, value_in = (
        lax.all_to_all(key_out, "ctx", split_axis=0, concat_axis=0, tiled=True),
        lax.all_to_all(value_out, "ctx", split_axis=0, concat_axis=0, tiled=True),
    )

    def one_group(packed):
        group_keys, group_values, group_span = packed
        blended, log_sums = partial_state(query_blocks[group_span], group_keys, group_values, False)
        return (blended.astype(jnp.bfloat16), log_sums)

    slot_out, slot_lse = lax.map(
        one_group,
        (
            key_in.reshape(-1, group_size, block_rows, heads_dev, HD),
            value_in.reshape(-1, group_size, block_rows, heads_dev, HD),
            slot_span.reshape(-1, group_size),
        ),
    )
    slot_out = slot_out.reshape(slot_count, block_rows, heads_dev, HD)
    slot_lse = slot_lse.reshape(slot_count, heads_dev, block_rows)
    own_out, own_lse = partial_state(query_blocks, key_blocks, value_blocks, True)
    live_pairs = is_live.reshape(per_dev, topk_count - 1)
    pair_out = (
        slot_out[slot_index]
        .reshape(per_dev, topk_count - 1, block_rows, heads_dev, HD)
        .astype(jnp.float32)
    )
    pair_lse = jnp.where(
        live_pairs[:, :, None, None],
        slot_lse[slot_index].reshape(per_dev, topk_count - 1, heads_dev, block_rows),
        -1e30,
    )
    highest = jnp.maximum(own_lse, jnp.max(pair_lse, axis=1))
    own_weight = jnp.exp(own_lse - highest)
    pair_weight = jnp.where(live_pairs[:, :, None, None], jnp.exp(pair_lse - highest[:, None]), 0.0)
    numerator = jnp.transpose(own_weight, (0, 2, 1))[..., None] * own_out
    numerator = numerator + jnp.sum(
        jnp.transpose(pair_weight, (0, 1, 3, 2))[..., None] * pair_out, axis=1
    )
    denominator = own_weight + jnp.sum(pair_weight, axis=1)
    attended = (numerator / jnp.transpose(denominator, (0, 2, 1))[..., None]).reshape(rows, width)
    squares = jnp.sum(attended * attended, axis=1)
    summed = lax.psum(squares, "head")
    factor = lax.rsqrt(summed / (HEADS * HD) + 1e-06)
    return (attended * factor[:, None] * norm_gain.astype(jnp.float32)[None, :]).astype(
        jnp.bfloat16
    )


LSE_ROWS = 32
UNROLL = 2
VMEM_LIMIT = 48 * 1024 * 1024


def unit_fields(code):
    return code & 31, (code >> 5) & 31, (code >> 10) & 63, (code >> 16) & 1, (code >> 17) & 1


def unit_code(slot, span, out, first, diagonal):
    return slot + span * 32 + out * 1024 + first * 65536 + diagonal * 131072


def attention_kernel(shape, own, plan, *refs):
    heads, n_q, n_kv, per_dev, block_rows = shape
    q_refs, refs = refs[:2], refs[2:]
    k_refs, refs = refs[:3], refs[3:]
    outs, refs = refs[:2], refs[2:]
    sides = (0,) if own else (0, 1)
    (q_scr, kv_scr, s0, s1, p0, p1, d0, d1, acc_scr, top_scr, sum_scr, o_scr, lse_scr, sems) = refs[:14]
    s_scr, p_scr, decay_scr = (s0, s1), (p0, p1), (d0, d1)
    spans = n_q * per_dev
    copies = []
    for h in range(heads):
        sources = [ref.at[h, 0] if own else ref.at[side, h] for ref in q_refs for side in sides]
        targets = [q_scr.at[h, i] for i in range(n_q)]
        for i in range(n_kv):
            sources.append(k_refs[i].at[h, pl.ds(1, 2)] if i < 2 else k_refs[2].at[i - 2, h])
            targets.append(kv_scr.at[h, i])
        for i, (source, target) in enumerate(zip(sources, targets)):
            copies.append(pltpu.make_async_copy(source, target, sems.at[h, i]))
    for copy in copies:
        copy.start()
    s1[...] = jnp.zeros_like(s1)
    p0[...] = jnp.zeros_like(p0)
    d0[...] = jnp.zeros_like(d0)
    acc_scr[...] = jnp.zeros_like(acc_scr)
    top_scr[...] = jnp.zeros_like(top_scr)
    sum_scr[...] = jnp.ones_like(sum_scr)
    if own:
        bias_scr = refs[14]
        key_pos = lax.broadcasted_iota(jnp.int32, (block_rows, block_rows), 0)
        query_pos = lax.broadcasted_iota(jnp.int32, (block_rows, block_rows), 1)
        bias_scr[0] = jnp.zeros((block_rows, block_rows), jnp.float32)
        bias_scr[1] = jnp.where(key_pos <= query_pos, 0.0, -1e30)
    for copy in copies:
        copy.wait()

    def rows_of(i):
        return pl.ds(pl.multiple_of((i % per_dev) * block_rows, block_rows), block_rows)

    def step(h, at, now, acc, top, total):
        before = 1 - now
        for u in range(UNROLL):
            slot, _, out, _, _ = unit_fields(plan[at + u])
            vt = kv_scr[h, slot // per_dev, 1, rows_of(slot), :]
            vt = jnp.concatenate([vt[:HD], vt[HD:]], axis=1)
            mixed = jnp.dot(vt, p_scr[now][u], preferred_element_type=jnp.float32)
            acc = acc * decay_scr[now][u, 0:1, :] + mixed
            o_scr[out] = (acc * decay_scr[now][u, 1:2, :]).astype(o_scr.dtype)
        for u in range(UNROLL):
            _, _, out, first, diagonal = unit_fields(plan[at + UNROLL + u])
            s = s_scr[before][u]
            if own:
                s = s + bias_scr[diagonal]
            old = jnp.where(first == 1, -1e30, top)
            top = jnp.maximum(old, jnp.max(s, axis=0, keepdims=True))
            decay = jnp.exp2((old - top) * EXP_SCALE)
            p = jnp.exp2((s - top) * EXP_SCALE)
            total = total * decay + jnp.sum(p, axis=0, keepdims=True)
            p_scr[before][u] = p.astype(jnp.bfloat16)
            decay_scr[before][u, 0:1, :] = decay
            decay_scr[before][u, 1:2, :] = 1.0 / total
            lse_scr[pl.ds(out, 1), :] = top * EXP_SCALE + jnp.log(total) * LOG2E
        for u in range(UNROLL):
            slot, span, _, _, _ = unit_fields(plan[at + 2 * UNROLL + u])
            k = kv_scr[h, slot // per_dev, 0, rows_of(slot), :]
            q = q_scr[h, span // per_dev, rows_of(span), :]
            s_scr[now][u] = lax.dot_general(
                k, q, (((1,), (1,)), ((), ())), preferred_element_type=jnp.float32
            )
        return acc, top, total

    for h in range(heads):
        o_scr[...] = jnp.zeros_like(o_scr)
        lse_scr[...] = jnp.full_like(lse_scr, -1e30)

        def two_steps(i, carry):
            state = (acc_scr[...], top_scr[...], sum_scr[...])
            state = step(h, 1 + 2 * i * UNROLL, 0, *state)
            state = step(h, 1 + (2 * i + 1) * UNROLL, 1, *state)
            acc_scr[...], top_scr[...], sum_scr[...] = state
            return carry

        lax.fori_loop(0, (plan[0] + 1) // 2, two_steps, 0)
        if own:
            outs[0][h] = o_scr[:spans]
            outs[1][h] = lse_scr[:spans, :]
        else:
            half = spans // 2
            for side in range(2):
                for span in range(half):
                    outs[side][h, span * HD : (span + 1) * HD, :] = o_scr[side * half + span]
                lse = lse_scr[side * half : (side + 1) * half, :]
                high = lse.astype(jnp.bfloat16).astype(jnp.float32)
                middle = (lse - high).astype(jnp.bfloat16).astype(jnp.float32)
                rest = jnp.zeros((LSE_ROWS - 3 * half, block_rows), jnp.float32)
                parts = jnp.concatenate([high, middle, lse - high - middle, rest], axis=0)
                outs[side][h, half * HD :, :] = parts.astype(jnp.bfloat16)


def attention_call(plan, q_pieces, kv_pieces, own, heads, per_dev, block_rows):
    n_q, n_kv = (2 if own else 4), 4
    spans = n_q * per_dev
    vmem, hbm = pl.BlockSpec(memory_space=pltpu.VMEM), pl.BlockSpec(memory_space=pl.ANY)
    f32, bf16 = jnp.float32, jnp.bfloat16
    if own:
        out_shape = (
            jax.ShapeDtypeStruct((heads, spans, HD, block_rows), f32),
            jax.ShapeDtypeStruct((heads, spans, block_rows), f32),
        )
    else:
        packed = jax.ShapeDtypeStruct((heads, spans // 2 * HD + LSE_ROWS, block_rows), bf16)
        out_shape = (packed, packed)
    scratch = [
        pltpu.VMEM((heads, n_q, per_dev * block_rows, HD), bf16),
        pltpu.VMEM((heads, n_kv, 2, per_dev * block_rows, HD), bf16),
        pltpu.VMEM((UNROLL, block_rows, block_rows), f32),
        pltpu.VMEM((UNROLL, block_rows, block_rows), f32),
        pltpu.VMEM((UNROLL, block_rows, block_rows), bf16),
        pltpu.VMEM((UNROLL, block_rows, block_rows), bf16),
        pltpu.VMEM((UNROLL, 8, block_rows), f32),
        pltpu.VMEM((UNROLL, 8, block_rows), f32),
        pltpu.VMEM((HD, block_rows), f32),
        pltpu.VMEM((1, block_rows), f32),
        pltpu.VMEM((1, block_rows), f32),
        pltpu.VMEM((spans + 1, HD, block_rows), f32 if own else bf16),
        pltpu.VMEM((spans + 8, block_rows), f32),
        pltpu.SemaphoreType.DMA((heads, n_q + n_kv)),
    ]
    if own:
        scratch.append(pltpu.VMEM((2, block_rows, block_rows), f32))
    return pl.pallas_call(
        partial(attention_kernel, (heads, n_q, n_kv, per_dev, block_rows), own),
        out_shape=out_shape,
        in_specs=[pl.BlockSpec(memory_space=pltpu.SMEM)] + [hbm] * 5,
        out_specs=(vmem, vmem),
        scratch_shapes=scratch,
        compiler_params=pltpu.CompilerParams(vmem_limit_bytes=VMEM_LIMIT),
        cost_estimate=pl.CostEstimate(
            flops=heads * 32 * 4 * block_rows * block_rows * HD,
            bytes_accessed=heads * 4 * 1024 * 1024,
            transcendentals=heads * 32 * block_rows * block_rows,
        ),
        name="own_attention" if own else "served_attention",
    )(plan, *q_pieces, *kv_pieces)


def pack_kernel(shape, place, q_ref, k_ref, v_ref, keep_ref, send_ref, v_scr, t_scr, sems):
    heads, first, half, rows = shape
    later, outs = [], (keep_ref, send_ref)
    loads = []
    n = 0
    for side in range(2):
        for h in range(heads):
            start = pl.multiple_of((place[side] * half + first + h) * HD, HD)
            load = pltpu.make_async_copy(v_ref.at[:, pl.ds(start, HD)], v_scr.at[side, h], sems.at[n])
            load.start()
            loads.append(load)
            n += 1
    for side in (1, 0):
        for h in range(heads):
            start = pl.multiple_of((place[side] * half + first + h) * HD, HD)
            for i, ref in enumerate((q_ref, k_ref)):
                copy = pltpu.make_async_copy(ref.at[:, pl.ds(start, HD)], outs[side].at[h, i], sems.at[n])
                copy.start()
                later.append(copy)
                n += 1
    for side in (1, 0):
        for h in range(heads):
            loads[side * heads + h].wait()
            for tile in range(rows // HD):
                at = slice(tile * HD, (tile + 1) * HD)
                t_scr[side, h, at, :] = v_scr[side, h, at, :].T
            copy = pltpu.make_async_copy(t_scr.at[side, h], outs[side].at[h, 2], sems.at[n])
            copy.start()
            later.append(copy)
            n += 1
    for copy in later:
        copy.wait()


def pack_call(place, queries, keys, values, heads, first, half):
    rows = queries.shape[0]
    hbm = pl.BlockSpec(memory_space=pl.ANY)
    packed = jax.ShapeDtypeStruct((heads, 3, rows, HD), jnp.bfloat16)
    return pl.pallas_call(
        partial(pack_kernel, (heads, first, half, rows)),
        out_shape=(packed, packed),
        in_specs=[pl.BlockSpec(memory_space=pltpu.SMEM)] + [hbm] * 3,
        out_specs=(hbm, hbm),
        scratch_shapes=[
            pltpu.VMEM((2, heads, rows, HD), jnp.bfloat16),
            pltpu.VMEM((2, heads, rows, HD), jnp.bfloat16),
            pltpu.SemaphoreType.DMA((8 * heads,)),
        ],
        compiler_params=pltpu.CompilerParams(vmem_limit_bytes=VMEM_LIMIT),
        name="pack",
    )(place, queries, keys, values)


def join_kernel(heads, keep_ref, swap_ref, q_ref, kv_ref, sems):
    copies = []
    for side, ref in enumerate((keep_ref, swap_ref)):
        for h in range(heads):
            copies.append((ref.at[h, 0], q_ref.at[side, h]))
            copies.append((ref.at[h, pl.ds(1, 2)], kv_ref.at[side, h]))
    copies = [pltpu.make_async_copy(s, t, sems.at[i]) for i, (s, t) in enumerate(copies)]
    for copy in copies:
        copy.start()
    for copy in copies:
        copy.wait()


def join_call(keep, swapped):
    heads, _, rows, _ = keep.shape
    hbm = pl.BlockSpec(memory_space=pl.ANY)
    return pl.pallas_call(
        partial(join_kernel, heads),
        out_shape=(
            jax.ShapeDtypeStruct((2, heads, rows, HD), jnp.bfloat16),
            jax.ShapeDtypeStruct((2, heads, 2, rows, HD), jnp.bfloat16),
        ),
        in_specs=[hbm, hbm],
        out_specs=(hbm, hbm),
        scratch_shapes=[pltpu.SemaphoreType.DMA((4 * heads,))],
        compiler_params=pltpu.CompilerParams(vmem_limit_bytes=VMEM_LIMIT),
        name="join",
    )(keep, swapped)


def merge_kernel(shape, valid, own_ref, own_lse_ref, near_ref, far_ref, sofar_ref, keep_ref, send_ref, squares_ref):
    heads, per_dev, block_rows = shape
    spans = 2 * per_dev
    squares_ref[...] = sofar_ref[...]
    for h in range(heads):
        lses = [own_lse_ref[h]]
        for i, ref in enumerate((near_ref, far_ref)):
            parts = ref[h, spans * HD :, :].astype(jnp.float32)
            lse = parts[:spans] + parts[spans : 2 * spans] + parts[2 * spans : 3 * spans]
            lses.append(jnp.where(valid[i] > 0, lse, -1e30))
        top = jnp.maximum(jnp.maximum(lses[0], lses[1]), lses[2])
        weights = [jnp.exp2(lse - top) for lse in lses]
        scale = 1.0 / (weights[0] + weights[1] + weights[2])
        weights = [weight * scale for weight in weights]
        for span in range(spans):
            rows = slice(span, span + 1)
            tile = slice(span * HD, (span + 1) * HD)
            mixed = weights[0][rows, :] * own_ref[h, span]
            mixed = mixed + weights[1][rows, :] * near_ref[h, tile, :].astype(jnp.float32)
            mixed = mixed + weights[2][rows, :] * far_ref[h, tile, :].astype(jnp.float32)
            squares_ref[rows, :] = squares_ref[rows, :] + jnp.sum(mixed * mixed, axis=0, keepdims=True)
            target = keep_ref if span < per_dev else send_ref
            start = (span % per_dev) * block_rows
            target[h, start : start + block_rows, :] = mixed.T.astype(target.dtype)


def merge_call(valid, own, near, far, sofar, per_dev):
    heads, spans, _, block_rows = own[0].shape
    vmem = pl.BlockSpec(memory_space=pltpu.VMEM)
    packed = jax.ShapeDtypeStruct((heads, per_dev * block_rows, HD), jnp.bfloat16)
    return pl.pallas_call(
        partial(merge_kernel, (heads, per_dev, block_rows)),
        out_shape=(packed, packed, jax.ShapeDtypeStruct((spans, block_rows), jnp.float32)),
        in_specs=[pl.BlockSpec(memory_space=pltpu.SMEM)] + [vmem] * 5,
        out_specs=(vmem, vmem, vmem),
        compiler_params=pltpu.CompilerParams(vmem_limit_bytes=VMEM_LIMIT),
        name="merge",
    )(valid, own[0], own[1], near, far, sofar)


def finish_kernel(per_dev, sizes, place, *refs):
    n = len(sizes)
    kept, returned = refs[:n], refs[n : 2 * n]
    squares_ref, gain_ref, out_ref = refs[2 * n :]
    block_rows = squares_ref.shape[1]
    half = sum(sizes)
    factor = lax.rsqrt(squares_ref[...] / (HEADS * HD) + 1e-06)
    for b in range(per_dev):
        column = jnp.broadcast_to(factor[b : b + 1, :], (HD, block_rows)).T
        rows = slice(b * block_rows, (b + 1) * block_rows)
        for side, pieces in enumerate((kept, returned)):
            head = 0
            for piece, size in zip(pieces, sizes):
                for h in range(size):
                    start = pl.multiple_of((place[side] * half + head) * HD, HD)
                    gain = gain_ref[:, pl.ds(start, HD)].astype(jnp.float32)
                    value = piece[h, rows, :].astype(jnp.float32) * column * gain
                    out_ref[rows, pl.ds(start, HD)] = value.astype(out_ref.dtype)
                    head += 1


def finish_call(place, kept, returned, squares, gain, per_dev):
    vmem = pl.BlockSpec(memory_space=pltpu.VMEM)
    rows, width = kept[0].shape[1], gain.shape[0]
    return pl.pallas_call(
        partial(finish_kernel, per_dev, [k.shape[0] for k in kept]),
        out_shape=jax.ShapeDtypeStruct((rows, width), jnp.bfloat16),
        in_specs=[pl.BlockSpec(memory_space=pltpu.SMEM)] + [vmem] * (2 * len(kept) + 2),
        out_specs=vmem,
        compiler_params=pltpu.CompilerParams(vmem_limit_bytes=VMEM_LIMIT),
        name="finish",
    )(place, *kept, *returned, squares, gain.reshape(1, width))


def plan_of(live, slot, diagonal, dump):
    spans, entries = live.shape
    t = jnp.arange(entries)
    earlier = jnp.sum((t[None, None, :] < t[None, :, None]) & live[:, None, :], axis=2)
    span = lax.broadcasted_iota(jnp.int32, live.shape, 0)
    code = unit_code(slot, span, span, (earlier == 0).astype(jnp.int32), diagonal)
    code, live = code.reshape(-1), live.reshape(-1)
    n = spans * entries
    i = jnp.arange(n)
    rank = jnp.sum((i[None, :] < i[:, None]) & live[None, :], axis=1)
    at = jnp.arange(n + 8 * UNROLL)
    hit = live[None, :] & (rank[None, :] + 2 * UNROLL == at[:, None])
    idle = unit_code(0, 0, dump, 1, 0)
    codes = jnp.sum(jnp.where(hit, code[None, :] - idle, 0), axis=1) + idle
    total = jnp.sum(live.astype(jnp.int32))
    steps = jnp.where(total > 0, (total + UNROLL - 1) // UNROLL + 2, 0)
    return jnp.concatenate([steps[None], codes]).astype(jnp.int32)


def level_shards(queries, keys, values, selection, norm_gain):
    device = lax.axis_index("ctx")
    level, x = device // 2, device % 2
    rows, width = queries.shape
    per_dev, topk = selection.shape
    block_rows = rows // per_dev
    spans = 2 * per_dev
    half = width // HD // 2

    def to(array, pairs):
        return lax.ppermute(array, "ctx", pairs)

    swap = [(d, d ^ 1) for d in range(8)]
    lift = [(0, 2), (1, 3)]
    near_down, far_down = [(4, 2), (5, 3), (6, 4), (7, 5)], [(6, 2), (7, 3)]
    near_up, far_up = [(2, 4), (3, 5), (4, 6), (5, 7)], [(2, 6), (3, 7)]
    valid = jnp.stack([level >= 2, level >= 3]).astype(jnp.int32)
    place = jnp.stack([x, 1 - x]).astype(jnp.int32)

    sizes = [1] * half
    packs = []
    for c, size in enumerate(sizes):
        keep, send = pack_call(place, queries, keys, values, size, sum(sizes[:c]), half)
        packs.append((keep, to(send, swap)))

    own_selection = jnp.concatenate([selection, to(selection, swap)], axis=0)
    near_selection, far_selection = to(own_selection, near_down), to(own_selection, far_down)

    def ids(at):
        first = jnp.stack([(at * 2 + x) * per_dev, (at * 2 + 1 - x) * per_dev])
        return (first[:, None] + jnp.arange(per_dev)[None, :]).reshape(-1, 1)

    def slots(blocks):
        owner = blocks // per_dev
        slot = jnp.where(owner // 2 == level, 0, spans) + jnp.where(owner % 2 == x, 0, per_dev)
        return owner // 2, slot + blocks % per_dev

    others = own_selection[:, 1:]
    block_level, slot = slots(others)
    live = (others != ids(level)) & ((block_level == level) | ((level == 1) & (block_level == 0)))
    first = jnp.ones((spans, 1), jnp.int32)
    own_plan = plan_of(
        jnp.concatenate([first > 0, live], axis=1),
        jnp.concatenate([jnp.arange(spans, dtype=jnp.int32)[:, None], slot], axis=1),
        jnp.concatenate([first, jnp.zeros_like(others)], axis=1),
        spans,
    )
    others = jnp.concatenate([near_selection, far_selection], axis=0)[:, 1:]
    block_level, slot = slots(others)
    is_near = lax.broadcasted_iota(jnp.int32, others.shape, 0) < spans
    mine = ((level == 1) & (block_level <= 1)) | ((level == 2) & (block_level == 2) & is_near)
    live = (others != jnp.concatenate([ids(level + 1), ids(level + 2)], axis=0)) & mine
    served_plan = plan_of(live, slot, jnp.zeros_like(others), 2 * spans)

    kept, returned = [], []
    squares = jnp.zeros((spans, block_rows), jnp.float32)
    for c, size in enumerate(sizes):
        keep, swapped = packs[c]
        level_q, level_kv = join_call(keep, swapped)
        low = to(level_kv, lift)
        near_q, far_q = to(level_q, near_down), to(level_q, far_down)
        kv = [keep, swapped, low]
        near, far = attention_call(served_plan, [near_q, far_q], kv, False, size, per_dev, block_rows)
        near, far = to(near, near_up), to(far, far_up)
        own = attention_call(own_plan, [keep, swapped], kv, True, size, per_dev, block_rows)
        keep, send, squares = merge_call(valid, own, near, far, squares, per_dev)
        kept.append(keep)
        returned.append(to(send, swap))
    square = squares[:per_dev] + to(squares[per_dev:], swap)
    n_head = lax.axis_size("head")
    hop = 1
    while hop < n_head:
        square = square + lax.ppermute(square, "head", [(i, i ^ hop) for i in range(n_head)])
        hop *= 2
    return finish_call(place, kept, returned, square, norm_gain, per_dev)


def solution(mesh):
    placed = (P("ctx", "head"), P("ctx", "head"), P("ctx", "head"), P("ctx", None), P("head"))
    body = level_shards if mesh.shape["ctx"] == 8 else shards
    return jax.shard_map(
        body, mesh=mesh, in_specs=placed, out_specs=P("ctx", "head"), check_vma=False
    )
```

```python
from functools import partial
import math

import jax
import jax.numpy as jnp
from jax import lax
from jax.experimental import pallas as pl
from jax.experimental.pallas import tpu as pltpu
from jax.sharding import PartitionSpec as P

HEADS = 32
HD = 128
CAP = 2
LOG2E = math.log2(math.e)
EXP_SCALE = HD ** (-0.5) * LOG2E


def partial_state(query_rows, key_block, value_block, causal):
    scores = jnp.einsum(
        "sqhd,skhd->shqk", query_rows, key_block, preferred_element_type=jnp.float32
    ) * query_rows.shape[3] ** (-0.5)
    if causal:
        query_pos = lax.broadcasted_iota(jnp.int32, scores.shape, 2)
        key_pos = lax.broadcasted_iota(jnp.int32, scores.shape, 3)
        scores = jnp.where(key_pos <= query_pos, scores, -1e30)
    row_peak = jnp.max(scores, axis=3)
    exponentials = jnp.exp(scores - row_peak[..., None])
    row_sum = jnp.sum(exponentials, axis=3)
    weights = exponentials.astype(jnp.bfloat16)
    blended = jnp.einsum(
        "shqk,skhd->sqhd", weights, value_block, preferred_element_type=jnp.float32
    )
    blended = blended / jnp.transpose(row_sum, (0, 2, 1))[..., None]
    return (blended, row_peak + jnp.log(row_sum))


def slot_plan(selected, first_span, per_dev, capacity):
    own_span = first_span + lax.broadcasted_iota(jnp.int32, selected.shape, 0)
    is_live = (selected != own_span).reshape(-1)
    owner_dev = (selected // per_dev).reshape(-1)
    pair_count = owner_dev.shape[0]
    is_later = lax.broadcasted_iota(jnp.int32, (pair_count, pair_count), 0) > lax.broadcasted_iota(
        jnp.int32, (pair_count, pair_count), 1
    )
    earlier = is_later & (owner_dev[:, None] == owner_dev[None, :]) & is_live[None, :]
    slot_rank = jnp.sum(earlier.astype(jnp.int32), axis=1)
    slot_index = jnp.where(is_live, owner_dev * capacity + slot_rank, 0)
    return (slot_index, is_live, (selected % per_dev).reshape(-1))


def shards(queries, keys, values, selection, norm_gain):
    n_ctx = lax.axis_size("ctx")
    device = lax.axis_index("ctx")
    rows, width = queries.shape
    per_dev, topk_count = selection.shape
    block_rows = rows // per_dev
    heads_dev = width // HD
    slot_count = n_ctx * CAP
    group_size = math.gcd(slot_count, 4)
    query_blocks = queries.reshape(per_dev, block_rows, heads_dev, HD)
    key_blocks = keys.reshape(per_dev, block_rows, heads_dev, HD)
    value_blocks = values.reshape(per_dev, block_rows, heads_dev, HD)
    slot_index, is_live, local_block = slot_plan(selection[:, 1:], device * per_dev, per_dev, CAP)
    pair_count = slot_index.shape[0]
    pair_span = lax.broadcasted_iota(jnp.int32, (pair_count,), 0) // (topk_count - 1)
    slot_ids = lax.broadcasted_iota(jnp.int32, (slot_count, pair_count), 0)
    placed = (slot_ids == slot_index[None, :]) & is_live[None, :]
    slot_span = jnp.sum(jnp.where(placed, pair_span[None, :], 0), axis=1)
    everyone = lax.all_gather(selection, "ctx", axis=0, tiled=True)
    requests = everyone[:, 1:].reshape(n_ctx, per_dev, topk_count - 1)
    first_spans = lax.broadcasted_iota(jnp.int32, (n_ctx,), 0) * per_dev
    all_slots, all_live, all_local = jax.vmap(partial(slot_plan, per_dev=per_dev, capacity=CAP))(
        requests, first_spans
    )
    owner_devs = requests.reshape(n_ctx, -1) // per_dev
    served = all_live & (owner_devs == device)
    capacity_ids = lax.broadcasted_iota(jnp.int32, (1, CAP, 1), 1)
    matched = served[:, None, :] & (all_slots[:, None, :] == device * CAP + capacity_ids)
    send_block = jnp.sum(jnp.where(matched, all_local[:, None, :], 0), axis=2)
    key_out = key_blocks[send_block].reshape(n_ctx, CAP, block_rows, width)
    value_out = value_blocks[send_block].reshape(n_ctx, CAP, block_rows, width)
    key_in, value_in = (
        lax.all_to_all(key_out, "ctx", split_axis=0, concat_axis=0, tiled=True),
        lax.all_to_all(value_out, "ctx", split_axis=0, concat_axis=0, tiled=True),
    )

    def one_group(packed):
        group_keys, group_values, group_span = packed
        blended, log_sums = partial_state(query_blocks[group_span], group_keys, group_values, False)
        return (blended.astype(jnp.bfloat16), log_sums)

    slot_out, slot_lse = lax.map(
        one_group,
        (
            key_in.reshape(-1, group_size, block_rows, heads_dev, HD),
            value_in.reshape(-1, group_size, block_rows, heads_dev, HD),
            slot_span.reshape(-1, group_size),
        ),
    )
    slot_out = slot_out.reshape(slot_count, block_rows, heads_dev, HD)
    slot_lse = slot_lse.reshape(slot_count, heads_dev, block_rows)
    own_out, own_lse = partial_state(query_blocks, key_blocks, value_blocks, True)
    live_pairs = is_live.reshape(per_dev, topk_count - 1)
    pair_out = (
        slot_out[slot_index]
        .reshape(per_dev, topk_count - 1, block_rows, heads_dev, HD)
        .astype(jnp.float32)
    )
    pair_lse = jnp.where(
        live_pairs[:, :, None, None],
        slot_lse[slot_index].reshape(per_dev, topk_count - 1, heads_dev, block_rows),
        -1e30,
    )
    highest = jnp.maximum(own_lse, jnp.max(pair_lse, axis=1))
    own_weight = jnp.exp(own_lse - highest)
    pair_weight = jnp.where(live_pairs[:, :, None, None], jnp.exp(pair_lse - highest[:, None]), 0.0)
    numerator = jnp.transpose(own_weight, (0, 2, 1))[..., None] * own_out
    numerator = numerator + jnp.sum(
        jnp.transpose(pair_weight, (0, 1, 3, 2))[..., None] * pair_out, axis=1
    )
    denominator = own_weight + jnp.sum(pair_weight, axis=1)
    attended = (numerator / jnp.transpose(denominator, (0, 2, 1))[..., None]).reshape(rows, width)
    squares = jnp.sum(attended * attended, axis=1)
    summed = lax.psum(squares, "head")
    factor = lax.rsqrt(summed / (HEADS * HD) + 1e-06)
    return (attended * factor[:, None] * norm_gain.astype(jnp.float32)[None, :]).astype(
        jnp.bfloat16
    )


LSE_ROWS = 32
UNROLL = 2
VMEM_LIMIT = 48 * 1024 * 1024


def unit_fields(code):
    return code & 31, (code >> 5) & 31, (code >> 10) & 63, (code >> 16) & 1, (code >> 17) & 1


def unit_code(slot, span, out, first, diagonal):
    return slot + span * 32 + out * 1024 + first * 65536 + diagonal * 131072


def attention_kernel(shape, own, plan, *refs):
    heads, n_q, n_kv, per_dev, block_rows = shape
    q_refs, refs = refs[:2], refs[2:]
    k_refs, refs = refs[:3], refs[3:]
    outs, refs = refs[:2], refs[2:]
    sides = (0,) if own else (0, 1)
    (q_scr, kv_scr, s0, s1, p0, p1, d0, d1, acc_scr, top_scr, sum_scr, o_scr, lse_scr, sems) = refs[:14]
    s_scr, p_scr, decay_scr = (s0, s1), (p0, p1), (d0, d1)
    spans = n_q * per_dev
    copies = []
    for h in range(heads):
        sources = [ref.at[h, 0] if own else ref.at[side, h] for ref in q_refs for side in sides]
        targets = [q_scr.at[h, i] for i in range(n_q)]
        for i in range(n_kv):
            sources.append(k_refs[i].at[h, pl.ds(1, 2)] if i < 2 else k_refs[2].at[i - 2, h])
            targets.append(kv_scr.at[h, i])
        for i, (source, target) in enumerate(zip(sources, targets)):
            copies.append(pltpu.make_async_copy(source, target, sems.at[h, i]))
    for copy in copies:
        copy.start()
    s1[...] = jnp.zeros_like(s1)
    p0[...] = jnp.zeros_like(p0)
    d0[...] = jnp.zeros_like(d0)
    acc_scr[...] = jnp.zeros_like(acc_scr)
    top_scr[...] = jnp.zeros_like(top_scr)
    sum_scr[...] = jnp.ones_like(sum_scr)
    if own:
        bias_scr = refs[14]
        key_pos = lax.broadcasted_iota(jnp.int32, (block_rows, block_rows), 0)
        query_pos = lax.broadcasted_iota(jnp.int32, (block_rows, block_rows), 1)
        bias_scr[0] = jnp.zeros((block_rows, block_rows), jnp.float32)
        bias_scr[1] = jnp.where(key_pos <= query_pos, 0.0, -1e30)
    for copy in copies:
        copy.wait()

    def rows_of(i):
        return pl.ds(pl.multiple_of((i % per_dev) * block_rows, block_rows), block_rows)

    def step(h, at, now, acc, top, total):
        before = 1 - now
        for u in range(UNROLL):
            slot, _, out, _, _ = unit_fields(plan[at + u])
            vt = kv_scr[h, slot // per_dev, 1, rows_of(slot), :]
            vt = jnp.concatenate([vt[:HD], vt[HD:]], axis=1)
            mixed = jnp.dot(vt, p_scr[now][u], preferred_element_type=jnp.float32)
            acc = acc * decay_scr[now][u, 0:1, :] + mixed
            o_scr[out] = (acc * decay_scr[now][u, 1:2, :]).astype(o_scr.dtype)
        for u in range(UNROLL):
            _, _, out, first, diagonal = unit_fields(plan[at + UNROLL + u])
            s = s_scr[before][u]
            if own:
                s = s + bias_scr[diagonal]
            old = jnp.where(first == 1, -1e30, top)
            top = jnp.maximum(old, jnp.max(s, axis=0, keepdims=True))
            decay = jnp.exp2((old - top) * EXP_SCALE)
            p = jnp.exp2((s - top) * EXP_SCALE)
            total = total * decay + jnp.sum(p, axis=0, keepdims=True)
            p_scr[before][u] = p.astype(jnp.bfloat16)
            decay_scr[before][u, 0:1, :] = decay
            decay_scr[before][u, 1:2, :] = 1.0 / total
            lse_scr[pl.ds(out, 1), :] = top * EXP_SCALE + jnp.log(total) * LOG2E
        for u in range(UNROLL):
            slot, span, _, _, _ = unit_fields(plan[at + 2 * UNROLL + u])
            k = kv_scr[h, slot // per_dev, 0, rows_of(slot), :]
            q = q_scr[h, span // per_dev, rows_of(span), :]
            s_scr[now][u] = lax.dot_general(
                k, q, (((1,), (1,)), ((), ())), preferred_element_type=jnp.float32
            )
        return acc, top, total

    for h in range(heads):
        o_scr[...] = jnp.zeros_like(o_scr)
        lse_scr[...] = jnp.full_like(lse_scr, -1e30)

        def two_steps(i, carry):
            state = (acc_scr[...], top_scr[...], sum_scr[...])
            state = step(h, 1 + 2 * i * UNROLL, 0, *state)
            state = step(h, 1 + (2 * i + 1) * UNROLL, 1, *state)
            acc_scr[...], top_scr[...], sum_scr[...] = state
            return carry

        lax.fori_loop(0, (plan[0] + 1) // 2, two_steps, 0)
        if own:
            outs[0][h] = o_scr[:spans]
            outs[1][h] = lse_scr[:spans, :]
        else:
            half = spans // 2
            for side in range(2):
                for span in range(half):
                    outs[side][h, span * HD : (span + 1) * HD, :] = o_scr[side * half + span]
                lse = lse_scr[side * half : (side + 1) * half, :]
                high = lse.astype(jnp.bfloat16).astype(jnp.float32)
                middle = (lse - high).astype(jnp.bfloat16).astype(jnp.float32)
                rest = jnp.zeros((LSE_ROWS - 3 * half, block_rows), jnp.float32)
                parts = jnp.concatenate([high, middle, lse - high - middle, rest], axis=0)
                outs[side][h, half * HD :, :] = parts.astype(jnp.bfloat16)


def ordered(kernel, n_after):
    def body(*refs):
        kernel(*refs[n_after:])

    return body


def attention_call(plan, q_pieces, kv_pieces, own, heads, per_dev, block_rows, after=()):
    n_q, n_kv = (2 if own else 4), 4
    spans = n_q * per_dev
    vmem, hbm = pl.BlockSpec(memory_space=pltpu.VMEM), pl.BlockSpec(memory_space=pltpu.HBM)
    f32, bf16 = jnp.float32, jnp.bfloat16
    if own:
        out_shape = (
            jax.ShapeDtypeStruct((heads, spans, HD, block_rows), f32),
            jax.ShapeDtypeStruct((heads, spans, block_rows), f32),
        )
    else:
        packed = jax.ShapeDtypeStruct((heads, spans // 2 * HD + LSE_ROWS, block_rows), bf16)
        out_shape = (packed, packed)
    scratch = [
        pltpu.VMEM((heads, n_q, per_dev * block_rows, HD), bf16),
        pltpu.VMEM((heads, n_kv, 2, per_dev * block_rows, HD), bf16),
        pltpu.VMEM((UNROLL, block_rows, block_rows), f32),
        pltpu.VMEM((UNROLL, block_rows, block_rows), f32),
        pltpu.VMEM((UNROLL, block_rows, block_rows), bf16),
        pltpu.VMEM((UNROLL, block_rows, block_rows), bf16),
        pltpu.VMEM((UNROLL, 8, block_rows), f32),
        pltpu.VMEM((UNROLL, 8, block_rows), f32),
        pltpu.VMEM((HD, block_rows), f32),
        pltpu.VMEM((1, block_rows), f32),
        pltpu.VMEM((1, block_rows), f32),
        pltpu.VMEM((spans + 1, HD, block_rows), f32 if own else bf16),
        pltpu.VMEM((spans + 8, block_rows), f32),
        pltpu.SemaphoreType.DMA((heads, n_q + n_kv)),
    ]
    if own:
        scratch.append(pltpu.VMEM((2, block_rows, block_rows), f32))
    return pl.pallas_call(
        ordered(partial(attention_kernel, (heads, n_q, n_kv, per_dev, block_rows), own), len(after)),
        out_shape=out_shape,
        in_specs=[hbm] * len(after) + [pl.BlockSpec(memory_space=pltpu.SMEM)] + [hbm] * 5,
        out_specs=(vmem, vmem),
        scratch_shapes=scratch,
        compiler_params=pltpu.CompilerParams(vmem_limit_bytes=VMEM_LIMIT),
        cost_estimate=pl.CostEstimate(flops=1, bytes_accessed=1, transcendentals=0),
        name="own_attention" if own else "served_attention",
    )(*after, plan, *q_pieces, *kv_pieces)


def pack_kernel(shape, place, q_ref, k_ref, v_ref, keep_ref, send_ref, v_scr, t_scr, sems):
    heads, first, half, rows = shape
    later, outs = [], (keep_ref, send_ref)
    loads = []
    n = 0
    for side in range(2):
        for h in range(heads):
            start = pl.multiple_of((place[side] * half + first + h) * HD, HD)
            load = pltpu.make_async_copy(v_ref.at[:, pl.ds(start, HD)], v_scr.at[side, h], sems.at[n])
            load.start()
            loads.append(load)
            n += 1
    for side in (1, 0):
        for h in range(heads):
            start = pl.multiple_of((place[side] * half + first + h) * HD, HD)
            for i, ref in enumerate((q_ref, k_ref)):
                copy = pltpu.make_async_copy(ref.at[:, pl.ds(start, HD)], outs[side].at[h, i], sems.at[n])
                copy.start()
                later.append(copy)
                n += 1
    for side in (1, 0):
        for h in range(heads):
            loads[side * heads + h].wait()
            for tile in range(rows // HD):
                at = slice(tile * HD, (tile + 1) * HD)
                t_scr[side, h, at, :] = v_scr[side, h, at, :].T
            copy = pltpu.make_async_copy(t_scr.at[side, h], outs[side].at[h, 2], sems.at[n])
            copy.start()
            later.append(copy)
            n += 1
    for copy in later:
        copy.wait()


def pack_call(place, queries, keys, values, heads, first, half, after=()):
    rows = queries.shape[0]
    hbm = pl.BlockSpec(memory_space=pltpu.HBM)
    packed = jax.ShapeDtypeStruct((heads, 3, rows, HD), jnp.bfloat16)
    return pl.pallas_call(
        ordered(partial(pack_kernel, (heads, first, half, rows)), len(after)),
        out_shape=(packed, packed),
        in_specs=[hbm] * len(after) + [pl.BlockSpec(memory_space=pltpu.SMEM)] + [hbm] * 3,
        out_specs=(hbm, hbm),
        scratch_shapes=[
            pltpu.VMEM((2, heads, rows, HD), jnp.bfloat16),
            pltpu.VMEM((2, heads, rows, HD), jnp.bfloat16),
            pltpu.SemaphoreType.DMA((8 * heads,)),
        ],
        compiler_params=pltpu.CompilerParams(vmem_limit_bytes=VMEM_LIMIT),
        cost_estimate=pl.CostEstimate(flops=1, bytes_accessed=1, transcendentals=0),
        name="pack",
    )(*after, place, queries, keys, values)


def join_kernel(heads, keep_ref, swap_ref, q_ref, kv_ref, scr, sems):
    loads, stores = [], []
    for side, ref in enumerate((keep_ref, swap_ref)):
        for h in range(heads):
            loads.append(pltpu.make_async_copy(ref.at[h], scr.at[side, h], sems.at[0, side, h]))
            stores.append(
                (
                    pltpu.make_async_copy(scr.at[side, h, 0], q_ref.at[side, h], sems.at[1, side, h]),
                    pltpu.make_async_copy(
                        scr.at[side, h, pl.ds(1, 2)], kv_ref.at[side, h], sems.at[2, side, h]
                    ),
                )
            )
    for load in loads:
        load.start()
    for load, pair in zip(loads, stores):
        load.wait()
        for store in pair:
            store.start()
    for pair in stores:
        for store in pair:
            store.wait()


def join_call(keep, swapped, after=()):
    heads, _, rows, _ = keep.shape
    hbm = pl.BlockSpec(memory_space=pltpu.HBM)
    return pl.pallas_call(
        ordered(partial(join_kernel, heads), len(after)),
        out_shape=(
            jax.ShapeDtypeStruct((2, heads, rows, HD), jnp.bfloat16),
            jax.ShapeDtypeStruct((2, heads, 2, rows, HD), jnp.bfloat16),
        ),
        in_specs=[hbm] * (len(after) + 2),
        out_specs=(hbm, hbm),
        scratch_shapes=[
            pltpu.VMEM((2, heads, 3, rows, HD), jnp.bfloat16),
            pltpu.SemaphoreType.DMA((3, 2, heads)),
        ],
        compiler_params=pltpu.CompilerParams(vmem_limit_bytes=VMEM_LIMIT),
        cost_estimate=pl.CostEstimate(flops=1, bytes_accessed=1, transcendentals=0),
        name="join",
    )(*after, keep, swapped)


def merge_kernel(shape, valid, own_ref, own_lse_ref, near_ref, far_ref, sofar_ref, keep_ref, send_ref, squares_ref):
    heads, per_dev, block_rows = shape
    spans = 2 * per_dev
    squares_ref[...] = sofar_ref[...]
    for h in range(heads):
        lses = [own_lse_ref[h]]
        for i, ref in enumerate((near_ref, far_ref)):
            parts = ref[h, spans * HD :, :].astype(jnp.float32)
            lse = parts[:spans] + parts[spans : 2 * spans] + parts[2 * spans : 3 * spans]
            lses.append(jnp.where(valid[i] > 0, lse, -1e30))
        top = jnp.maximum(jnp.maximum(lses[0], lses[1]), lses[2])
        weights = [jnp.exp2(lse - top) for lse in lses]
        scale = 1.0 / (weights[0] + weights[1] + weights[2])
        weights = [weight * scale for weight in weights]
        for span in range(spans):
            rows = slice(span, span + 1)
            tile = slice(span * HD, (span + 1) * HD)
            mixed = weights[0][rows, :] * own_ref[h, span]
            mixed = mixed + weights[1][rows, :] * near_ref[h, tile, :].astype(jnp.float32)
            mixed = mixed + weights[2][rows, :] * far_ref[h, tile, :].astype(jnp.float32)
            squares_ref[rows, :] = squares_ref[rows, :] + jnp.sum(mixed * mixed, axis=0, keepdims=True)
            target = keep_ref if span < per_dev else send_ref
            start = (span % per_dev) * block_rows
            target[h, start : start + block_rows, :] = mixed.T.astype(target.dtype)


def merge_call(valid, own, near, far, sofar, per_dev, after=()):
    heads, spans, _, block_rows = own[0].shape
    vmem = pl.BlockSpec(memory_space=pltpu.VMEM)
    packed = jax.ShapeDtypeStruct((heads, per_dev * block_rows, HD), jnp.bfloat16)
    return pl.pallas_call(
        ordered(partial(merge_kernel, (heads, per_dev, block_rows)), len(after)),
        out_shape=(packed, packed, jax.ShapeDtypeStruct((spans, block_rows), jnp.float32)),
        in_specs=[pl.BlockSpec(memory_space=pltpu.HBM)] * len(after) + [pl.BlockSpec(memory_space=pltpu.SMEM)] + [vmem] * 5,
        out_specs=(vmem, vmem, vmem),
        compiler_params=pltpu.CompilerParams(vmem_limit_bytes=VMEM_LIMIT),
        cost_estimate=pl.CostEstimate(flops=1, bytes_accessed=1, transcendentals=0),
        name="merge",
    )(*after, valid, own[0], own[1], near, far, sofar)


def finish_kernel(per_dev, sizes, place, *refs):
    n = len(sizes)
    kept, returned = refs[:n], refs[n : 2 * n]
    squares_ref, gain_ref, out_ref = refs[2 * n :]
    block_rows = squares_ref.shape[1]
    half = sum(sizes)
    factor = lax.rsqrt(squares_ref[...] / (HEADS * HD) + 1e-06)
    for b in range(per_dev):
        column = jnp.broadcast_to(factor[b : b + 1, :], (HD, block_rows)).T
        rows = slice(b * block_rows, (b + 1) * block_rows)
        for side, pieces in enumerate((kept, returned)):
            head = 0
            for piece, size in zip(pieces, sizes):
                for h in range(size):
                    start = pl.multiple_of((place[side] * half + head) * HD, HD)
                    gain = gain_ref[:, pl.ds(start, HD)].astype(jnp.float32)
                    value = piece[h, rows, :].astype(jnp.float32) * column * gain
                    out_ref[rows, pl.ds(start, HD)] = value.astype(out_ref.dtype)
                    head += 1


def finish_call(place, kept, returned, squares, gain, per_dev):
    vmem = pl.BlockSpec(memory_space=pltpu.VMEM)
    rows, width = kept[0].shape[1], gain.shape[0]
    return pl.pallas_call(
        partial(finish_kernel, per_dev, [k.shape[0] for k in kept]),
        out_shape=jax.ShapeDtypeStruct((rows, width), jnp.bfloat16),
        in_specs=[pl.BlockSpec(memory_space=pltpu.SMEM)] + [vmem] * (2 * len(kept) + 2),
        out_specs=vmem,
        compiler_params=pltpu.CompilerParams(vmem_limit_bytes=VMEM_LIMIT),
        cost_estimate=pl.CostEstimate(flops=1, bytes_accessed=1, transcendentals=0),
        name="finish",
    )(place, *kept, *returned, squares, gain.reshape(1, width))


def plan_of(live, slot, diagonal, dump):
    spans, entries = live.shape
    t = jnp.arange(entries)
    earlier = jnp.sum((t[None, None, :] < t[None, :, None]) & live[:, None, :], axis=2)
    span = lax.broadcasted_iota(jnp.int32, live.shape, 0)
    code = unit_code(slot, span, span, (earlier == 0).astype(jnp.int32), diagonal)
    code, live = code.reshape(-1), live.reshape(-1)
    n = spans * entries
    i = jnp.arange(n)
    rank = jnp.sum((i[None, :] < i[:, None]) & live[None, :], axis=1)
    at = jnp.arange(n + 8 * UNROLL)
    hit = live[None, :] & (rank[None, :] + 2 * UNROLL == at[:, None])
    idle = unit_code(0, 0, dump, 1, 0)
    codes = jnp.sum(jnp.where(hit, code[None, :] - idle, 0), axis=1) + idle
    total = jnp.sum(live.astype(jnp.int32))
    steps = jnp.where(total > 0, (total + UNROLL - 1) // UNROLL + 2, 0)
    return jnp.concatenate([steps[None], codes]).astype(jnp.int32)


def level_shards(queries, keys, values, selection, norm_gain):
    device = lax.axis_index("ctx")
    level, x = device // 2, device % 2
    rows, width = queries.shape
    per_dev, topk = selection.shape
    block_rows = rows // per_dev
    spans = 2 * per_dev
    half = width // HD // 2

    def to(array, pairs, name):
        with jax.named_scope(name):
            return lax.ppermute(array, "ctx", pairs)

    swap = [(d, d ^ 1) for d in range(8)]
    lift = [(0, 2), (1, 3)]
    near_down, far_down = [(4, 2), (5, 3), (6, 4), (7, 5)], [(6, 2), (7, 3)]
    near_up, far_up = [(2, 4), (3, 5), (4, 6), (5, 7)], [(2, 6), (3, 7)]
    valid = jnp.stack([level >= 2, level >= 3]).astype(jnp.int32)
    place = jnp.stack([x, 1 - x]).astype(jnp.int32)

    own_selection = jnp.concatenate([selection, to(selection, swap, "selection_swap")], axis=0)
    near_selection, far_selection = (
        to(own_selection, near_down, "selection_near"),
        to(own_selection, far_down, "selection_far"),
    )

    def ids(at):
        first = jnp.stack([(at * 2 + x) * per_dev, (at * 2 + 1 - x) * per_dev])
        return (first[:, None] + jnp.arange(per_dev)[None, :]).reshape(-1, 1)

    def slots(blocks):
        owner = blocks // per_dev
        slot = jnp.where(owner // 2 == level, 0, spans) + jnp.where(owner % 2 == x, 0, per_dev)
        return owner // 2, slot + blocks % per_dev

    others = own_selection[:, 1:]
    block_level, slot = slots(others)
    live = (others != ids(level)) & ((block_level == level) | ((level == 1) & (block_level == 0)))
    first = jnp.ones((spans, 1), jnp.int32)
    own_plan = plan_of(
        jnp.concatenate([first > 0, live], axis=1),
        jnp.concatenate([jnp.arange(spans, dtype=jnp.int32)[:, None], slot], axis=1),
        jnp.concatenate([first, jnp.zeros_like(others)], axis=1),
        spans,
    )
    others = jnp.concatenate([near_selection, far_selection], axis=0)[:, 1:]
    block_level, slot = slots(others)
    is_near = lax.broadcasted_iota(jnp.int32, others.shape, 0) < spans
    mine = ((level == 1) & (block_level <= 1)) | ((level == 2) & (block_level == 2) & is_near)
    live = (others != jnp.concatenate([ids(level + 1), ids(level + 2)], axis=0)) & mine
    served_plan = plan_of(live, slot, jnp.zeros_like(others), 2 * spans)

    sizes = [1] * half
    n = len(sizes)
    packs, lows, nears, fars, levels = [None] * n, [None] * n, [None] * n, [None] * n, [None] * n
    ups, owns, kept, returned = [None] * n, [None] * n, [None] * n, [None] * n
    squares = [jnp.zeros((spans, block_rows), jnp.float32)]
    last = []

    def pack(c, after=()):
        keep, send = pack_call(
            place, queries, keys, values, sizes[c], sum(sizes[:c]), half, (*after, *last)
        )
        last[:] = [keep]
        packs[c] = (keep, to(send, swap, f"swap_c{c}"))

    def join(c):
        level_q, level_kv = join_call(*packs[c], last)
        last[:] = [level_q]
        lows[c] = to(level_kv, lift, f"lift_c{c}")
        fars[c] = to(level_q, far_down, f"far_down_c{c}")
        nears[c] = to(level_q, near_down, f"near_down_c{c}")

    def serve(c):
        kv, q = [*packs[c], lows[c]], [nears[c], fars[c]]
        near, far = attention_call(served_plan, q, kv, False, sizes[c], per_dev, block_rows, last)
        last[:] = [near]
        ups[c] = (to(near, near_up, f"near_up_c{c}"), to(far, far_up, f"far_up_c{c}"))

    def attend(c):
        kv = [*packs[c], lows[c]]
        owns[c] = attention_call(own_plan, packs[c], kv, True, sizes[c], per_dev, block_rows, last)
        last[:] = [owns[c][1]]

    def merge(c):
        keep, send, total = merge_call(valid, owns[c], *ups[c], squares[0], per_dev, last)
        squares[0] = total
        last[:] = [keep]
        kept[c], returned[c] = keep, to(send, swap, f"back_c{c}")

    pack(0)
    pack(1, (own_plan, served_plan))
    join(0)
    pack(2)
    join(1)
    serve(0)
    attend(0)
    join(2)
    pack(3)
    serve(1)
    attend(1)
    merge(0)
    join(3)
    serve(2)
    attend(2)
    merge(1)
    serve(3)
    merge(2)
    attend(3)
    merge(3)
    squares = squares[0]
    square = squares[:per_dev] + to(squares[per_dev:], swap, "squares_swap")
    n_head = lax.axis_size("head")
    hop = 1
    while hop < n_head:
        square = square + lax.ppermute(square, "head", [(i, i ^ hop) for i in range(n_head)])
        hop *= 2
    return finish_call(place, kept, returned, square, norm_gain, per_dev)


def solution(mesh):
    placed = (P("ctx", "head"), P("ctx", "head"), P("ctx", "head"), P("ctx", None), P("head"))
    body = level_shards if mesh.shape["ctx"] == 8 else shards
    return jax.shard_map(
        body, mesh=mesh, in_specs=placed, out_specs=P("ctx", "head"), check_vma=False
    )
```

```python
from functools import partial
import math

import jax
import jax.numpy as jnp
from jax import lax
from jax.experimental import pallas as pl
from jax.experimental.pallas import tpu as pltpu
from jax.sharding import PartitionSpec as P

HEADS = 32
HD = 128
CAP = 2
LOG2E = math.log2(math.e)
EXP_SCALE = HD ** (-0.5) * LOG2E


def partial_state(query_rows, key_block, value_block, causal):
    scores = jnp.einsum(
        "sqhd,skhd->shqk", query_rows, key_block, preferred_element_type=jnp.float32
    ) * query_rows.shape[3] ** (-0.5)
    if causal:
        query_pos = lax.broadcasted_iota(jnp.int32, scores.shape, 2)
        key_pos = lax.broadcasted_iota(jnp.int32, scores.shape, 3)
        scores = jnp.where(key_pos <= query_pos, scores, -1e30)
    row_peak = jnp.max(scores, axis=3)
    exponentials = jnp.exp(scores - row_peak[..., None])
    row_sum = jnp.sum(exponentials, axis=3)
    weights = exponentials.astype(jnp.bfloat16)
    blended = jnp.einsum(
        "shqk,skhd->sqhd", weights, value_block, preferred_element_type=jnp.float32
    )
    blended = blended / jnp.transpose(row_sum, (0, 2, 1))[..., None]
    return (blended, row_peak + jnp.log(row_sum))


def slot_plan(selected, first_span, per_dev, capacity):
    own_span = first_span + lax.broadcasted_iota(jnp.int32, selected.shape, 0)
    is_live = (selected != own_span).reshape(-1)
    owner_dev = (selected // per_dev).reshape(-1)
    pair_count = owner_dev.shape[0]
    is_later = lax.broadcasted_iota(jnp.int32, (pair_count, pair_count), 0) > lax.broadcasted_iota(
        jnp.int32, (pair_count, pair_count), 1
    )
    earlier = is_later & (owner_dev[:, None] == owner_dev[None, :]) & is_live[None, :]
    slot_rank = jnp.sum(earlier.astype(jnp.int32), axis=1)
    slot_index = jnp.where(is_live, owner_dev * capacity + slot_rank, 0)
    return (slot_index, is_live, (selected % per_dev).reshape(-1))


def shards(queries, keys, values, selection, norm_gain):
    n_ctx = lax.axis_size("ctx")
    device = lax.axis_index("ctx")
    rows, width = queries.shape
    per_dev, topk_count = selection.shape
    block_rows = rows // per_dev
    heads_dev = width // HD
    slot_count = n_ctx * CAP
    group_size = math.gcd(slot_count, 4)
    query_blocks = queries.reshape(per_dev, block_rows, heads_dev, HD)
    key_blocks = keys.reshape(per_dev, block_rows, heads_dev, HD)
    value_blocks = values.reshape(per_dev, block_rows, heads_dev, HD)
    slot_index, is_live, local_block = slot_plan(selection[:, 1:], device * per_dev, per_dev, CAP)
    pair_count = slot_index.shape[0]
    pair_span = lax.broadcasted_iota(jnp.int32, (pair_count,), 0) // (topk_count - 1)
    slot_ids = lax.broadcasted_iota(jnp.int32, (slot_count, pair_count), 0)
    placed = (slot_ids == slot_index[None, :]) & is_live[None, :]
    slot_span = jnp.sum(jnp.where(placed, pair_span[None, :], 0), axis=1)
    everyone = lax.all_gather(selection, "ctx", axis=0, tiled=True)
    requests = everyone[:, 1:].reshape(n_ctx, per_dev, topk_count - 1)
    first_spans = lax.broadcasted_iota(jnp.int32, (n_ctx,), 0) * per_dev
    all_slots, all_live, all_local = jax.vmap(partial(slot_plan, per_dev=per_dev, capacity=CAP))(
        requests, first_spans
    )
    owner_devs = requests.reshape(n_ctx, -1) // per_dev
    served = all_live & (owner_devs == device)
    capacity_ids = lax.broadcasted_iota(jnp.int32, (1, CAP, 1), 1)
    matched = served[:, None, :] & (all_slots[:, None, :] == device * CAP + capacity_ids)
    send_block = jnp.sum(jnp.where(matched, all_local[:, None, :], 0), axis=2)
    key_out = key_blocks[send_block].reshape(n_ctx, CAP, block_rows, width)
    value_out = value_blocks[send_block].reshape(n_ctx, CAP, block_rows, width)
    key_in, value_in = (
        lax.all_to_all(key_out, "ctx", split_axis=0, concat_axis=0, tiled=True),
        lax.all_to_all(value_out, "ctx", split_axis=0, concat_axis=0, tiled=True),
    )

    def one_group(packed):
        group_keys, group_values, group_span = packed
        blended, log_sums = partial_state(query_blocks[group_span], group_keys, group_values, False)
        return (blended.astype(jnp.bfloat16), log_sums)

    slot_out, slot_lse = lax.map(
        one_group,
        (
            key_in.reshape(-1, group_size, block_rows, heads_dev, HD),
            value_in.reshape(-1, group_size, block_rows, heads_dev, HD),
            slot_span.reshape(-1, group_size),
        ),
    )
    slot_out = slot_out.reshape(slot_count, block_rows, heads_dev, HD)
    slot_lse = slot_lse.reshape(slot_count, heads_dev, block_rows)
    own_out, own_lse = partial_state(query_blocks, key_blocks, value_blocks, True)
    live_pairs = is_live.reshape(per_dev, topk_count - 1)
    pair_out = (
        slot_out[slot_index]
        .reshape(per_dev, topk_count - 1, block_rows, heads_dev, HD)
        .astype(jnp.float32)
    )
    pair_lse = jnp.where(
        live_pairs[:, :, None, None],
        slot_lse[slot_index].reshape(per_dev, topk_count - 1, heads_dev, block_rows),
        -1e30,
    )
    highest = jnp.maximum(own_lse, jnp.max(pair_lse, axis=1))
    own_weight = jnp.exp(own_lse - highest)
    pair_weight = jnp.where(live_pairs[:, :, None, None], jnp.exp(pair_lse - highest[:, None]), 0.0)
    numerator = jnp.transpose(own_weight, (0, 2, 1))[..., None] * own_out
    numerator = numerator + jnp.sum(
        jnp.transpose(pair_weight, (0, 1, 3, 2))[..., None] * pair_out, axis=1
    )
    denominator = own_weight + jnp.sum(pair_weight, axis=1)
    attended = (numerator / jnp.transpose(denominator, (0, 2, 1))[..., None]).reshape(rows, width)
    squares = jnp.sum(attended * attended, axis=1)
    summed = lax.psum(squares, "head")
    factor = lax.rsqrt(summed / (HEADS * HD) + 1e-06)
    return (attended * factor[:, None] * norm_gain.astype(jnp.float32)[None, :]).astype(
        jnp.bfloat16
    )


SIZES = (1, 1, 1, 1,)
SPLIT = (False, False, False, False,)
ORDER = (
    ("p", 0),
    ("w", "plans"),
    ("p", 1),
    ("j", 0),
    ("p", 2),
    ("j", 1),
    ("p", 3),
    ("s", 0),
    ("a", 0),
    ("j", 2),
    ("s", 1),
    ("a", 1),
    ("w", "lift_c1"),
    ("m", 0),
    ("j", 3),
    ("s", 2),
    ("w", "near_up_c1"),
    ("a", 2),
    ("m", 1),
    ("s", 3),
    ("m", 2),
    ("a", 3),
    ("m", 3),
)
LSE_ROWS = 32
UNROLL = 2
VMEM_LIMIT = 63 * 1024 * 1024


def unit_fields(code):
    return code & 31, (code >> 5) & 31, (code >> 10) & 63, (code >> 16) & 1, (code >> 17) & 1


def unit_code(slot, span, out, first, diagonal):
    return slot + span * 32 + out * 1024 + first * 65536 + diagonal * 131072


PIECES = {
    "head": lambda ref, h: ref.at[h],
    "queries": lambda ref, h: ref.at[h, 0],
    "keys_values": lambda ref, h: ref.at[h, pl.ds(1, 2)],
    "first": lambda ref, h: ref.at[0, h],
    "second": lambda ref, h: ref.at[1, h],
}


def attention_kernel(shape, own, q_pieces, kv_pieces, n_in, plan, *refs):
    heads, per_dev, block_rows = shape
    n_q, n_kv = len(q_pieces), len(kv_pieces)
    inputs, refs = refs[:n_in], refs[n_in:]
    outs, refs = refs[:2], refs[2:]
    (q_scr, kv_scr, s0, s1, p0, p1, d0, d1, acc_scr, top_scr, sum_scr, o_scr, lse_scr, sems) = refs[:14]
    s_scr, p_scr, decay_scr = (s0, s1), (p0, p1), (d0, d1)
    spans = n_q * per_dev
    copies = []
    for h in range(heads):
        for i, (n, kind) in enumerate(q_pieces):
            copies.append((PIECES[kind](inputs[n], h), q_scr.at[h, i], sems.at[h, i]))
        for i, (n, kind) in enumerate(kv_pieces):
            copies.append((PIECES[kind](inputs[n], h), kv_scr.at[h, i], sems.at[h, n_q + i]))
    copies = [pltpu.make_async_copy(*copy) for copy in copies]
    for copy in copies:
        copy.start()
    s1[...] = jnp.zeros_like(s1)
    p0[...] = jnp.zeros_like(p0)
    d0[...] = jnp.zeros_like(d0)
    acc_scr[...] = jnp.zeros_like(acc_scr)
    top_scr[...] = jnp.zeros_like(top_scr)
    sum_scr[...] = jnp.ones_like(sum_scr)
    if own:
        bias_scr = refs[14]
        key_pos = lax.broadcasted_iota(jnp.int32, (block_rows, block_rows), 0)
        query_pos = lax.broadcasted_iota(jnp.int32, (block_rows, block_rows), 1)
        bias_scr[0] = jnp.zeros((block_rows, block_rows), jnp.float32)
        bias_scr[1] = jnp.where(key_pos <= query_pos, 0.0, -1e30)
    for copy in copies:
        copy.wait()

    def rows_of(i):
        return pl.ds(pl.multiple_of((i % per_dev) * block_rows, block_rows), block_rows)

    def step(h, at, now, acc, top, total):
        before = 1 - now
        for u in range(UNROLL):
            slot, _, out, _, _ = unit_fields(plan[at + u])
            vt = kv_scr[h, slot // per_dev, 1, rows_of(slot), :]
            vt = jnp.concatenate([vt[:HD], vt[HD:]], axis=1)
            mixed = jnp.dot(vt, p_scr[now][u], preferred_element_type=jnp.float32)
            acc = acc * decay_scr[now][u, 0:1, :] + mixed
            o_scr[out] = (acc * decay_scr[now][u, 1:2, :]).astype(o_scr.dtype)
        for u in range(UNROLL):
            _, _, out, first, diagonal = unit_fields(plan[at + UNROLL + u])
            s = s_scr[before][u]
            if own:
                s = s + bias_scr[diagonal]
            old = jnp.where(first == 1, -1e30, top)
            top = jnp.maximum(old, jnp.max(s, axis=0, keepdims=True))
            decay = jnp.exp2((old - top) * EXP_SCALE)
            p = jnp.exp2((s - top) * EXP_SCALE)
            total = total * decay + jnp.sum(p, axis=0, keepdims=True)
            p_scr[before][u] = p.astype(jnp.bfloat16)
            decay_scr[before][u, 0:1, :] = decay
            decay_scr[before][u, 1:2, :] = 1.0 / total
            lse_scr[pl.ds(out, 1), :] = top * EXP_SCALE + jnp.log(total) * LOG2E
        for u in range(UNROLL):
            slot, span, _, _, _ = unit_fields(plan[at + 2 * UNROLL + u])
            k = kv_scr[h, slot // per_dev, 0, rows_of(slot), :]
            q = q_scr[h, span // per_dev, rows_of(span), :]
            s_scr[now][u] = lax.dot_general(
                k, q, (((1,), (1,)), ((), ())), preferred_element_type=jnp.float32
            )
        return acc, top, total

    for h in range(heads):
        o_scr[...] = jnp.zeros_like(o_scr)
        lse_scr[...] = jnp.full_like(lse_scr, -1e30)

        def two_steps(i, carry):
            state = (acc_scr[...], top_scr[...], sum_scr[...])
            state = step(h, 1 + 2 * i * UNROLL, 0, *state)
            state = step(h, 1 + (2 * i + 1) * UNROLL, 1, *state)
            acc_scr[...], top_scr[...], sum_scr[...] = state
            return carry

        lax.fori_loop(0, (plan[0] + 1) // 2, two_steps, 0)
        if own:
            outs[0][h] = o_scr[:spans]
            outs[1][h] = lse_scr[:spans, :]
        else:
            half = spans // 2
            for side in range(2):
                for span in range(half):
                    outs[side][h, span * HD : (span + 1) * HD, :] = o_scr[side * half + span]
                lse = lse_scr[side * half : (side + 1) * half, :]
                high = lse.astype(jnp.bfloat16).astype(jnp.float32)
                middle = (lse - high).astype(jnp.bfloat16).astype(jnp.float32)
                rest = jnp.zeros((LSE_ROWS - 3 * half, block_rows), jnp.float32)
                parts = jnp.concatenate([high, middle, lse - high - middle, rest], axis=0)
                outs[side][h, half * HD :, :] = parts.astype(jnp.bfloat16)


def ordered(kernel, n_after):
    def body(*refs):
        kernel(*refs[n_after:])

    return body


def attention_call(plan, q_pieces, kv_pieces, own, heads, per_dev, block_rows, after=()):
    inputs = []

    def numbered(pieces):
        out = []
        for array, kind in pieces:
            if not any(array is known for known in inputs):
                inputs.append(array)
            out.append(([array is known for known in inputs].index(True), kind))
        return out

    q_pieces, kv_pieces = numbered(q_pieces), numbered(kv_pieces)
    n_q, n_kv = len(q_pieces), len(kv_pieces)
    spans = n_q * per_dev
    vmem, hbm = pl.BlockSpec(memory_space=pltpu.VMEM), pl.BlockSpec(memory_space=pltpu.HBM)
    f32, bf16 = jnp.float32, jnp.bfloat16
    if own:
        out_shape = (
            jax.ShapeDtypeStruct((heads, spans, HD, block_rows), f32),
            jax.ShapeDtypeStruct((heads, spans, block_rows), f32),
        )
    else:
        packed = jax.ShapeDtypeStruct((heads, spans // 2 * HD + LSE_ROWS, block_rows), bf16)
        out_shape = (packed, packed)
    scratch = [
        pltpu.VMEM((heads, n_q, per_dev * block_rows, HD), bf16),
        pltpu.VMEM((heads, n_kv, 2, per_dev * block_rows, HD), bf16),
        pltpu.VMEM((UNROLL, block_rows, block_rows), f32),
        pltpu.VMEM((UNROLL, block_rows, block_rows), f32),
        pltpu.VMEM((UNROLL, block_rows, block_rows), bf16),
        pltpu.VMEM((UNROLL, block_rows, block_rows), bf16),
        pltpu.VMEM((UNROLL, 8, block_rows), f32),
        pltpu.VMEM((UNROLL, 8, block_rows), f32),
        pltpu.VMEM((HD, block_rows), f32),
        pltpu.VMEM((1, block_rows), f32),
        pltpu.VMEM((1, block_rows), f32),
        pltpu.VMEM((spans + 1, HD, block_rows), f32 if own else bf16),
        pltpu.VMEM((spans + 8, block_rows), f32),
        pltpu.SemaphoreType.DMA((heads, n_q + n_kv)),
    ]
    if own:
        scratch.append(pltpu.VMEM((2, block_rows, block_rows), f32))
    return pl.pallas_call(
        ordered(
            partial(
                attention_kernel, (heads, per_dev, block_rows), own, q_pieces, kv_pieces, len(inputs)
            ),
            len(after),
        ),
        out_shape=out_shape,
        in_specs=[hbm] * len(after) + [pl.BlockSpec(memory_space=pltpu.SMEM)] + [hbm] * len(inputs),
        out_specs=(vmem, vmem),
        scratch_shapes=scratch,
        compiler_params=pltpu.CompilerParams(vmem_limit_bytes=VMEM_LIMIT),
        cost_estimate=pl.CostEstimate(flops=1, bytes_accessed=1, transcendentals=0),
        name="own_attention" if own else "served_attention",
    )(*after, plan, *inputs)


def pack_kernel(shape, place, q_ref, k_ref, v_ref, *refs):
    heads, first, half, rows, split = shape
    outs, (scr, t_scr, sems) = refs[:-3], refs[-3:]
    loads, stores = {}, []
    for side in (1, 0):
        for h in range(heads):
            start = pl.multiple_of((place[side] * half + first + h) * HD, HD)
            for i, ref in enumerate((q_ref, k_ref, v_ref)):
                load = pltpu.make_async_copy(
                    ref.at[:, pl.ds(start, HD)], scr.at[side, h, i], sems.at[0, side, h, i]
                )
                load.start()
                loads[side, h, i] = load

    def store(side, h, i, source):
        if split:
            out = outs[2 * side + (i > 0)]
            target = out.at[h, i - 1] if i else out.at[h]
        else:
            target = outs[side].at[h, i]
        copy = pltpu.make_async_copy(source, target, sems.at[1, side, h, i])
        copy.start()
        stores.append(copy)

    for side in (1, 0):
        for h in range(heads):
            for i in range(2):
                loads[side, h, i].wait()
                store(side, h, i, scr.at[side, h, i])
            loads[side, h, 2].wait()
            for tile in range(rows // HD):
                at = slice(tile * HD, (tile + 1) * HD)
                t_scr[side, h, at, :] = scr[side, h, 2, at, :].T
            store(side, h, 2, t_scr.at[side, h])
    for copy in stores:
        copy.wait()


def pack_call(place, queries, keys, values, heads, first, half, split, after=()):
    rows = queries.shape[0]
    hbm = pl.BlockSpec(memory_space=pltpu.HBM)
    bf16 = jnp.bfloat16
    if split:
        side = [
            jax.ShapeDtypeStruct((heads, rows, HD), bf16),
            jax.ShapeDtypeStruct((heads, 2, rows, HD), bf16),
        ]
    else:
        side = [jax.ShapeDtypeStruct((heads, 3, rows, HD), bf16)]
    return pl.pallas_call(
        ordered(partial(pack_kernel, (heads, first, half, rows, split)), len(after)),
        out_shape=side * 2,
        in_specs=[hbm] * len(after) + [pl.BlockSpec(memory_space=pltpu.SMEM)] + [hbm] * 3,
        out_specs=[hbm] * (2 * len(side)),
        scratch_shapes=[
            pltpu.VMEM((2, heads, 3, rows, HD), bf16),
            pltpu.VMEM((2, heads, rows, HD), bf16),
            pltpu.SemaphoreType.DMA((2, 2, heads, 3)),
        ],
        compiler_params=pltpu.CompilerParams(vmem_limit_bytes=VMEM_LIMIT),
        cost_estimate=pl.CostEstimate(flops=1, bytes_accessed=1, transcendentals=0),
        name="pack",
    )(*after, place, queries, keys, values)


def join_kernel(heads, keep_ref, swap_ref, q_ref, kv_ref, scr, sems):
    loads, stores = [], []
    for side, ref in enumerate((keep_ref, swap_ref)):
        for h in range(heads):
            loads.append(pltpu.make_async_copy(ref.at[h], scr.at[side, h], sems.at[0, side, h]))
            stores.append(
                (
                    pltpu.make_async_copy(scr.at[side, h, 0], q_ref.at[side, h], sems.at[1, side, h]),
                    pltpu.make_async_copy(
                        scr.at[side, h, pl.ds(1, 2)], kv_ref.at[side, h], sems.at[2, side, h]
                    ),
                )
            )
    for load in loads:
        load.start()
    for load, pair in zip(loads, stores):
        load.wait()
        for store in pair:
            store.start()
    for pair in stores:
        for store in pair:
            store.wait()


def join_call(keep, swapped, after=()):
    heads, _, rows, _ = keep.shape
    hbm = pl.BlockSpec(memory_space=pltpu.HBM)
    return pl.pallas_call(
        ordered(partial(join_kernel, heads), len(after)),
        out_shape=(
            jax.ShapeDtypeStruct((2, heads, rows, HD), jnp.bfloat16),
            jax.ShapeDtypeStruct((2, heads, 2, rows, HD), jnp.bfloat16),
        ),
        in_specs=[hbm] * (len(after) + 2),
        out_specs=(hbm, hbm),
        scratch_shapes=[
            pltpu.VMEM((2, heads, 3, rows, HD), jnp.bfloat16),
            pltpu.SemaphoreType.DMA((3, 2, heads)),
        ],
        compiler_params=pltpu.CompilerParams(vmem_limit_bytes=VMEM_LIMIT),
        cost_estimate=pl.CostEstimate(flops=1, bytes_accessed=1, transcendentals=0),
        name="join",
    )(*after, keep, swapped)


def merge_kernel(per_dev, block_rows, sizes, valid, sofar_ref, *refs):
    inputs, (keep_ref, send_ref, squares_ref) = refs[:-3], refs[-3:]
    spans = 2 * per_dev
    squares_ref[...] = sofar_ref[...]
    at = 0
    for c, size in enumerate(sizes):
        own_ref, own_lse_ref, near_ref, far_ref = inputs[4 * c : 4 * c + 4]
        for h in range(size):
            lses = [own_lse_ref[h]]
            for i, ref in enumerate((near_ref, far_ref)):
                parts = ref[h, spans * HD :, :].astype(jnp.float32)
                lse = parts[:spans] + parts[spans : 2 * spans] + parts[2 * spans : 3 * spans]
                lses.append(jnp.where(valid[i] > 0, lse, -1e30))
            top = jnp.maximum(jnp.maximum(lses[0], lses[1]), lses[2])
            weights = [jnp.exp2(lse - top) for lse in lses]
            scale = 1.0 / (weights[0] + weights[1] + weights[2])
            weights = [weight * scale for weight in weights]
            for span in range(spans):
                rows = slice(span, span + 1)
                tile = slice(span * HD, (span + 1) * HD)
                mixed = weights[0][rows, :] * own_ref[h, span]
                mixed = mixed + weights[1][rows, :] * near_ref[h, tile, :].astype(jnp.float32)
                mixed = mixed + weights[2][rows, :] * far_ref[h, tile, :].astype(jnp.float32)
                squares_ref[rows, :] = squares_ref[rows, :] + jnp.sum(mixed * mixed, axis=0, keepdims=True)
                target = keep_ref if span < per_dev else send_ref
                start = (span % per_dev) * block_rows
                target[at, start : start + block_rows, :] = mixed.T.astype(target.dtype)
            at += 1


def merge_call(valid, sofar, parts, per_dev, after=()):
    block_rows = sofar.shape[1]
    sizes = [own[0].shape[0] for own, _, _ in parts]
    arrays = [array for own, near, far in parts for array in (*own, near, far)]
    vmem = pl.BlockSpec(memory_space=pltpu.VMEM)
    hbm = pl.BlockSpec(memory_space=pltpu.HBM)
    packed = jax.ShapeDtypeStruct((sum(sizes), per_dev * block_rows, HD), jnp.bfloat16)
    return pl.pallas_call(
        ordered(partial(merge_kernel, per_dev, block_rows, sizes), len(after)),
        out_shape=(packed, packed, jax.ShapeDtypeStruct(sofar.shape, jnp.float32)),
        in_specs=[hbm] * len(after)
        + [pl.BlockSpec(memory_space=pltpu.SMEM)]
        + [vmem] * (1 + len(arrays)),
        out_specs=(vmem, vmem, vmem),
        compiler_params=pltpu.CompilerParams(vmem_limit_bytes=VMEM_LIMIT),
        cost_estimate=pl.CostEstimate(flops=1, bytes_accessed=1, transcendentals=0),
        name="merge",
    )(*after, valid, sofar, *arrays)


def finish_kernel(per_dev, sizes, place, *refs):
    n = len(sizes)
    kept, returned = refs[:n], refs[n : 2 * n]
    squares_ref, gain_ref, out_ref = refs[2 * n :]
    block_rows = squares_ref.shape[1]
    half = sum(sizes)
    factor = lax.rsqrt(squares_ref[...] / (HEADS * HD) + 1e-06)
    for b in range(per_dev):
        column = jnp.broadcast_to(factor[b : b + 1, :], (HD, block_rows)).T
        rows = slice(b * block_rows, (b + 1) * block_rows)
        for side, pieces in enumerate((kept, returned)):
            head = 0
            for piece, size in zip(pieces, sizes):
                for h in range(size):
                    start = pl.multiple_of((place[side] * half + head) * HD, HD)
                    gain = gain_ref[:, pl.ds(start, HD)].astype(jnp.float32)
                    value = piece[h, rows, :].astype(jnp.float32) * column * gain
                    out_ref[rows, pl.ds(start, HD)] = value.astype(out_ref.dtype)
                    head += 1


def finish_call(place, kept, returned, squares, gain, per_dev):
    vmem = pl.BlockSpec(memory_space=pltpu.VMEM)
    rows, width = kept[0].shape[1], gain.shape[0]
    return pl.pallas_call(
        partial(finish_kernel, per_dev, [k.shape[0] for k in kept]),
        out_shape=jax.ShapeDtypeStruct((rows, width), jnp.bfloat16),
        in_specs=[pl.BlockSpec(memory_space=pltpu.SMEM)] + [vmem] * (2 * len(kept) + 2),
        out_specs=vmem,
        compiler_params=pltpu.CompilerParams(vmem_limit_bytes=VMEM_LIMIT),
        cost_estimate=pl.CostEstimate(flops=1, bytes_accessed=1, transcendentals=0),
        name="finish",
    )(place, *kept, *returned, squares, gain.reshape(1, width))


def plan_of(live, slot, diagonal, dump):
    spans, entries = live.shape
    t = jnp.arange(entries)
    earlier = jnp.sum((t[None, None, :] < t[None, :, None]) & live[:, None, :], axis=2)
    span = lax.broadcasted_iota(jnp.int32, live.shape, 0)
    code = unit_code(slot, span, span, (earlier == 0).astype(jnp.int32), diagonal)
    code, live = code.reshape(-1), live.reshape(-1)
    n = spans * entries
    i = jnp.arange(n)
    rank = jnp.sum((i[None, :] < i[:, None]) & live[None, :], axis=1)
    at = jnp.arange(n + 8 * UNROLL)
    hit = live[None, :] & (rank[None, :] + 2 * UNROLL == at[:, None])
    idle = unit_code(0, 0, dump, 1, 0)
    codes = jnp.sum(jnp.where(hit, code[None, :] - idle, 0), axis=1) + idle
    total = jnp.sum(live.astype(jnp.int32))
    steps = jnp.where(total > 0, (total + UNROLL - 1) // UNROLL + 2, 0)
    return jnp.concatenate([steps[None], codes]).astype(jnp.int32)


def level_shards(queries, keys, values, selection, norm_gain):
    device = lax.axis_index("ctx")
    level, x = device // 2, device % 2
    rows, width = queries.shape
    per_dev, topk = selection.shape
    block_rows = rows // per_dev
    spans = 2 * per_dev
    half = width // HD // 2

    sent = {}

    def to(array, pairs, name):
        with jax.named_scope(name):
            sent[name] = lax.ppermute(array, "ctx", pairs)
        return sent[name]

    swap = [(d, d ^ 1) for d in range(8)]
    lift = [(0, 2), (1, 3)]
    near_down, far_down = [(4, 2), (5, 3), (6, 4), (7, 5)], [(6, 2), (7, 3)]
    near_up, far_up = [(2, 4), (3, 5), (4, 6), (5, 7)], [(2, 6), (3, 7)]
    valid = jnp.stack([level >= 2, level >= 3]).astype(jnp.int32)
    place = jnp.stack([x, 1 - x]).astype(jnp.int32)

    own_selection = jnp.concatenate([selection, to(selection, swap, "selection_swap")], axis=0)
    near_selection, far_selection = (
        to(own_selection, near_down, "selection_near"),
        to(own_selection, far_down, "selection_far"),
    )

    def ids(at):
        first = jnp.stack([(at * 2 + x) * per_dev, (at * 2 + 1 - x) * per_dev])
        return (first[:, None] + jnp.arange(per_dev)[None, :]).reshape(-1, 1)

    def slots(blocks):
        owner = blocks // per_dev
        slot = jnp.where(owner // 2 == level, 0, spans) + jnp.where(owner % 2 == x, 0, per_dev)
        return owner // 2, slot + blocks % per_dev

    others = own_selection[:, 1:]
    block_level, slot = slots(others)
    live = (others != ids(level)) & ((block_level == level) | ((level == 1) & (block_level == 0)))
    first = jnp.ones((spans, 1), jnp.int32)
    own_plan = plan_of(
        jnp.concatenate([first > 0, live], axis=1),
        jnp.concatenate([jnp.arange(spans, dtype=jnp.int32)[:, None], slot], axis=1),
        jnp.concatenate([first, jnp.zeros_like(others)], axis=1),
        spans,
    )
    others = jnp.concatenate([near_selection, far_selection], axis=0)[:, 1:]
    block_level, slot = slots(others)
    is_near = lax.broadcasted_iota(jnp.int32, others.shape, 0) < spans
    mine = ((level == 1) & (block_level <= 1)) | ((level == 2) & (block_level == 2) & is_near)
    live = (others != jnp.concatenate([ids(level + 1), ids(level + 2)], axis=0)) & mine
    served_plan = plan_of(live, slot, jnp.zeros_like(others), 2 * spans)

    sizes, split, order = SIZES, SPLIT, ORDER
    n = len(sizes)
    own_pieces, z_arrays, served_pieces = [None] * n, [None] * n, [None] * n
    ups, owns, kept, returned = [None] * n, [None] * n, [], []
    squares = [jnp.zeros((spans, block_rows), jnp.float32)]
    last = []

    def pack(c):
        packed = pack_call(
            place, queries, keys, values, sizes[c], sum(sizes[:c]), half, split[c], last
        )
        last[:] = [packed[0]]
        if split[c]:
            q_keep, kv_keep, q_send, kv_send = packed
            z_arrays[c] = (q_keep, kv_keep)
            kv_swap = to(kv_send, swap, f"swap_kv_c{c}")
            q_swap = to(q_send, swap, f"swap_q_c{c}")
            own_pieces[c] = (
                [(q_keep, "head"), (q_swap, "head")],
                [(kv_keep, "head"), (kv_swap, "head")],
            )
        else:
            keep, send = packed
            swapped = to(send, swap, f"swap_c{c}")
            z_arrays[c] = (keep, swapped)
            own_pieces[c] = (
                [(keep, "queries"), (swapped, "queries")],
                [(keep, "keys_values"), (swapped, "keys_values")],
            )

    def downs(c, q, kv, name):
        low = to(kv, lift, f"lift_{name}c{c}")
        far = to(q, far_down, f"far_down_{name}c{c}")
        return to(q, near_down, f"near_down_{name}c{c}"), far, low

    def join(c):
        if split[c]:
            (q_keep, q_swap), (kv_keep, kv_swap) = own_pieces[c]
            keeps = downs(c, q_keep[0], kv_keep[0], "keep_")
            swaps = downs(c, q_swap[0], kv_swap[0], "recv_")
            near, far, low = [[(k, "head"), (r, "head")] for k, r in zip(keeps, swaps)]
        else:
            level_q, level_kv = join_call(*z_arrays[c], last)
            last[:] = [level_q]
            near, far, low = [
                [(array, "first"), (array, "second")] for array in downs(c, level_q, level_kv, "")
            ]
        served_pieces[c] = (near + far, own_pieces[c][1] + low)

    def serve(c):
        near, far = attention_call(
            served_plan, *served_pieces[c], False, sizes[c], per_dev, block_rows, last
        )
        last[:] = [near]
        far = to(far, far_up, f"far_up_c{c}")
        ups[c] = (to(near, near_up, f"near_up_c{c}"), far)

    def attend(c):
        owns[c] = attention_call(
            own_plan, own_pieces[c][0], served_pieces[c][1], True, sizes[c], per_dev, block_rows, last
        )
        last[:] = [owns[c][1]]

    def merge(*chunks):
        parts = [(owns[c], *ups[c]) for c in chunks]
        keep, send, squares[0] = merge_call(valid, squares[0], parts, per_dev, last)
        last[:] = [keep]
        kept.append(keep)
        returned.append(to(send, swap, f"back_c{chunks[0]}"))

    steps = {"p": pack, "j": join, "s": serve, "a": attend, "m": merge}
    for what, *args in order:
        if what == "w":
            last.extend([own_plan, served_plan] if args[0] == "plans" else [sent[args[0]]])
        else:
            steps[what](*args)
    squares = squares[0]
    square = squares[:per_dev] + to(squares[per_dev:], swap, "squares_swap")
    n_head = lax.axis_size("head")
    hop = 1
    while hop < n_head:
        square = square + lax.ppermute(square, "head", [(i, i ^ hop) for i in range(n_head)])
        hop *= 2
    return finish_call(place, kept, returned, square, norm_gain, per_dev)


def solution(mesh):
    placed = (P("ctx", "head"), P("ctx", "head"), P("ctx", "head"), P("ctx", None), P("head"))
    body = level_shards if mesh.shape["ctx"] == 8 else shards
    return jax.shard_map(
        body, mesh=mesh, in_specs=placed, out_specs=P("ctx", "head"), check_vma=False
    )
```

```python
from functools import partial
import math

import jax
import jax.numpy as jnp
from jax import lax
from jax.experimental import pallas as pl
from jax.experimental.pallas import tpu as pltpu
from jax.sharding import PartitionSpec as P

HEADS = 32
HD = 128
CAP = 2
LOG2E = math.log2(math.e)
EXP_SCALE = HD ** (-0.5) * LOG2E


def partial_state(query_rows, key_block, value_block, causal):
    scores = jnp.einsum(
        "sqhd,skhd->shqk", query_rows, key_block, preferred_element_type=jnp.float32
    ) * query_rows.shape[3] ** (-0.5)
    if causal:
        query_pos = lax.broadcasted_iota(jnp.int32, scores.shape, 2)
        key_pos = lax.broadcasted_iota(jnp.int32, scores.shape, 3)
        scores = jnp.where(key_pos <= query_pos, scores, -1e30)
    row_peak = jnp.max(scores, axis=3)
    exponentials = jnp.exp(scores - row_peak[..., None])
    row_sum = jnp.sum(exponentials, axis=3)
    weights = exponentials.astype(jnp.bfloat16)
    blended = jnp.einsum(
        "shqk,skhd->sqhd", weights, value_block, preferred_element_type=jnp.float32
    )
    blended = blended / jnp.transpose(row_sum, (0, 2, 1))[..., None]
    return (blended, row_peak + jnp.log(row_sum))


def slot_plan(selected, first_span, per_dev, capacity):
    own_span = first_span + lax.broadcasted_iota(jnp.int32, selected.shape, 0)
    is_live = (selected != own_span).reshape(-1)
    owner_dev = (selected // per_dev).reshape(-1)
    pair_count = owner_dev.shape[0]
    is_later = lax.broadcasted_iota(jnp.int32, (pair_count, pair_count), 0) > lax.broadcasted_iota(
        jnp.int32, (pair_count, pair_count), 1
    )
    earlier = is_later & (owner_dev[:, None] == owner_dev[None, :]) & is_live[None, :]
    slot_rank = jnp.sum(earlier.astype(jnp.int32), axis=1)
    slot_index = jnp.where(is_live, owner_dev * capacity + slot_rank, 0)
    return (slot_index, is_live, (selected % per_dev).reshape(-1))


def shards(queries, keys, values, selection, norm_gain):
    n_ctx = lax.axis_size("ctx")
    device = lax.axis_index("ctx")
    rows, width = queries.shape
    per_dev, topk_count = selection.shape
    block_rows = rows // per_dev
    heads_dev = width // HD
    slot_count = n_ctx * CAP
    group_size = math.gcd(slot_count, 4)
    query_blocks = queries.reshape(per_dev, block_rows, heads_dev, HD)
    key_blocks = keys.reshape(per_dev, block_rows, heads_dev, HD)
    value_blocks = values.reshape(per_dev, block_rows, heads_dev, HD)
    slot_index, is_live, local_block = slot_plan(selection[:, 1:], device * per_dev, per_dev, CAP)
    pair_count = slot_index.shape[0]
    pair_span = lax.broadcasted_iota(jnp.int32, (pair_count,), 0) // (topk_count - 1)
    slot_ids = lax.broadcasted_iota(jnp.int32, (slot_count, pair_count), 0)
    placed = (slot_ids == slot_index[None, :]) & is_live[None, :]
    slot_span = jnp.sum(jnp.where(placed, pair_span[None, :], 0), axis=1)
    everyone = lax.all_gather(selection, "ctx", axis=0, tiled=True)
    requests = everyone[:, 1:].reshape(n_ctx, per_dev, topk_count - 1)
    first_spans = lax.broadcasted_iota(jnp.int32, (n_ctx,), 0) * per_dev
    all_slots, all_live, all_local = jax.vmap(partial(slot_plan, per_dev=per_dev, capacity=CAP))(
        requests, first_spans
    )
    owner_devs = requests.reshape(n_ctx, -1) // per_dev
    served = all_live & (owner_devs == device)
    capacity_ids = lax.broadcasted_iota(jnp.int32, (1, CAP, 1), 1)
    matched = served[:, None, :] & (all_slots[:, None, :] == device * CAP + capacity_ids)
    send_block = jnp.sum(jnp.where(matched, all_local[:, None, :], 0), axis=2)
    key_out = key_blocks[send_block].reshape(n_ctx, CAP, block_rows, width)
    value_out = value_blocks[send_block].reshape(n_ctx, CAP, block_rows, width)
    key_in, value_in = (
        lax.all_to_all(key_out, "ctx", split_axis=0, concat_axis=0, tiled=True),
        lax.all_to_all(value_out, "ctx", split_axis=0, concat_axis=0, tiled=True),
    )

    def one_group(packed):
        group_keys, group_values, group_span = packed
        blended, log_sums = partial_state(query_blocks[group_span], group_keys, group_values, False)
        return (blended.astype(jnp.bfloat16), log_sums)

    slot_out, slot_lse = lax.map(
        one_group,
        (
            key_in.reshape(-1, group_size, block_rows, heads_dev, HD),
            value_in.reshape(-1, group_size, block_rows, heads_dev, HD),
            slot_span.reshape(-1, group_size),
        ),
    )
    slot_out = slot_out.reshape(slot_count, block_rows, heads_dev, HD)
    slot_lse = slot_lse.reshape(slot_count, heads_dev, block_rows)
    own_out, own_lse = partial_state(query_blocks, key_blocks, value_blocks, True)
    live_pairs = is_live.reshape(per_dev, topk_count - 1)
    pair_out = (
        slot_out[slot_index]
        .reshape(per_dev, topk_count - 1, block_rows, heads_dev, HD)
        .astype(jnp.float32)
    )
    pair_lse = jnp.where(
        live_pairs[:, :, None, None],
        slot_lse[slot_index].reshape(per_dev, topk_count - 1, heads_dev, block_rows),
        -1e30,
    )
    highest = jnp.maximum(own_lse, jnp.max(pair_lse, axis=1))
    own_weight = jnp.exp(own_lse - highest)
    pair_weight = jnp.where(live_pairs[:, :, None, None], jnp.exp(pair_lse - highest[:, None]), 0.0)
    numerator = jnp.transpose(own_weight, (0, 2, 1))[..., None] * own_out
    numerator = numerator + jnp.sum(
        jnp.transpose(pair_weight, (0, 1, 3, 2))[..., None] * pair_out, axis=1
    )
    denominator = own_weight + jnp.sum(pair_weight, axis=1)
    attended = (numerator / jnp.transpose(denominator, (0, 2, 1))[..., None]).reshape(rows, width)
    squares = jnp.sum(attended * attended, axis=1)
    summed = lax.psum(squares, "head")
    factor = lax.rsqrt(summed / (HEADS * HD) + 1e-06)
    return (attended * factor[:, None] * norm_gain.astype(jnp.float32)[None, :]).astype(
        jnp.bfloat16
    )


SIZES = (1, 1, 1, 1,)
SPLIT = (False, False, False, False,)
ORDER = (
    ("p", 0),
    ("p", 2),
    ("w", "plans"),
    ("p", 1),
    ("j", 0),
    ("j", 1),
    ("p", 3),
    ("s", 0),
    ("a", 0),
    ("j", 2),
    ("s", 1),
    ("a", 1),
    ("w", "lift_c1"),
    ("w", "near_up_c0"),
    ("w", "far_up_c0"),
    ("j", 3),
    ("s", 2),
    ("s", 3),
    ("a", 2),
    ("m", 0, 1),
    ("m", 2),
    ("a", 3),
    ("m", 3),
)
LSE_ROWS = 32
UNROLL = 2
VMEM_LIMIT = 16 * 1024 * 1024


def unit_fields(code):
    return code & 31, (code >> 5) & 31, (code >> 10) & 63, (code >> 16) & 1, (code >> 17) & 1


def unit_code(slot, span, out, first, diagonal):
    return slot + span * 32 + out * 1024 + first * 65536 + diagonal * 131072


PIECES = {
    "head": lambda ref, h: ref.at[h],
    "queries": lambda ref, h: ref.at[h, 0],
    "keys_values": lambda ref, h: ref.at[h, pl.ds(1, 2)],
    "first": lambda ref, h: ref.at[0, h],
    "second": lambda ref, h: ref.at[1, h],
}


def attention_kernel(shape, own, q_pieces, kv_pieces, n_in, plan, *refs):
    heads, per_dev, block_rows = shape
    n_q, n_kv = len(q_pieces), len(kv_pieces)
    inputs, refs = refs[:n_in], refs[n_in:]
    outs, refs = refs[:2], refs[2:]
    (q_scr, kv_scr, s0, s1, p0, p1, d0, d1, acc_scr, top_scr, sum_scr, o_scr, lse_scr, sems) = refs[:14]
    s_scr, p_scr, decay_scr = (s0, s1), (p0, p1), (d0, d1)
    spans = n_q * per_dev
    copies = []
    for h in range(heads):
        for i, (n, kind) in enumerate(q_pieces):
            copies.append((PIECES[kind](inputs[n], h), q_scr.at[h, i], sems.at[h, i]))
        for i, (n, kind) in enumerate(kv_pieces):
            copies.append((PIECES[kind](inputs[n], h), kv_scr.at[h, i], sems.at[h, n_q + i]))
    copies = [pltpu.make_async_copy(*copy) for copy in copies]
    for copy in copies:
        copy.start()
    s1[...] = jnp.zeros_like(s1)
    p0[...] = jnp.zeros_like(p0)
    d0[...] = jnp.zeros_like(d0)
    acc_scr[...] = jnp.zeros_like(acc_scr)
    top_scr[...] = jnp.zeros_like(top_scr)
    sum_scr[...] = jnp.ones_like(sum_scr)
    if own:
        bias_scr = refs[14]
        key_pos = lax.broadcasted_iota(jnp.int32, (block_rows, block_rows), 0)
        query_pos = lax.broadcasted_iota(jnp.int32, (block_rows, block_rows), 1)
        bias_scr[0] = jnp.zeros((block_rows, block_rows), jnp.float32)
        bias_scr[1] = jnp.where(key_pos <= query_pos, 0.0, -1e30)
    for copy in copies:
        copy.wait()

    def rows_of(i):
        return pl.ds(pl.multiple_of((i % per_dev) * block_rows, block_rows), block_rows)

    def step(h, at, now, acc, top, total):
        before = 1 - now
        for u in range(UNROLL):
            slot, _, out, _, _ = unit_fields(plan[at + u])
            vt = kv_scr[h, slot // per_dev, 1, rows_of(slot), :]
            vt = jnp.concatenate([vt[:HD], vt[HD:]], axis=1)
            mixed = jnp.dot(vt, p_scr[now][u], preferred_element_type=jnp.float32)
            acc = acc * decay_scr[now][u, 0:1, :] + mixed
            o_scr[out] = (acc * decay_scr[now][u, 1:2, :]).astype(o_scr.dtype)
        for u in range(UNROLL):
            _, _, out, first, diagonal = unit_fields(plan[at + UNROLL + u])
            s = s_scr[before][u]
            if own:
                s = s + bias_scr[diagonal]
            old = jnp.where(first == 1, -1e30, top)
            top = jnp.maximum(old, jnp.max(s, axis=0, keepdims=True))
            decay = jnp.exp2((old - top) * EXP_SCALE)
            p = jnp.exp2((s - top) * EXP_SCALE)
            total = total * decay + jnp.sum(p, axis=0, keepdims=True)
            p_scr[before][u] = p.astype(jnp.bfloat16)
            decay_scr[before][u, 0:1, :] = decay
            decay_scr[before][u, 1:2, :] = 1.0 / total
            lse_scr[pl.ds(out, 1), :] = top * EXP_SCALE + jnp.log(total) * LOG2E
        for u in range(UNROLL):
            slot, span, _, _, _ = unit_fields(plan[at + 2 * UNROLL + u])
            k = kv_scr[h, slot // per_dev, 0, rows_of(slot), :]
            q = q_scr[h, span // per_dev, rows_of(span), :]
            s_scr[now][u] = lax.dot_general(
                k, q, (((1,), (1,)), ((), ())), preferred_element_type=jnp.float32
            )
        return acc, top, total

    for h in range(heads):
        o_scr[...] = jnp.zeros_like(o_scr)
        lse_scr[...] = jnp.full_like(lse_scr, -1e30)

        def two_steps(i, carry):
            state = (acc_scr[...], top_scr[...], sum_scr[...])
            state = step(h, 1 + 2 * i * UNROLL, 0, *state)
            state = step(h, 1 + (2 * i + 1) * UNROLL, 1, *state)
            acc_scr[...], top_scr[...], sum_scr[...] = state
            return carry

        lax.fori_loop(0, (plan[0] + 1) // 2, two_steps, 0)
        if own:
            outs[0][h] = o_scr[:spans]
            outs[1][h] = lse_scr[:spans, :]
        else:
            half = spans // 2
            for side in range(2):
                for span in range(half):
                    outs[side][h, span * HD : (span + 1) * HD, :] = o_scr[side * half + span]
                lse = lse_scr[side * half : (side + 1) * half, :]
                high = lse.astype(jnp.bfloat16).astype(jnp.float32)
                middle = (lse - high).astype(jnp.bfloat16).astype(jnp.float32)
                rest = jnp.zeros((LSE_ROWS - 3 * half, block_rows), jnp.float32)
                parts = jnp.concatenate([high, middle, lse - high - middle, rest], axis=0)
                outs[side][h, half * HD :, :] = parts.astype(jnp.bfloat16)


def ordered(kernel, n_after):
    def body(*refs):
        kernel(*refs[n_after:])

    return body


def attention_call(plan, q_pieces, kv_pieces, own, heads, per_dev, block_rows, after=()):
    inputs = []

    def numbered(pieces):
        out = []
        for array, kind in pieces:
            if not any(array is known for known in inputs):
                inputs.append(array)
            out.append(([array is known for known in inputs].index(True), kind))
        return out

    q_pieces, kv_pieces = numbered(q_pieces), numbered(kv_pieces)
    n_q, n_kv = len(q_pieces), len(kv_pieces)
    spans = n_q * per_dev
    vmem, hbm = pl.BlockSpec(memory_space=pltpu.VMEM), pl.BlockSpec(memory_space=pltpu.HBM)
    f32, bf16 = jnp.float32, jnp.bfloat16
    if own:
        out_shape = (
            jax.ShapeDtypeStruct((heads, spans, HD, block_rows), f32),
            jax.ShapeDtypeStruct((heads, spans, block_rows), f32),
        )
    else:
        packed = jax.ShapeDtypeStruct((heads, spans // 2 * HD + LSE_ROWS, block_rows), bf16)
        out_shape = (packed, packed)
    scratch = [
        pltpu.VMEM((heads, n_q, per_dev * block_rows, HD), bf16),
        pltpu.VMEM((heads, n_kv, 2, per_dev * block_rows, HD), bf16),
        pltpu.VMEM((UNROLL, block_rows, block_rows), f32),
        pltpu.VMEM((UNROLL, block_rows, block_rows), f32),
        pltpu.VMEM((UNROLL, block_rows, block_rows), bf16),
        pltpu.VMEM((UNROLL, block_rows, block_rows), bf16),
        pltpu.VMEM((UNROLL, 8, block_rows), f32),
        pltpu.VMEM((UNROLL, 8, block_rows), f32),
        pltpu.VMEM((HD, block_rows), f32),
        pltpu.VMEM((1, block_rows), f32),
        pltpu.VMEM((1, block_rows), f32),
        pltpu.VMEM((spans + 1, HD, block_rows), f32 if own else bf16),
        pltpu.VMEM((spans + 8, block_rows), f32),
        pltpu.SemaphoreType.DMA((heads, n_q + n_kv)),
    ]
    if own:
        scratch.append(pltpu.VMEM((2, block_rows, block_rows), f32))
    return pl.pallas_call(
        ordered(
            partial(
                attention_kernel, (heads, per_dev, block_rows), own, q_pieces, kv_pieces, len(inputs)
            ),
            len(after),
        ),
        out_shape=out_shape,
        in_specs=[hbm] * len(after) + [pl.BlockSpec(memory_space=pltpu.SMEM)] + [hbm] * len(inputs),
        out_specs=(vmem, vmem),
        scratch_shapes=scratch,
        compiler_params=pltpu.CompilerParams(vmem_limit_bytes=VMEM_LIMIT),
        cost_estimate=pl.CostEstimate(flops=1, bytes_accessed=1, transcendentals=0),
        name="own_attention" if own else "served_attention",
    )(*after, plan, *inputs)


def pack_kernel(shape, place, q_ref, k_ref, v_ref, *refs):
    heads, first, half, rows, split = shape
    outs, (scr, t_scr, sems) = refs[:-3], refs[-3:]
    loads, stores = {}, []
    for side in (1, 0):
        for h in range(heads):
            start = pl.multiple_of((place[side] * half + first + h) * HD, HD)
            for i, ref in enumerate((q_ref, k_ref, v_ref)):
                load = pltpu.make_async_copy(
                    ref.at[:, pl.ds(start, HD)], scr.at[side, h, i], sems.at[0, side, h, i]
                )
                load.start()
                loads[side, h, i] = load

    def store(side, h, i, source):
        if split:
            out = outs[2 * side + (i > 0)]
            target = out.at[h, i - 1] if i else out.at[h]
        else:
            target = outs[side].at[h, i]
        copy = pltpu.make_async_copy(source, target, sems.at[1, side, h, i])
        copy.start()
        stores.append(copy)

    for side in (1, 0):
        for h in range(heads):
            for i in range(2):
                loads[side, h, i].wait()
                store(side, h, i, scr.at[side, h, i])
            loads[side, h, 2].wait()
            for tile in range(rows // HD):
                at = slice(tile * HD, (tile + 1) * HD)
                t_scr[side, h, at, :] = scr[side, h, 2, at, :].T
            store(side, h, 2, t_scr.at[side, h])
    for copy in stores:
        copy.wait()


def pack_call(place, queries, keys, values, heads, first, half, split, after=()):
    rows = queries.shape[0]
    hbm = pl.BlockSpec(memory_space=pltpu.HBM)
    bf16 = jnp.bfloat16
    queries, keys, values = (
        pltpu.with_memory_space_constraint(array, pltpu.HBM) for array in (queries, keys, values)
    )
    if split:
        side = [
            jax.ShapeDtypeStruct((heads, rows, HD), bf16),
            jax.ShapeDtypeStruct((heads, 2, rows, HD), bf16),
        ]
    else:
        side = [jax.ShapeDtypeStruct((heads, 3, rows, HD), bf16)]
    return pl.pallas_call(
        ordered(partial(pack_kernel, (heads, first, half, rows, split)), len(after)),
        out_shape=side * 2,
        in_specs=[hbm] * len(after) + [pl.BlockSpec(memory_space=pltpu.SMEM)] + [hbm] * 3,
        out_specs=[hbm] * (2 * len(side)),
        scratch_shapes=[
            pltpu.VMEM((2, heads, 3, rows, HD), bf16),
            pltpu.VMEM((2, heads, rows, HD), bf16),
            pltpu.SemaphoreType.DMA((2, 2, heads, 3)),
        ],
        compiler_params=pltpu.CompilerParams(vmem_limit_bytes=VMEM_LIMIT),
        cost_estimate=pl.CostEstimate(flops=1, bytes_accessed=1, transcendentals=0),
        name="pack",
    )(*after, place, queries, keys, values)


def join_kernel(heads, keep_ref, swap_ref, q_ref, kv_ref, scr, sems):
    loads, stores = [], []
    for side, ref in enumerate((keep_ref, swap_ref)):
        for h in range(heads):
            loads.append(pltpu.make_async_copy(ref.at[h], scr.at[side, h], sems.at[0, side, h]))
            stores.append(
                (
                    pltpu.make_async_copy(scr.at[side, h, 0], q_ref.at[side, h], sems.at[1, side, h]),
                    pltpu.make_async_copy(
                        scr.at[side, h, pl.ds(1, 2)], kv_ref.at[side, h], sems.at[2, side, h]
                    ),
                )
            )
    for load in loads:
        load.start()
    for load, pair in zip(loads, stores):
        load.wait()
        for store in pair:
            store.start()
    for pair in stores:
        for store in pair:
            store.wait()


def join_call(keep, swapped, after=()):
    heads, _, rows, _ = keep.shape
    hbm = pl.BlockSpec(memory_space=pltpu.HBM)
    return pl.pallas_call(
        ordered(partial(join_kernel, heads), len(after)),
        out_shape=(
            jax.ShapeDtypeStruct((2, heads, rows, HD), jnp.bfloat16),
            jax.ShapeDtypeStruct((2, heads, 2, rows, HD), jnp.bfloat16),
        ),
        in_specs=[hbm] * (len(after) + 2),
        out_specs=(hbm, hbm),
        scratch_shapes=[
            pltpu.VMEM((2, heads, 3, rows, HD), jnp.bfloat16),
            pltpu.SemaphoreType.DMA((3, 2, heads)),
        ],
        compiler_params=pltpu.CompilerParams(vmem_limit_bytes=VMEM_LIMIT),
        cost_estimate=pl.CostEstimate(flops=1, bytes_accessed=1, transcendentals=0),
        name="join",
    )(*after, keep, swapped)


def merge_kernel(per_dev, block_rows, sizes, valid, sofar_ref, *refs):
    inputs, (keep_ref, send_ref, squares_ref) = refs[:-3], refs[-3:]
    spans = 2 * per_dev
    squares_ref[...] = sofar_ref[...]
    at = 0
    for c, size in enumerate(sizes):
        own_ref, own_lse_ref, near_ref, far_ref = inputs[4 * c : 4 * c + 4]
        for h in range(size):
            lses = [own_lse_ref[h]]
            for i, ref in enumerate((near_ref, far_ref)):
                parts = ref[h, spans * HD :, :].astype(jnp.float32)
                lse = parts[:spans] + parts[spans : 2 * spans] + parts[2 * spans : 3 * spans]
                lses.append(jnp.where(valid[i] > 0, lse, -1e30))
            top = jnp.maximum(jnp.maximum(lses[0], lses[1]), lses[2])
            weights = [jnp.exp2(lse - top) for lse in lses]
            scale = 1.0 / (weights[0] + weights[1] + weights[2])
            weights = [weight * scale for weight in weights]
            for span in range(spans):
                rows = slice(span, span + 1)
                tile = slice(span * HD, (span + 1) * HD)
                mixed = weights[0][rows, :] * own_ref[h, span]
                mixed = mixed + weights[1][rows, :] * near_ref[h, tile, :].astype(jnp.float32)
                mixed = mixed + weights[2][rows, :] * far_ref[h, tile, :].astype(jnp.float32)
                squares_ref[rows, :] = squares_ref[rows, :] + jnp.sum(mixed * mixed, axis=0, keepdims=True)
                target = keep_ref if span < per_dev else send_ref
                start = (span % per_dev) * block_rows
                target[at, start : start + block_rows, :] = mixed.T.astype(target.dtype)
            at += 1


def merge_call(valid, sofar, parts, per_dev, after=()):
    block_rows = sofar.shape[1]
    sizes = [own[0].shape[0] for own, _, _ in parts]
    arrays = [array for own, near, far in parts for array in (*own, near, far)]
    vmem = pl.BlockSpec(memory_space=pltpu.VMEM)
    hbm = pl.BlockSpec(memory_space=pltpu.HBM)
    packed = jax.ShapeDtypeStruct((sum(sizes), per_dev * block_rows, HD), jnp.bfloat16)
    return pl.pallas_call(
        ordered(partial(merge_kernel, per_dev, block_rows, sizes), len(after)),
        out_shape=(packed, packed, jax.ShapeDtypeStruct(sofar.shape, jnp.float32)),
        in_specs=[hbm] * len(after)
        + [pl.BlockSpec(memory_space=pltpu.SMEM)]
        + [vmem] * (1 + len(arrays)),
        out_specs=(vmem, vmem, vmem),
        compiler_params=pltpu.CompilerParams(vmem_limit_bytes=VMEM_LIMIT),
        cost_estimate=pl.CostEstimate(flops=1, bytes_accessed=1, transcendentals=0),
        name="merge",
    )(*after, valid, sofar, *arrays)


def finish_kernel(per_dev, sizes, place, *refs):
    n = len(sizes)
    kept, returned = refs[:n], refs[n : 2 * n]
    squares_ref, gain_ref, out_ref = refs[2 * n :]
    block_rows = squares_ref.shape[1]
    half = sum(sizes)
    factor = lax.rsqrt(squares_ref[...] / (HEADS * HD) + 1e-06)
    for b in range(per_dev):
        column = jnp.broadcast_to(factor[b : b + 1, :], (HD, block_rows)).T
        rows = slice(b * block_rows, (b + 1) * block_rows)
        for side, pieces in enumerate((kept, returned)):
            head = 0
            for piece, size in zip(pieces, sizes):
                for h in range(size):
                    start = pl.multiple_of((place[side] * half + head) * HD, HD)
                    gain = gain_ref[:, pl.ds(start, HD)].astype(jnp.float32)
                    value = piece[h, rows, :].astype(jnp.float32) * column * gain
                    out_ref[rows, pl.ds(start, HD)] = value.astype(out_ref.dtype)
                    head += 1


def finish_call(place, kept, returned, squares, gain, per_dev):
    vmem = pl.BlockSpec(memory_space=pltpu.VMEM)
    rows, width = kept[0].shape[1], gain.shape[0]
    return pl.pallas_call(
        partial(finish_kernel, per_dev, [k.shape[0] for k in kept]),
        out_shape=jax.ShapeDtypeStruct((rows, width), jnp.bfloat16),
        in_specs=[pl.BlockSpec(memory_space=pltpu.SMEM)] + [vmem] * (2 * len(kept) + 2),
        out_specs=vmem,
        compiler_params=pltpu.CompilerParams(vmem_limit_bytes=VMEM_LIMIT),
        cost_estimate=pl.CostEstimate(flops=1, bytes_accessed=1, transcendentals=0),
        name="finish",
    )(place, *kept, *returned, squares, gain.reshape(1, width))


def plan_of(live, slot, diagonal, dump):
    spans, entries = live.shape
    t = jnp.arange(entries)
    earlier = jnp.sum((t[None, None, :] < t[None, :, None]) & live[:, None, :], axis=2)
    span = lax.broadcasted_iota(jnp.int32, live.shape, 0)
    code = unit_code(slot, span, span, (earlier == 0).astype(jnp.int32), diagonal)
    code, live = code.reshape(-1), live.reshape(-1)
    n = spans * entries
    i = jnp.arange(n)
    rank = jnp.sum((i[None, :] < i[:, None]) & live[None, :], axis=1)
    at = jnp.arange(n + 8 * UNROLL)
    hit = live[None, :] & (rank[None, :] + 2 * UNROLL == at[:, None])
    idle = unit_code(0, 0, dump, 1, 0)
    codes = jnp.sum(jnp.where(hit, code[None, :] - idle, 0), axis=1) + idle
    total = jnp.sum(live.astype(jnp.int32))
    steps = jnp.where(total > 0, (total + UNROLL - 1) // UNROLL + 2, 0)
    return jnp.concatenate([steps[None], codes]).astype(jnp.int32)


def level_shards(queries, keys, values, selection, norm_gain):
    device = lax.axis_index("ctx")
    level, x = device // 2, device % 2
    rows, width = queries.shape
    per_dev, topk = selection.shape
    block_rows = rows // per_dev
    spans = 2 * per_dev
    half = width // HD // 2

    sent = {}

    def to(array, pairs, name):
        with jax.named_scope(name):
            sent[name] = lax.ppermute(array, "ctx", pairs)
        return sent[name]

    swap = [(d, d ^ 1) for d in range(8)]
    lift = [(0, 2), (1, 3)]
    near_down, far_down = [(4, 2), (5, 3), (6, 4), (7, 5)], [(6, 2), (7, 3)]
    near_up, far_up = [(2, 4), (3, 5), (4, 6), (5, 7)], [(2, 6), (3, 7)]
    valid = jnp.stack([level >= 2, level >= 3]).astype(jnp.int32)
    place = jnp.stack([x, 1 - x]).astype(jnp.int32)

    own_selection = jnp.concatenate([selection, to(selection, swap, "selection_swap")], axis=0)
    near_selection, far_selection = (
        to(own_selection, near_down, "selection_near"),
        to(own_selection, far_down, "selection_far"),
    )

    def ids(at):
        first = jnp.stack([(at * 2 + x) * per_dev, (at * 2 + 1 - x) * per_dev])
        return (first[:, None] + jnp.arange(per_dev)[None, :]).reshape(-1, 1)

    def slots(blocks):
        owner = blocks // per_dev
        slot = jnp.where(owner // 2 == level, 0, spans) + jnp.where(owner % 2 == x, 0, per_dev)
        return owner // 2, slot + blocks % per_dev

    others = own_selection[:, 1:]
    block_level, slot = slots(others)
    live = (others != ids(level)) & ((block_level == level) | ((level == 1) & (block_level == 0)))
    first = jnp.ones((spans, 1), jnp.int32)
    own_plan = plan_of(
        jnp.concatenate([first > 0, live], axis=1),
        jnp.concatenate([jnp.arange(spans, dtype=jnp.int32)[:, None], slot], axis=1),
        jnp.concatenate([first, jnp.zeros_like(others)], axis=1),
        spans,
    )
    others = jnp.concatenate([near_selection, far_selection], axis=0)[:, 1:]
    block_level, slot = slots(others)
    is_near = lax.broadcasted_iota(jnp.int32, others.shape, 0) < spans
    mine = ((level == 1) & (block_level <= 1)) | ((level == 2) & (block_level == 2) & is_near)
    live = (others != jnp.concatenate([ids(level + 1), ids(level + 2)], axis=0)) & mine
    served_plan = plan_of(live, slot, jnp.zeros_like(others), 2 * spans)

    sizes, split, order = SIZES, SPLIT, ORDER
    n = len(sizes)
    own_pieces, z_arrays, served_pieces = [None] * n, [None] * n, [None] * n
    ups, owns, kept, returned = [None] * n, [None] * n, [], []
    squares = [jnp.zeros((spans, block_rows), jnp.float32)]
    last = []

    def pack(c):
        packed = pack_call(
            place, queries, keys, values, sizes[c], sum(sizes[:c]), half, split[c], last
        )
        last[:] = [packed[0]]
        if split[c]:
            q_keep, kv_keep, q_send, kv_send = packed
            z_arrays[c] = (q_keep, kv_keep)
            kv_swap = to(kv_send, swap, f"swap_kv_c{c}")
            q_swap = to(q_send, swap, f"swap_q_c{c}")
            own_pieces[c] = (
                [(q_keep, "head"), (q_swap, "head")],
                [(kv_keep, "head"), (kv_swap, "head")],
            )
        else:
            keep, send = packed
            swapped = to(send, swap, f"swap_c{c}")
            z_arrays[c] = (keep, swapped)
            own_pieces[c] = (
                [(keep, "queries"), (swapped, "queries")],
                [(keep, "keys_values"), (swapped, "keys_values")],
            )

    def downs(c, q, kv, name):
        low = to(kv, lift, f"lift_{name}c{c}")
        far = to(q, far_down, f"far_down_{name}c{c}")
        return to(q, near_down, f"near_down_{name}c{c}"), far, low

    def join(c):
        if split[c]:
            (q_keep, q_swap), (kv_keep, kv_swap) = own_pieces[c]
            keeps = downs(c, q_keep[0], kv_keep[0], "keep_")
            swaps = downs(c, q_swap[0], kv_swap[0], "recv_")
            near, far, low = [[(k, "head"), (r, "head")] for k, r in zip(keeps, swaps)]
        else:
            level_q, level_kv = join_call(*z_arrays[c], last)
            last[:] = [level_q]
            near, far, low = [
                [(array, "first"), (array, "second")] for array in downs(c, level_q, level_kv, "")
            ]
        served_pieces[c] = (near + far, own_pieces[c][1] + low)

    def serve(c):
        near, far = attention_call(
            served_plan, *served_pieces[c], False, sizes[c], per_dev, block_rows, last
        )
        last[:] = [near]
        far = to(far, far_up, f"far_up_c{c}")
        ups[c] = (to(near, near_up, f"near_up_c{c}"), far)

    def attend(c):
        owns[c] = attention_call(
            own_plan, own_pieces[c][0], served_pieces[c][1], True, sizes[c], per_dev, block_rows, last
        )
        last[:] = [owns[c][1]]

    def merge(*chunks):
        parts = [(owns[c], *ups[c]) for c in chunks]
        keep, send, squares[0] = merge_call(valid, squares[0], parts, per_dev, last)
        last[:] = [keep]
        kept.append(keep)
        returned.append(to(send, swap, f"back_c{chunks[0]}"))

    steps = {"p": pack, "j": join, "s": serve, "a": attend, "m": merge}
    for what, *args in order:
        if what == "w":
            last.extend([own_plan, served_plan] if args[0] == "plans" else [sent[args[0]]])
        else:
            steps[what](*args)
    squares = squares[0]
    square = squares[:per_dev] + to(squares[per_dev:], swap, "squares_swap")
    n_head = lax.axis_size("head")
    hop = 1
    while hop < n_head:
        square = square + lax.ppermute(square, "head", [(i, i ^ hop) for i in range(n_head)])
        hop *= 2
    return finish_call(place, kept, returned, square, norm_gain, per_dev)


def solution(mesh):
    placed = (P("ctx", "head"), P("ctx", "head"), P("ctx", "head"), P("ctx", None), P("head"))
    body = level_shards if mesh.shape["ctx"] == 8 else shards
    return jax.shard_map(
        body, mesh=mesh, in_specs=placed, out_specs=P("ctx", "head"), check_vma=False
    )
```

```python
from functools import partial
import math

import jax
import jax.numpy as jnp
from jax import lax
from jax.experimental import pallas as pl
from jax.experimental.pallas import tpu as pltpu
from jax.sharding import PartitionSpec as P

HEADS = 32
HD = 128
CAP = 2
LOG2E = math.log2(math.e)
EXP_SCALE = HD ** (-0.5) * LOG2E


def partial_state(query_rows, key_block, value_block, causal):
    scores = jnp.einsum(
        "sqhd,skhd->shqk", query_rows, key_block, preferred_element_type=jnp.float32
    ) * query_rows.shape[3] ** (-0.5)
    if causal:
        query_pos = lax.broadcasted_iota(jnp.int32, scores.shape, 2)
        key_pos = lax.broadcasted_iota(jnp.int32, scores.shape, 3)
        scores = jnp.where(key_pos <= query_pos, scores, -1e30)
    row_peak = jnp.max(scores, axis=3)
    exponentials = jnp.exp(scores - row_peak[..., None])
    row_sum = jnp.sum(exponentials, axis=3)
    weights = exponentials.astype(jnp.bfloat16)
    blended = jnp.einsum(
        "shqk,skhd->sqhd", weights, value_block, preferred_element_type=jnp.float32
    )
    blended = blended / jnp.transpose(row_sum, (0, 2, 1))[..., None]
    return (blended, row_peak + jnp.log(row_sum))


def slot_plan(selected, first_span, per_dev, capacity):
    own_span = first_span + lax.broadcasted_iota(jnp.int32, selected.shape, 0)
    is_live = (selected != own_span).reshape(-1)
    owner_dev = (selected // per_dev).reshape(-1)
    pair_count = owner_dev.shape[0]
    is_later = lax.broadcasted_iota(jnp.int32, (pair_count, pair_count), 0) > lax.broadcasted_iota(
        jnp.int32, (pair_count, pair_count), 1
    )
    earlier = is_later & (owner_dev[:, None] == owner_dev[None, :]) & is_live[None, :]
    slot_rank = jnp.sum(earlier.astype(jnp.int32), axis=1)
    slot_index = jnp.where(is_live, owner_dev * capacity + slot_rank, 0)
    return (slot_index, is_live, (selected % per_dev).reshape(-1))


def shards(queries, keys, values, selection, norm_gain):
    n_ctx = lax.axis_size("ctx")
    device = lax.axis_index("ctx")
    rows, width = queries.shape
    per_dev, topk_count = selection.shape
    block_rows = rows // per_dev
    heads_dev = width // HD
    slot_count = n_ctx * CAP
    group_size = math.gcd(slot_count, 4)
    query_blocks = queries.reshape(per_dev, block_rows, heads_dev, HD)
    key_blocks = keys.reshape(per_dev, block_rows, heads_dev, HD)
    value_blocks = values.reshape(per_dev, block_rows, heads_dev, HD)
    slot_index, is_live, local_block = slot_plan(selection[:, 1:], device * per_dev, per_dev, CAP)
    pair_count = slot_index.shape[0]
    pair_span = lax.broadcasted_iota(jnp.int32, (pair_count,), 0) // (topk_count - 1)
    slot_ids = lax.broadcasted_iota(jnp.int32, (slot_count, pair_count), 0)
    placed = (slot_ids == slot_index[None, :]) & is_live[None, :]
    slot_span = jnp.sum(jnp.where(placed, pair_span[None, :], 0), axis=1)
    everyone = lax.all_gather(selection, "ctx", axis=0, tiled=True)
    requests = everyone[:, 1:].reshape(n_ctx, per_dev, topk_count - 1)
    first_spans = lax.broadcasted_iota(jnp.int32, (n_ctx,), 0) * per_dev
    all_slots, all_live, all_local = jax.vmap(partial(slot_plan, per_dev=per_dev, capacity=CAP))(
        requests, first_spans
    )
    owner_devs = requests.reshape(n_ctx, -1) // per_dev
    served = all_live & (owner_devs == device)
    capacity_ids = lax.broadcasted_iota(jnp.int32, (1, CAP, 1), 1)
    matched = served[:, None, :] & (all_slots[:, None, :] == device * CAP + capacity_ids)
    send_block = jnp.sum(jnp.where(matched, all_local[:, None, :], 0), axis=2)
    key_out = key_blocks[send_block].reshape(n_ctx, CAP, block_rows, width)
    value_out = value_blocks[send_block].reshape(n_ctx, CAP, block_rows, width)
    key_in, value_in = (
        lax.all_to_all(key_out, "ctx", split_axis=0, concat_axis=0, tiled=True),
        lax.all_to_all(value_out, "ctx", split_axis=0, concat_axis=0, tiled=True),
    )

    def one_group(packed):
        group_keys, group_values, group_span = packed
        blended, log_sums = partial_state(query_blocks[group_span], group_keys, group_values, False)
        return (blended.astype(jnp.bfloat16), log_sums)

    slot_out, slot_lse = lax.map(
        one_group,
        (
            key_in.reshape(-1, group_size, block_rows, heads_dev, HD),
            value_in.reshape(-1, group_size, block_rows, heads_dev, HD),
            slot_span.reshape(-1, group_size),
        ),
    )
    slot_out = slot_out.reshape(slot_count, block_rows, heads_dev, HD)
    slot_lse = slot_lse.reshape(slot_count, heads_dev, block_rows)
    own_out, own_lse = partial_state(query_blocks, key_blocks, value_blocks, True)
    live_pairs = is_live.reshape(per_dev, topk_count - 1)
    pair_out = (
        slot_out[slot_index]
        .reshape(per_dev, topk_count - 1, block_rows, heads_dev, HD)
        .astype(jnp.float32)
    )
    pair_lse = jnp.where(
        live_pairs[:, :, None, None],
        slot_lse[slot_index].reshape(per_dev, topk_count - 1, heads_dev, block_rows),
        -1e30,
    )
    highest = jnp.maximum(own_lse, jnp.max(pair_lse, axis=1))
    own_weight = jnp.exp(own_lse - highest)
    pair_weight = jnp.where(live_pairs[:, :, None, None], jnp.exp(pair_lse - highest[:, None]), 0.0)
    numerator = jnp.transpose(own_weight, (0, 2, 1))[..., None] * own_out
    numerator = numerator + jnp.sum(
        jnp.transpose(pair_weight, (0, 1, 3, 2))[..., None] * pair_out, axis=1
    )
    denominator = own_weight + jnp.sum(pair_weight, axis=1)
    attended = (numerator / jnp.transpose(denominator, (0, 2, 1))[..., None]).reshape(rows, width)
    squares = jnp.sum(attended * attended, axis=1)
    summed = lax.psum(squares, "head")
    factor = lax.rsqrt(summed / (HEADS * HD) + 1e-06)
    return (attended * factor[:, None] * norm_gain.astype(jnp.float32)[None, :]).astype(
        jnp.bfloat16
    )


SPLIT = (True, True, False, False)
SCATTER = (False, False, False, False)
ORDER = (
    ("p", 0, 1),
    ("w", "plans"),
    ("w", "near_down_keep_c0"),
    ("w", "far_down_keep_c0"),
    ("w", "lift_keep_c0"),
    ("j", 0),
    ("p", 2),
    ("j", 1),
    ("p", 3),
    ("s", 0),
    ("a", 0),
    ("j", 2),
    ("s", 1),
    ("a", 1),
    ("w", "near_up_c0"),
    ("w", "far_up_c0"),
    ("j", 3),
    ("s", 2),
    ("a", 2),
    ("m", 0, 1),
    ("a", 3),
    ("s", 3),
    ("m", 2),
    ("m", 3),
)
COSTS = {"pack": 0.0, "join": 0.0, "served": 0.0, "own": 0.0, "merge": 0.0, "finish": 0.0}
DIRECT = True
UNROLL = 2
VMEM_LIMIT = 16 * 1024 * 1024


def unit_fields(code):
    return code & 31, (code >> 5) & 31, (code >> 10) & 63, (code >> 16) & 1, (code >> 17) & 1


def unit_code(slot, span, out, first, diagonal):
    return slot + span * 32 + out * 1024 + first * 65536 + diagonal * 131072


PIECES = {
    "head": lambda ref, h: ref.at[h],
    "next head": lambda ref, h: ref.at[h + 1],
    "queries": lambda ref, h: ref.at[h, 0],
    "keys_values": lambda ref, h: ref.at[h, pl.ds(1, 2)],
    "first": lambda ref, h: ref.at[0, h],
    "second": lambda ref, h: ref.at[1, h],
}


def attention_kernel(shape, own, groups, q_pieces, kv_pieces, n_in, plan, *refs):
    heads, per_dev, block_rows = shape
    n_q, n_kv = len(q_pieces), len(kv_pieces)
    inputs, refs = refs[:n_in], refs[n_in:]
    n_out = len(groups) + 2 * own
    outs, refs = refs[:n_out], refs[n_out:]
    (q_scr, kv_scr, s0, s1, p0, p1, d0, d1, acc_scr, top_scr, sum_scr, o_scr, lse_scr, sems) = refs[:14]
    s_scr, p_scr, decay_scr = (s0, s1), (p0, p1), (d0, d1)
    spans = n_q * per_dev
    copies = []
    for h in range(heads):
        for i, (n, kind) in enumerate(q_pieces):
            copies.append((PIECES[kind](inputs[n], h), q_scr.at[h, i], sems.at[h, i]))
        for i, (n, kind) in enumerate(kv_pieces):
            copies.append((PIECES[kind](inputs[n], h), kv_scr.at[h, i], sems.at[h, n_q + i]))
    copies = [pltpu.make_async_copy(*copy) for copy in copies]
    for copy in copies:
        copy.start()
    s1[...] = jnp.zeros_like(s1)
    p0[...] = jnp.zeros_like(p0)
    d0[...] = jnp.zeros_like(d0)
    acc_scr[...] = jnp.zeros_like(acc_scr)
    top_scr[...] = jnp.zeros_like(top_scr)
    sum_scr[...] = jnp.ones_like(sum_scr)
    if own:
        bias_scr = refs[14]
        key_pos = lax.broadcasted_iota(jnp.int32, (block_rows, block_rows), 0)
        query_pos = lax.broadcasted_iota(jnp.int32, (block_rows, block_rows), 1)
        bias_scr[0] = jnp.zeros((block_rows, block_rows), jnp.float32)
        bias_scr[1] = jnp.where(key_pos <= query_pos, 0.0, -1e30)
    for copy in copies:
        copy.wait()

    def rows_of(i):
        return pl.ds(pl.multiple_of((i % per_dev) * block_rows, block_rows), block_rows)

    def step(h, at, now, acc, top, total):
        before = 1 - now
        for u in range(UNROLL):
            slot, _, out, _, _ = unit_fields(plan[at + u])
            vt = kv_scr[h, slot // per_dev, 1, rows_of(slot), :]
            vt = jnp.concatenate([vt[:HD], vt[HD:]], axis=1)
            mixed = jnp.dot(vt, p_scr[now][u], preferred_element_type=jnp.float32)
            acc = acc * decay_scr[now][u, 0:1, :] + mixed
            o_scr[out] = (acc * decay_scr[now][u, 1:2, :]).astype(o_scr.dtype)
        for u in range(UNROLL):
            _, _, out, first, diagonal = unit_fields(plan[at + UNROLL + u])
            s = s_scr[before][u]
            if own:
                s = s + bias_scr[diagonal]
            old = jnp.where(first == 1, -1e30, top)
            top = jnp.maximum(old, jnp.max(s, axis=0, keepdims=True))
            decay = jnp.exp2((old - top) * EXP_SCALE)
            p = jnp.exp2((s - top) * EXP_SCALE)
            total = total * decay + jnp.sum(p, axis=0, keepdims=True)
            p_scr[before][u] = p.astype(jnp.bfloat16)
            decay_scr[before][u, 0:1, :] = decay
            decay_scr[before][u, 1:2, :] = 1.0 / total
            lse_scr[pl.ds(out, 1), :] = top * EXP_SCALE + jnp.log(total) * LOG2E
        for u in range(UNROLL):
            slot, span, _, _, _ = unit_fields(plan[at + 2 * UNROLL + u])
            k = kv_scr[h, slot // per_dev, 0, rows_of(slot), :]
            q = q_scr[h, span // per_dev, rows_of(span), :]
            s_scr[now][u] = lax.dot_general(
                k, q, (((1,), (1,)), ((), ())), preferred_element_type=jnp.float32
            )
        return acc, top, total

    for h in range(heads):
        o_scr[...] = jnp.zeros_like(o_scr)
        lse_scr[...] = jnp.full_like(lse_scr, -1e30)

        def two_steps(i, carry):
            state = (acc_scr[...], top_scr[...], sum_scr[...])
            state = step(h, 1 + 2 * i * UNROLL, 0, *state)
            state = step(h, 1 + (2 * i + 1) * UNROLL, 1, *state)
            acc_scr[...], top_scr[...], sum_scr[...] = state
            return carry

        lax.fori_loop(0, (plan[0] + 1) // 2, two_steps, 0)
        if own:
            kept = outs[0].shape[1]
            outs[0][h] = o_scr[:kept]
            outs[1][h] = lse_scr[:kept, :]
        for out, (start, stop) in zip(outs[2 if own else 0 :], groups):
            n = stop - start
            for span in range(n):
                out[h, span * HD : (span + 1) * HD, :] = o_scr[start + span].astype(jnp.bfloat16)
            lse = lse_scr[start:stop, :]
            high = lse.astype(jnp.bfloat16).astype(jnp.float32)
            middle = (lse - high).astype(jnp.bfloat16).astype(jnp.float32)
            rest = jnp.zeros((lse_rows(n) - 3 * n, block_rows), jnp.float32)
            parts = jnp.concatenate([high, middle, lse - high - middle, rest], axis=0)
            out[h, n * HD :, :] = parts.astype(jnp.bfloat16)


def lse_rows(spans):
    return -(-3 * spans // 16) * 16


def unpacked_lse(ref, h, spans):
    parts = ref[h, spans * HD :, :].astype(jnp.float32)
    return parts[:spans] + parts[spans : 2 * spans] + parts[2 * spans : 3 * spans]


def cost(name):
    us = COSTS[name]
    return pl.CostEstimate(flops=int(us * 1e9) + 1, bytes_accessed=int(us * 3.4e6) + 1, transcendentals=0)


def ordered(kernel, n_after):
    def body(*refs):
        kernel(*refs[n_after:])

    return body


def attention_call(plan, q_pieces, kv_pieces, own, direct, heads, per_dev, block_rows, after=()):
    inputs = []

    def numbered(pieces):
        out = []
        for array, kind in pieces:
            if not any(array is known for known in inputs):
                inputs.append(array)
            out.append(([array is known for known in inputs].index(True), kind))
        return out

    q_pieces, kv_pieces = numbered(q_pieces), numbered(kv_pieces)
    n_q, n_kv = len(q_pieces), len(kv_pieces)
    spans = n_q * per_dev
    vmem, hbm = pl.BlockSpec(memory_space=pltpu.VMEM), pl.BlockSpec(memory_space=pltpu.HBM)
    f32, bf16 = jnp.float32, jnp.bfloat16
    if own:
        kept = per_dev if direct else spans
        groups = ((per_dev, spans),) if direct else ()
        out_shape = [
            jax.ShapeDtypeStruct((heads, kept, HD, block_rows), f32),
            jax.ShapeDtypeStruct((heads, kept, block_rows), f32),
        ]
    else:
        size = per_dev if direct else 2 * per_dev
        groups = tuple((start, start + size) for start in range(0, spans, size))
        out_shape = []
    for start, stop in groups:
        packed_rows = (stop - start) * HD + lse_rows(stop - start)
        out_shape.append(jax.ShapeDtypeStruct((heads, packed_rows, block_rows), bf16))
    scratch = [
        pltpu.VMEM((heads, n_q, per_dev * block_rows, HD), bf16),
        pltpu.VMEM((heads, n_kv, 2, per_dev * block_rows, HD), bf16),
        pltpu.VMEM((UNROLL, block_rows, block_rows), f32),
        pltpu.VMEM((UNROLL, block_rows, block_rows), f32),
        pltpu.VMEM((UNROLL, block_rows, block_rows), bf16),
        pltpu.VMEM((UNROLL, block_rows, block_rows), bf16),
        pltpu.VMEM((UNROLL, 8, block_rows), f32),
        pltpu.VMEM((UNROLL, 8, block_rows), f32),
        pltpu.VMEM((HD, block_rows), f32),
        pltpu.VMEM((1, block_rows), f32),
        pltpu.VMEM((1, block_rows), f32),
        pltpu.VMEM((spans + 1, HD, block_rows), f32 if own else bf16),
        pltpu.VMEM((spans + 8, block_rows), f32),
        pltpu.SemaphoreType.DMA((heads, n_q + n_kv)),
    ]
    if own:
        scratch.append(pltpu.VMEM((2, block_rows, block_rows), f32))
    return pl.pallas_call(
        ordered(
            partial(
                attention_kernel,
                (heads, per_dev, block_rows),
                own,
                groups,
                q_pieces,
                kv_pieces,
                len(inputs),
            ),
            len(after),
        ),
        out_shape=out_shape,
        in_specs=[hbm] * len(after) + [pl.BlockSpec(memory_space=pltpu.SMEM)] + [hbm] * len(inputs),
        out_specs=[vmem] * len(out_shape),
        scratch_shapes=scratch,
        compiler_params=pltpu.CompilerParams(vmem_limit_bytes=VMEM_LIMIT),
        cost_estimate=cost("own" if own else "served"),
        name="own_attention" if own else "served_attention",
    )(*after, plan, *inputs)


def pack_kernel(shape, place, q_ref, k_ref, v_ref, *refs):
    heads, first, half, rows, split, scatter = shape
    outs, (scr, t_scr, sems) = refs[:-3], refs[-3:]
    loads, stores = {}, []
    places = [(side, h) for h in range(heads) for side in (1, 0)]
    for side, h in places:
        start = pl.multiple_of((place[side] * half + first + h) * HD, HD)
        for i, ref in enumerate((q_ref, k_ref, v_ref)):
            loads[side, h, i] = pltpu.make_async_copy(
                ref.at[:, pl.ds(start, HD)], scr.at[side, h, i], sems.at[0, side, h, i]
            )
            loads[side, h, i].start()

    if scatter:
        for h in range(heads):
            t_scr[0, h] = jnp.zeros_like(t_scr[0, h])
            for i in range(3):
                blank = pltpu.make_async_copy(
                    t_scr.at[0, h], outs[-heads + h].at[place[0], i], sems.at[2, 0, h, i]
                )
                blank.start()
                blank.wait()

    def store(side, h, i, source):
        if side:
            target = outs[-heads + h].at[place[1] if scatter else 0, i]
        elif split:
            target = outs[1].at[h, i - 1] if i else outs[0].at[h]
        else:
            target = outs[0].at[h, i]
        copy = pltpu.make_async_copy(source, target, sems.at[1, side, h, i])
        copy.start()
        stores.append(copy)

    for side, h in places:
        for i in range(2):
            loads[side, h, i].wait()
            store(side, h, i, scr.at[side, h, i])
        loads[side, h, 2].wait()
        for tile in range(rows // HD):
            at = slice(tile * HD, (tile + 1) * HD)
            t_scr[side, h, at, :] = scr[side, h, 2, at, :].T
        store(side, h, 2, t_scr.at[side, h])
    for copy in stores:
        copy.wait()


def pack_call(place, queries, keys, values, heads, first, half, split, scatter, after=()):
    rows = queries.shape[0]
    hbm = pl.BlockSpec(memory_space=pltpu.HBM)
    bf16 = jnp.bfloat16
    queries, keys, values = (
        pltpu.with_memory_space_constraint(array, pltpu.HBM) for array in (queries, keys, values)
    )
    if split:
        outs = [
            jax.ShapeDtypeStruct((heads, rows, HD), bf16),
            jax.ShapeDtypeStruct((heads, 2, rows, HD), bf16),
        ]
    else:
        outs = [jax.ShapeDtypeStruct((heads, 3, rows, HD), bf16)]
    outs += [jax.ShapeDtypeStruct((2 if scatter else 1, 3, rows, HD), bf16)] * heads
    return pl.pallas_call(
        ordered(partial(pack_kernel, (heads, first, half, rows, split, scatter)), len(after)),
        out_shape=outs,
        in_specs=[hbm] * len(after) + [pl.BlockSpec(memory_space=pltpu.SMEM)] + [hbm] * 3,
        out_specs=[hbm] * len(outs),
        scratch_shapes=[
            pltpu.VMEM((2, heads, 3, rows, HD), bf16),
            pltpu.VMEM((2, heads, rows, HD), bf16),
            pltpu.SemaphoreType.DMA((3, 2, heads, 3)),
        ],
        compiler_params=pltpu.CompilerParams(vmem_limit_bytes=VMEM_LIMIT),
        cost_estimate=cost("pack"),
        name="pack",
    )(*after, place, queries, keys, values)


def cut_kernel(ref, q_ref, kv_ref, scr, sems):
    load = pltpu.make_async_copy(ref, scr, sems.at[0])
    load.start()
    load.wait()
    stores = [
        pltpu.make_async_copy(scr.at[0, 0], q_ref.at[0], sems.at[1]),
        pltpu.make_async_copy(scr.at[0, pl.ds(1, 2)], kv_ref.at[0], sems.at[2]),
    ]
    for store in stores:
        store.start()
    for store in stores:
        store.wait()


def cut_call(packed, after=()):
    _, _, rows, _ = packed.shape
    hbm = pl.BlockSpec(memory_space=pltpu.HBM)
    return pl.pallas_call(
        ordered(cut_kernel, len(after)),
        out_shape=(
            jax.ShapeDtypeStruct((1, rows, HD), jnp.bfloat16),
            jax.ShapeDtypeStruct((1, 2, rows, HD), jnp.bfloat16),
        ),
        in_specs=[hbm] * (len(after) + 1),
        out_specs=(hbm, hbm),
        scratch_shapes=[
            pltpu.VMEM(packed.shape, jnp.bfloat16),
            pltpu.SemaphoreType.DMA((3,)),
        ],
        compiler_params=pltpu.CompilerParams(vmem_limit_bytes=VMEM_LIMIT),
        cost_estimate=cost("join"),
        name="join",
    )(*after, packed)


def join_kernel(heads, keep_ref, swap_ref, q_ref, kv_ref, scr, sems):
    loads, stores = [], []
    for side, ref in enumerate((keep_ref, swap_ref)):
        for h in range(heads):
            loads.append(pltpu.make_async_copy(ref.at[h], scr.at[side, h], sems.at[0, side, h]))
            stores.append(
                (
                    pltpu.make_async_copy(scr.at[side, h, 0], q_ref.at[side, h], sems.at[1, side, h]),
                    pltpu.make_async_copy(
                        scr.at[side, h, pl.ds(1, 2)], kv_ref.at[side, h], sems.at[2, side, h]
                    ),
                )
            )
    for load in loads:
        load.start()
    for load, pair in zip(loads, stores):
        load.wait()
        for store in pair:
            store.start()
    for pair in stores:
        for store in pair:
            store.wait()


def join_call(keep, swapped, after=()):
    heads, _, rows, _ = keep.shape
    hbm = pl.BlockSpec(memory_space=pltpu.HBM)
    return pl.pallas_call(
        ordered(partial(join_kernel, heads), len(after)),
        out_shape=(
            jax.ShapeDtypeStruct((2, heads, rows, HD), jnp.bfloat16),
            jax.ShapeDtypeStruct((2, heads, 2, rows, HD), jnp.bfloat16),
        ),
        in_specs=[hbm] * (len(after) + 2),
        out_specs=(hbm, hbm),
        scratch_shapes=[
            pltpu.VMEM((2, heads, 3, rows, HD), jnp.bfloat16),
            pltpu.SemaphoreType.DMA((3, 2, heads)),
        ],
        compiler_params=pltpu.CompilerParams(vmem_limit_bytes=VMEM_LIMIT),
        cost_estimate=cost("join"),
        name="join",
    )(*after, keep, swapped)


def merge_kernel(per_dev, block_rows, sizes, valid, sofar_ref, *refs):
    inputs, (keep_ref, send_ref, squares_ref) = refs[:-3], refs[-3:]
    spans = 2 * per_dev
    squares_ref[...] = sofar_ref[...]
    at = 0
    for c, size in enumerate(sizes):
        own_ref, own_lse_ref, near_ref, far_ref = inputs[4 * c : 4 * c + 4]
        for h in range(size):
            lses = [own_lse_ref[h]]
            for i, ref in enumerate((near_ref, far_ref)):
                lses.append(jnp.where(valid[i] > 0, unpacked_lse(ref, h, spans), -1e30))
            top = jnp.maximum(jnp.maximum(lses[0], lses[1]), lses[2])
            weights = [jnp.exp2(lse - top) for lse in lses]
            scale = 1.0 / (weights[0] + weights[1] + weights[2])
            weights = [weight * scale for weight in weights]
            for span in range(spans):
                rows = slice(span, span + 1)
                tile = slice(span * HD, (span + 1) * HD)
                mixed = weights[0][rows, :] * own_ref[h, span]
                mixed = mixed + weights[1][rows, :] * near_ref[h, tile, :].astype(jnp.float32)
                mixed = mixed + weights[2][rows, :] * far_ref[h, tile, :].astype(jnp.float32)
                squares_ref[rows, :] = squares_ref[rows, :] + jnp.sum(mixed * mixed, axis=0, keepdims=True)
                target = keep_ref if span < per_dev else send_ref
                start = (span % per_dev) * block_rows
                target[at, start : start + block_rows, :] = mixed.T.astype(target.dtype)
            at += 1


def merge_call(valid, sofar, parts, per_dev, after=()):
    block_rows = sofar.shape[1]
    sizes = [own[0].shape[0] for own, _, _ in parts]
    arrays = [array for own, near, far in parts for array in (*own, near, far)]
    vmem = pl.BlockSpec(memory_space=pltpu.VMEM)
    hbm = pl.BlockSpec(memory_space=pltpu.HBM)
    packed = jax.ShapeDtypeStruct((sum(sizes), per_dev * block_rows, HD), jnp.bfloat16)
    return pl.pallas_call(
        ordered(partial(merge_kernel, per_dev, block_rows, sizes), len(after)),
        out_shape=(packed, packed, jax.ShapeDtypeStruct(sofar.shape, jnp.float32)),
        in_specs=[hbm] * len(after)
        + [pl.BlockSpec(memory_space=pltpu.SMEM)]
        + [vmem] * (1 + len(arrays)),
        out_specs=(vmem, vmem, vmem),
        compiler_params=pltpu.CompilerParams(vmem_limit_bytes=VMEM_LIMIT),
        cost_estimate=cost("merge"),
        name="merge",
    )(*after, valid, sofar, *arrays)


def own_merge_kernel(per_dev, block_rows, valid, sofar_ref, squares_in_ref, own_ref, own_lse_ref, *refs):
    other_ref, packs, outs, squares_ref = refs[0], refs[1:5], refs[5:7], refs[7]
    squares_ref[...] = sofar_ref[:per_dev, :] + squares_in_ref[...]
    for side in range(2):
        arrivals = (packs[side], packs[2 + side])
        lses = [unpacked_lse(other_ref, 0, per_dev) if side else own_lse_ref[0]]
        for i, ref in enumerate(arrivals):
            lses.append(jnp.where(valid[i] > 0, unpacked_lse(ref, 0, per_dev), -1e30))
        top = jnp.maximum(jnp.maximum(lses[0], lses[1]), lses[2])
        weights = [jnp.exp2(lse - top) for lse in lses]
        scale = 1.0 / (weights[0] + weights[1] + weights[2])
        weights = [weight * scale for weight in weights]
        for span in range(per_dev):
            rows = slice(span, span + 1)
            tile = slice(span * HD, (span + 1) * HD)
            mixed = other_ref[0, tile, :].astype(jnp.float32) if side else own_ref[0, span]
            mixed = weights[0][rows, :] * mixed
            for weight, ref in zip(weights[1:], arrivals):
                mixed = mixed + weight[rows, :] * ref[0, tile, :].astype(jnp.float32)
            squares_ref[rows, :] = squares_ref[rows, :] + jnp.sum(mixed * mixed, axis=0, keepdims=True)
            at = slice(span * block_rows, (span + 1) * block_rows)
            outs[side][0, at, :] = mixed.T.astype(jnp.bfloat16)


def own_merge_call(valid, sofar, squares_in, own, other, packs, per_dev, after=()):
    block_rows = sofar.shape[1]
    vmem = pl.BlockSpec(memory_space=pltpu.VMEM)
    hbm = pl.BlockSpec(memory_space=pltpu.HBM)
    packed = jax.ShapeDtypeStruct((1, per_dev * block_rows, HD), jnp.bfloat16)
    return pl.pallas_call(
        ordered(partial(own_merge_kernel, per_dev, block_rows), len(after)),
        out_shape=(packed, packed, jax.ShapeDtypeStruct((per_dev, block_rows), jnp.float32)),
        in_specs=[hbm] * len(after) + [pl.BlockSpec(memory_space=pltpu.SMEM)] + [vmem] * 9,
        out_specs=(vmem, vmem, vmem),
        compiler_params=pltpu.CompilerParams(vmem_limit_bytes=VMEM_LIMIT),
        cost_estimate=cost("merge"),
        name="merge",
    )(*after, valid, sofar, squares_in, *own, other, *packs)


def finish_kernel(per_dev, sizes, place, *refs):
    n = len(sizes)
    kept, returned = refs[:n], refs[n : 2 * n]
    squares_ref, gain_ref, out_ref = refs[2 * n :]
    block_rows = squares_ref.shape[1]
    half = sum(sizes)
    factor = lax.rsqrt(squares_ref[...] / (HEADS * HD) + 1e-06)
    for b in range(per_dev):
        column = jnp.broadcast_to(factor[b : b + 1, :], (HD, block_rows)).T
        rows = slice(b * block_rows, (b + 1) * block_rows)
        for side, pieces in enumerate((kept, returned)):
            head = 0
            for piece, size in zip(pieces, sizes):
                for h in range(size):
                    start = pl.multiple_of((place[side] * half + head) * HD, HD)
                    gain = gain_ref[:, pl.ds(start, HD)].astype(jnp.float32)
                    value = piece[h, rows, :].astype(jnp.float32) * column * gain
                    out_ref[rows, pl.ds(start, HD)] = value.astype(out_ref.dtype)
                    head += 1


def finish_call(place, kept, returned, squares, gain, per_dev):
    vmem = pl.BlockSpec(memory_space=pltpu.VMEM)
    rows, width = kept[0].shape[1], gain.shape[0]
    return pl.pallas_call(
        partial(finish_kernel, per_dev, [k.shape[0] for k in kept]),
        out_shape=jax.ShapeDtypeStruct((rows, width), jnp.bfloat16),
        in_specs=[pl.BlockSpec(memory_space=pltpu.SMEM)] + [vmem] * (2 * len(kept) + 2),
        out_specs=vmem,
        compiler_params=pltpu.CompilerParams(vmem_limit_bytes=VMEM_LIMIT),
        cost_estimate=cost("finish"),
        name="finish",
    )(place, *kept, *returned, squares, gain.reshape(1, width))


def plan_of(live, slot, diagonal, dump):
    spans, entries = live.shape
    t = jnp.arange(entries)
    earlier = jnp.sum((t[None, None, :] < t[None, :, None]) & live[:, None, :], axis=2)
    span = lax.broadcasted_iota(jnp.int32, live.shape, 0)
    code = unit_code(slot, span, span, (earlier == 0).astype(jnp.int32), diagonal)
    code, live = code.reshape(-1), live.reshape(-1)
    n = spans * entries
    i = jnp.arange(n)
    rank = jnp.sum((i[None, :] < i[:, None]) & live[None, :], axis=1)
    at = jnp.arange(n + 8 * UNROLL)
    hit = live[None, :] & (rank[None, :] + 2 * UNROLL == at[:, None])
    idle = unit_code(0, 0, dump, 1, 0)
    codes = jnp.sum(jnp.where(hit, code[None, :] - idle, 0), axis=1) + idle
    total = jnp.sum(live.astype(jnp.int32))
    steps = jnp.where(total > 0, (total + UNROLL - 1) // UNROLL + 2, 0)
    return jnp.concatenate([steps[None], codes]).astype(jnp.int32)


def level_shards(queries, keys, values, selection, norm_gain):
    device = lax.axis_index("ctx")
    level, x = device // 2, device % 2
    rows, width = queries.shape
    per_dev, topk = selection.shape
    block_rows = rows // per_dev
    spans = 2 * per_dev
    half = width // HD // 2

    sent = {}

    def to(array, pairs, name):
        with jax.named_scope(name):
            sent[name] = lax.ppermute(array, "ctx", pairs)
        return sent[name]

    def exchange(array, name):
        pairs = [[d, d + 1] for d in range(0, 8, 2)]
        with jax.named_scope(name):
            sent[name] = lax.psum_scatter(
                array, "ctx", scatter_dimension=0, axis_index_groups=pairs, tiled=True
            )
        return sent[name]

    swap = [(d, d ^ 1) for d in range(8)]
    lift = [(0, 2), (1, 3)]
    near_down, far_down = [(4, 2), (5, 3), (6, 4), (7, 5)], [(6, 2), (7, 3)]

    def crossed(pairs):
        return [(source, target ^ 1) for source, target in pairs]

    near_up, far_up = [(2, 4), (3, 5), (4, 6), (5, 7)], [(2, 6), (3, 7)]
    valid = jnp.stack([level >= 2, level >= 3]).astype(jnp.int32)
    place = jnp.stack([x, 1 - x]).astype(jnp.int32)

    own_selection = jnp.concatenate([selection, to(selection, swap, "selection_swap")], axis=0)
    above = to(own_selection, [(6, 4), (7, 5)], "selection_near")
    two = to(jnp.concatenate([own_selection, above], axis=0), [(4, 2), (5, 3)], "selection_far")
    near_selection = jnp.where(level == 2, above, two[:spans])
    far_selection = two[spans:]

    def ids(at):
        first = jnp.stack([(at * 2 + x) * per_dev, (at * 2 + 1 - x) * per_dev])
        return (first[:, None] + jnp.arange(per_dev)[None, :]).reshape(-1, 1)

    def slots(blocks):
        owner = blocks // per_dev
        slot = jnp.where(owner // 2 == level, 0, spans) + jnp.where(owner % 2 == x, 0, per_dev)
        return owner // 2, slot + blocks % per_dev

    others = own_selection[:, 1:]
    block_level, slot = slots(others)
    live = (others != ids(level)) & ((block_level == level) | ((level == 1) & (block_level == 0)))
    first = jnp.ones((spans, 1), jnp.int32)
    own_plan = plan_of(
        jnp.concatenate([first > 0, live], axis=1),
        jnp.concatenate([jnp.arange(spans, dtype=jnp.int32)[:, None], slot], axis=1),
        jnp.concatenate([first, jnp.zeros_like(others)], axis=1),
        spans,
    )
    others = jnp.concatenate([near_selection, far_selection], axis=0)[:, 1:]
    block_level, slot = slots(others)
    is_near = lax.broadcasted_iota(jnp.int32, others.shape, 0) < spans
    mine = ((level == 1) & (block_level <= 1)) | ((level == 2) & (block_level == 2) & is_near)
    live = (others != jnp.concatenate([ids(level + 1), ids(level + 2)], axis=0)) & mine
    served_plan = plan_of(live, slot, jnp.zeros_like(others), 2 * spans)

    n, split, order = half, SPLIT, ORDER
    own_pieces, z_arrays, served_pieces, downs_of = {}, {}, {}, {}
    ups, owns, others, squares_in, kept, returned = {}, {}, {}, [], [], []
    squares = [jnp.zeros((spans, block_rows), jnp.float32)]
    last = []

    def downs(q, kv, name):
        low = to(kv, lift, f"lift_{name}")
        far = to(q, far_down, f"far_down_{name}")
        return to(q, near_down, f"near_down_{name}"), far, low

    def pack(*chunks):
        c = chunks[0]
        packed = pack_call(
            place, queries, keys, values, len(chunks), c, half, split[c], SCATTER[c], last
        )
        last[:] = [packed[0]]
        if SCATTER[c]:
            swapped = [exchange(p, f"swap_c{d}") for d, p in zip(chunks, packed[-len(chunks) :])]
        else:
            swapped = [to(p, swap, f"swap_c{d}") for d, p in zip(chunks, packed[-len(chunks) :])]
        if split[c]:
            keeps = downs(packed[0], packed[1], f"keep_c{c}")
            for d, kind, swap_d in zip(chunks, ("head", "next head"), swapped):
                downs_of[d] = [(array, kind) for array in keeps]
                z_arrays[d] = (swap_d,)
                own_pieces[d] = (
                    [(packed[0], kind), (swap_d, "queries")],
                    [(packed[1], kind), (swap_d, "keys_values")],
                )
        else:
            z_arrays[c] = (packed[0], swapped[0])
            own_pieces[c] = (
                [(array, "queries") for array in z_arrays[c]],
                [(array, "keys_values") for array in z_arrays[c]],
            )

    def join(c):
        if split[c]:
            q_swap, kv_swap = cut_call(*z_arrays[c], last)
            last[:] = [q_swap]
            swaps = downs(q_swap, kv_swap, f"recv_c{c}")
            near, far, low = [[k, (r, "head")] for k, r in zip(downs_of[c], swaps)]
        else:
            level_q, level_kv = join_call(*z_arrays[c], last)
            last[:] = [level_q]
            near, far, low = [
                [(array, "first"), (array, "second")] for array in downs(level_q, level_kv, f"c{c}")
            ]
        served_pieces[c] = (near + far, own_pieces[c][1] + low)

    def is_direct(c):
        return DIRECT and c == n - 1

    def serve(c):
        packs = attention_call(
            served_plan, *served_pieces[c], False, is_direct(c), 1, per_dev, block_rows, last
        )
        last[:] = [packs[0]]
        if is_direct(c):
            near_same, near_cross, far_same, far_cross = packs
            far = (
                to(far_same, far_up, f"far_up_same_c{c}"),
                to(far_cross, crossed(far_up), f"far_up_cross_c{c}"),
            )
            near = (
                to(near_same, near_up, f"near_up_same_c{c}"),
                to(near_cross, crossed(near_up), f"near_up_cross_c{c}"),
            )
            ups[c] = (*near, *far)
        else:
            near, far = packs
            far = to(far, far_up, f"far_up_c{c}")
            ups[c] = (to(near, near_up, f"near_up_c{c}"), far)

    def attend(c):
        state = attention_call(
            own_plan,
            own_pieces[c][0],
            served_pieces[c][1],
            True,
            is_direct(c),
            1,
            per_dev,
            block_rows,
            last,
        )
        last[:] = [state[1]]
        owns[c] = state[:2]
        if is_direct(c):
            others[c] = to(state[2], swap, f"back_own_c{c}")

    def merge(*chunks):
        if is_direct(chunks[0]):
            c = chunks[0]
            keep, back, squares[0] = own_merge_call(
                valid, squares[0], squares_in[0], owns[c], others[c], ups[c], per_dev, last
            )
            kept.append(keep)
            returned.append(back)
            return
        parts = [(owns[c], *ups[c]) for c in chunks]
        keep, send, squares[0] = merge_call(valid, squares[0], parts, per_dev, last)
        last[:] = [keep]
        kept.append(keep)
        returned.append(to(send, swap, f"back_c{chunks[0]}"))
        if DIRECT and chunks[-1] == n - 2:
            squares_in.append(to(squares[0][per_dev:], swap, "squares_swap"))

    steps = {"p": pack, "j": join, "s": serve, "a": attend, "m": merge}
    for what, *args in order:
        if what == "w":
            last.extend([own_plan, served_plan] if args[0] == "plans" else [sent[args[0]]])
        else:
            steps[what](*args)
    square = squares[0]
    if not DIRECT:
        square = square[:per_dev] + to(square[per_dev:], swap, "squares_swap")
    n_head = lax.axis_size("head")
    hop = 1
    while hop < n_head:
        square = square + lax.ppermute(square, "head", [(i, i ^ hop) for i in range(n_head)])
        hop *= 2
    return finish_call(place, kept, returned, square, norm_gain, per_dev)


def solution(mesh):
    placed = (P("ctx", "head"), P("ctx", "head"), P("ctx", "head"), P("ctx", None), P("head"))
    body = level_shards if mesh.shape["ctx"] == 8 else shards
    return jax.shard_map(
        body, mesh=mesh, in_specs=placed, out_specs=P("ctx", "head"), check_vma=False
    )
```

```python
from functools import partial
import math

import jax
import jax.numpy as jnp
from jax import lax
from jax.experimental import pallas as pl
from jax.experimental.pallas import tpu as pltpu
from jax.sharding import PartitionSpec as P

HEADS = 32
HD = 128
CAP = 2
LOG2E = math.log2(math.e)
EXP_SCALE = HD ** (-0.5) * LOG2E


def partial_state(query_rows, key_block, value_block, causal):
    scores = jnp.einsum(
        "sqhd,skhd->shqk", query_rows, key_block, preferred_element_type=jnp.float32
    ) * query_rows.shape[3] ** (-0.5)
    if causal:
        query_pos = lax.broadcasted_iota(jnp.int32, scores.shape, 2)
        key_pos = lax.broadcasted_iota(jnp.int32, scores.shape, 3)
        scores = jnp.where(key_pos <= query_pos, scores, -1e30)
    row_peak = jnp.max(scores, axis=3)
    exponentials = jnp.exp(scores - row_peak[..., None])
    row_sum = jnp.sum(exponentials, axis=3)
    weights = exponentials.astype(jnp.bfloat16)
    blended = jnp.einsum(
        "shqk,skhd->sqhd", weights, value_block, preferred_element_type=jnp.float32
    )
    blended = blended / jnp.transpose(row_sum, (0, 2, 1))[..., None]
    return (blended, row_peak + jnp.log(row_sum))


def slot_plan(selected, first_span, per_dev, capacity):
    own_span = first_span + lax.broadcasted_iota(jnp.int32, selected.shape, 0)
    is_live = (selected != own_span).reshape(-1)
    owner_dev = (selected // per_dev).reshape(-1)
    pair_count = owner_dev.shape[0]
    is_later = lax.broadcasted_iota(jnp.int32, (pair_count, pair_count), 0) > lax.broadcasted_iota(
        jnp.int32, (pair_count, pair_count), 1
    )
    earlier = is_later & (owner_dev[:, None] == owner_dev[None, :]) & is_live[None, :]
    slot_rank = jnp.sum(earlier.astype(jnp.int32), axis=1)
    slot_index = jnp.where(is_live, owner_dev * capacity + slot_rank, 0)
    return (slot_index, is_live, (selected % per_dev).reshape(-1))


def shards(queries, keys, values, selection, norm_gain):
    n_ctx = lax.axis_size("ctx")
    device = lax.axis_index("ctx")
    rows, width = queries.shape
    per_dev, topk_count = selection.shape
    block_rows = rows // per_dev
    heads_dev = width // HD
    slot_count = n_ctx * CAP
    group_size = math.gcd(slot_count, 4)
    query_blocks = queries.reshape(per_dev, block_rows, heads_dev, HD)
    key_blocks = keys.reshape(per_dev, block_rows, heads_dev, HD)
    value_blocks = values.reshape(per_dev, block_rows, heads_dev, HD)
    slot_index, is_live, local_block = slot_plan(selection[:, 1:], device * per_dev, per_dev, CAP)
    pair_count = slot_index.shape[0]
    pair_span = lax.broadcasted_iota(jnp.int32, (pair_count,), 0) // (topk_count - 1)
    slot_ids = lax.broadcasted_iota(jnp.int32, (slot_count, pair_count), 0)
    placed = (slot_ids == slot_index[None, :]) & is_live[None, :]
    slot_span = jnp.sum(jnp.where(placed, pair_span[None, :], 0), axis=1)
    everyone = lax.all_gather(selection, "ctx", axis=0, tiled=True)
    requests = everyone[:, 1:].reshape(n_ctx, per_dev, topk_count - 1)
    first_spans = lax.broadcasted_iota(jnp.int32, (n_ctx,), 0) * per_dev
    all_slots, all_live, all_local = jax.vmap(partial(slot_plan, per_dev=per_dev, capacity=CAP))(
        requests, first_spans
    )
    owner_devs = requests.reshape(n_ctx, -1) // per_dev
    served = all_live & (owner_devs == device)
    capacity_ids = lax.broadcasted_iota(jnp.int32, (1, CAP, 1), 1)
    matched = served[:, None, :] & (all_slots[:, None, :] == device * CAP + capacity_ids)
    send_block = jnp.sum(jnp.where(matched, all_local[:, None, :], 0), axis=2)
    key_out = key_blocks[send_block].reshape(n_ctx, CAP, block_rows, width)
    value_out = value_blocks[send_block].reshape(n_ctx, CAP, block_rows, width)
    key_in, value_in = (
        lax.all_to_all(key_out, "ctx", split_axis=0, concat_axis=0, tiled=True),
        lax.all_to_all(value_out, "ctx", split_axis=0, concat_axis=0, tiled=True),
    )

    def one_group(packed):
        group_keys, group_values, group_span = packed
        blended, log_sums = partial_state(query_blocks[group_span], group_keys, group_values, False)
        return (blended.astype(jnp.bfloat16), log_sums)

    slot_out, slot_lse = lax.map(
        one_group,
        (
            key_in.reshape(-1, group_size, block_rows, heads_dev, HD),
            value_in.reshape(-1, group_size, block_rows, heads_dev, HD),
            slot_span.reshape(-1, group_size),
        ),
    )
    slot_out = slot_out.reshape(slot_count, block_rows, heads_dev, HD)
    slot_lse = slot_lse.reshape(slot_count, heads_dev, block_rows)
    own_out, own_lse = partial_state(query_blocks, key_blocks, value_blocks, True)
    live_pairs = is_live.reshape(per_dev, topk_count - 1)
    pair_out = (
        slot_out[slot_index]
        .reshape(per_dev, topk_count - 1, block_rows, heads_dev, HD)
        .astype(jnp.float32)
    )
    pair_lse = jnp.where(
        live_pairs[:, :, None, None],
        slot_lse[slot_index].reshape(per_dev, topk_count - 1, heads_dev, block_rows),
        -1e30,
    )
    highest = jnp.maximum(own_lse, jnp.max(pair_lse, axis=1))
    own_weight = jnp.exp(own_lse - highest)
    pair_weight = jnp.where(live_pairs[:, :, None, None], jnp.exp(pair_lse - highest[:, None]), 0.0)
    numerator = jnp.transpose(own_weight, (0, 2, 1))[..., None] * own_out
    numerator = numerator + jnp.sum(
        jnp.transpose(pair_weight, (0, 1, 3, 2))[..., None] * pair_out, axis=1
    )
    denominator = own_weight + jnp.sum(pair_weight, axis=1)
    attended = (numerator / jnp.transpose(denominator, (0, 2, 1))[..., None]).reshape(rows, width)
    squares = jnp.sum(attended * attended, axis=1)
    summed = lax.psum(squares, "head")
    factor = lax.rsqrt(summed / (HEADS * HD) + 1e-06)
    return (attended * factor[:, None] * norm_gain.astype(jnp.float32)[None, :]).astype(
        jnp.bfloat16
    )


SPLIT = (True, False, False, False)
SCATTER = (False, False, False, False)
ORDER = (
    ("p", 0),
    ("w", "plan"),
    ("w", "near_down_keep_c0"),
    ("w", "far_down_keep_c0"),
    ("w", "lift_keep_c0"),
    ("p", 1),
    ("j", 0),
    ("p", 2),
    ("j", 1),
    ("s", 0),
    ("j", 2),
    ("a", 0),
    ("p", 3),
    ("s", 1),
    ("m", 0),
    ("a", 1),
    ("j", 3),
    ("s", 2),
    ("m", 1),
    ("a", 2),
    ("w", "back_c0"),
    ("s", 3),
    ("a", 3),
    ("m", 2),
    ("m", 3),
)
COSTS = {"pack": 2, "join": 1, "served": 6, "own": 5, "merge": 1, "finish": 3}
DIRECT = True
NOTE_ROWS = 16
UNROLL = 2
VMEM_LIMIT = 16 * 1024 * 1024


def unit_fields(code):
    return code & 31, (code >> 5) & 31, (code >> 10) & 63, (code >> 16) & 1, (code >> 17) & 1


def unit_code(slot, span, out, first, diagonal):
    return slot + span * 32 + out * 1024 + first * 65536 + diagonal * 131072


PIECES = {
    "head": lambda ref, h, rows: ref.at[h],
    "next head": lambda ref, h, rows: ref.at[h + 1],
    "top rows": lambda ref, h, rows: ref.at[h, pl.ds(0, rows)],
    "queries": lambda ref, h, rows: ref.at[h, 0],
    "keys_values": lambda ref, h, rows: ref.at[h, pl.ds(1, 2)],
    "first": lambda ref, h, rows: ref.at[0, h],
    "second": lambda ref, h, rows: ref.at[1, h],
}


def attention_kernel(shape, own, groups, q_pieces, kv_pieces, n_in, plan, *refs):
    heads, per_dev, block_rows = shape
    n_q, n_kv = len(q_pieces), len(kv_pieces)
    inputs, refs = refs[:n_in], refs[n_in:]
    n_out = len(groups) + 2 * own
    outs, refs = refs[:n_out], refs[n_out:]
    (q_scr, kv_scr, s0, s1, p0, p1, d0, d1, acc_scr, top_scr, sum_scr, o_scr, lse_scr, sems) = refs[:14]
    s_scr, p_scr, decay_scr = (s0, s1), (p0, p1), (d0, d1)
    spans = n_q * per_dev
    copies = []
    for h in range(heads):
        for i, (n, kind) in enumerate(q_pieces):
            copies.append((PIECES[kind](inputs[n], h, per_dev * block_rows), q_scr.at[h, i], sems.at[h, i]))
        for i, (n, kind) in enumerate(kv_pieces):
            copies.append((PIECES[kind](inputs[n], h, per_dev * block_rows), kv_scr.at[h, i], sems.at[h, n_q + i]))
    copies = [pltpu.make_async_copy(*copy) for copy in copies]
    for copy in copies:
        copy.start()
    s1[...] = jnp.zeros_like(s1)
    p0[...] = jnp.zeros_like(p0)
    d0[...] = jnp.zeros_like(d0)
    d1[...] = jnp.zeros_like(d1)
    acc_scr[...] = jnp.zeros_like(acc_scr)
    top_scr[...] = jnp.zeros_like(top_scr)
    sum_scr[...] = jnp.ones_like(sum_scr)
    if own:
        bias_scr = refs[14]
        key_pos = lax.broadcasted_iota(jnp.int32, (block_rows, block_rows), 0)
        query_pos = lax.broadcasted_iota(jnp.int32, (block_rows, block_rows), 1)
        bias_scr[0] = jnp.zeros((block_rows, block_rows), jnp.float32)
        bias_scr[1] = jnp.where(key_pos <= query_pos, 0.0, -1e30)
    for copy in copies:
        copy.wait()

    def rows_of(i):
        return pl.ds(pl.multiple_of((i % per_dev) * block_rows, block_rows), block_rows)

    def step(h, at, now, acc, top, total):
        before = 1 - now
        for u in range(UNROLL):
            slot, _, out, _, _ = unit_fields(plan[at + u])
            vt = kv_scr[h, slot // per_dev, 1, rows_of(slot), :]
            vt = jnp.concatenate([vt[:HD], vt[HD:]], axis=1)
            mixed = jnp.dot(vt, p_scr[now][u], preferred_element_type=jnp.float32)
            acc = acc * decay_scr[now][u, 0:1, :] + mixed
            o_scr[out] = (acc * decay_scr[now][u, 1:2, :]).astype(o_scr.dtype)
        for u in range(UNROLL):
            _, _, out, first, _ = unit_fields(plan[at + UNROLL + u])
            s = s_scr[before][u]
            old = jnp.where(first == 1, -1e30, top)
            top = jnp.maximum(old, decay_scr[before][u, 2:3, :])
            decay = jnp.exp2((old - top) * EXP_SCALE)
            p = jnp.exp2((s - top) * EXP_SCALE)
            total = total * decay + jnp.sum(p, axis=0, keepdims=True)
            p_scr[before][u] = p.astype(jnp.bfloat16)
            decay_scr[before][u, 0:1, :] = decay
            decay_scr[before][u, 1:2, :] = 1.0 / total
            lse_scr[pl.ds(out, 1), :] = top * EXP_SCALE + jnp.log(total) * LOG2E
        for u in range(UNROLL):
            slot, span, _, _, diagonal = unit_fields(plan[at + 2 * UNROLL + u])
            k = kv_scr[h, slot // per_dev, 0, rows_of(slot), :]
            q = q_scr[h, span // per_dev, rows_of(span), :]
            s = lax.dot_general(k, q, (((1,), (1,)), ((), ())), preferred_element_type=jnp.float32)
            if own:
                s = s + bias_scr[diagonal]
            s_scr[now][u] = s
            decay_scr[now][u, 2:3, :] = jnp.max(s, axis=0, keepdims=True)
        return acc, top, total

    for h in range(heads):
        o_scr[...] = jnp.zeros_like(o_scr)
        lse_scr[...] = jnp.full_like(lse_scr, -1e30)

        def two_steps(i, carry):
            state = (acc_scr[...], top_scr[...], sum_scr[...])
            state = step(h, 1 + 2 * i * UNROLL, 0, *state)
            state = step(h, 1 + (2 * i + 1) * UNROLL, 1, *state)
            acc_scr[...], top_scr[...], sum_scr[...] = state
            return carry

        lax.fori_loop(0, (plan[0] + 1) // 2, two_steps, 0)
        if own:
            kept = outs[0].shape[1]
            outs[0][h] = o_scr[:kept]
            outs[1][h] = lse_scr[:kept, :]
        for out, (start, stop) in zip(outs[2 if own else 0 :], groups):
            n = stop - start
            for span in range(n):
                out[h, span * HD : (span + 1) * HD, :] = o_scr[start + span].astype(jnp.bfloat16)
            lse = lse_scr[start:stop, :]
            high = lse.astype(jnp.bfloat16).astype(jnp.float32)
            middle = (lse - high).astype(jnp.bfloat16).astype(jnp.float32)
            rest = jnp.zeros((lse_rows(n) - 3 * n, block_rows), jnp.float32)
            parts = jnp.concatenate([high, middle, lse - high - middle, rest], axis=0)
            out[h, n * HD :, :] = parts.astype(jnp.bfloat16)


def lse_rows(spans):
    return -(-3 * spans // 16) * 16


def unpacked_lse(ref, h, spans):
    parts = ref[h, spans * HD :, :].astype(jnp.float32)
    return parts[:spans] + parts[spans : 2 * spans] + parts[2 * spans : 3 * spans]


def cost(name):
    us = COSTS[name]
    return pl.CostEstimate(flops=int(us * 1e9) + 1, bytes_accessed=int(us * 3.4e6) + 1, transcendentals=0)


def ordered(kernel, n_after):
    def body(*refs):
        kernel(*refs[n_after:])

    return body


def attention_call(plan, q_pieces, kv_pieces, own, direct, heads, per_dev, block_rows, after=()):
    inputs = []

    def numbered(pieces):
        out = []
        for array, kind in pieces:
            if not any(array is known for known in inputs):
                inputs.append(array)
            out.append(([array is known for known in inputs].index(True), kind))
        return out

    q_pieces, kv_pieces = numbered(q_pieces), numbered(kv_pieces)
    n_q, n_kv = len(q_pieces), len(kv_pieces)
    spans = n_q * per_dev
    vmem, hbm = pl.BlockSpec(memory_space=pltpu.VMEM), pl.BlockSpec(memory_space=pltpu.HBM)
    f32, bf16 = jnp.float32, jnp.bfloat16
    if own:
        kept = per_dev if direct else spans
        groups = ((per_dev, spans),) if direct else ()
        out_shape = [
            jax.ShapeDtypeStruct((heads, kept, HD, block_rows), f32),
            jax.ShapeDtypeStruct((heads, kept, block_rows), f32),
        ]
    else:
        size = per_dev if direct else 2 * per_dev
        groups = tuple((start, start + size) for start in range(0, spans, size))
        out_shape = []
    for start, stop in groups:
        packed_rows = (stop - start) * HD + lse_rows(stop - start)
        out_shape.append(jax.ShapeDtypeStruct((heads, packed_rows, block_rows), bf16))
    scratch = [
        pltpu.VMEM((heads, n_q, per_dev * block_rows, HD), bf16),
        pltpu.VMEM((heads, n_kv, 2, per_dev * block_rows, HD), bf16),
        pltpu.VMEM((UNROLL, block_rows, block_rows), f32),
        pltpu.VMEM((UNROLL, block_rows, block_rows), f32),
        pltpu.VMEM((UNROLL, block_rows, block_rows), bf16),
        pltpu.VMEM((UNROLL, block_rows, block_rows), bf16),
        pltpu.VMEM((UNROLL, 8, block_rows), f32),
        pltpu.VMEM((UNROLL, 8, block_rows), f32),
        pltpu.VMEM((HD, block_rows), f32),
        pltpu.VMEM((1, block_rows), f32),
        pltpu.VMEM((1, block_rows), f32),
        pltpu.VMEM((spans + 1, HD, block_rows), f32 if own else bf16),
        pltpu.VMEM((spans + 8, block_rows), f32),
        pltpu.SemaphoreType.DMA((heads, n_q + n_kv)),
    ]
    if own:
        scratch.append(pltpu.VMEM((2, block_rows, block_rows), f32))
    return pl.pallas_call(
        ordered(
            partial(
                attention_kernel,
                (heads, per_dev, block_rows),
                own,
                groups,
                q_pieces,
                kv_pieces,
                len(inputs),
            ),
            len(after),
        ),
        out_shape=out_shape,
        in_specs=[hbm] * len(after) + [pl.BlockSpec(memory_space=pltpu.SMEM)] + [hbm] * len(inputs),
        out_specs=[vmem] * len(out_shape),
        scratch_shapes=scratch,
        compiler_params=pltpu.CompilerParams(vmem_limit_bytes=VMEM_LIMIT),
        cost_estimate=cost("own" if own else "served"),
        name="own_attention" if own else "served_attention",
    )(*after, plan, *inputs)


def pack_kernel(shape, place, q_ref, k_ref, v_ref, *refs):
    heads, first, half, rows, split, scatter = shape
    outs, (scr, t_scr, sems) = refs[:-3], refs[-3:]
    loads, stores = {}, []
    places = [(side, h) for h in range(heads) for side in (1, 0)]
    for side, h in places:
        start = pl.multiple_of((place[side] * half + first + h) * HD, HD)
        for i, ref in enumerate((q_ref, k_ref, v_ref)):
            loads[side, h, i] = pltpu.make_async_copy(
                ref.at[:, pl.ds(start, HD)], scr.at[side, h, i], sems.at[0, side, h, i]
            )
            loads[side, h, i].start()

    if scatter:
        for h in range(heads):
            t_scr[0, h] = jnp.zeros_like(t_scr[0, h])
            for i in range(3):
                blank = pltpu.make_async_copy(
                    t_scr.at[0, h], outs[-heads + h].at[place[0], i], sems.at[2, 0, h, i]
                )
                blank.start()
                blank.wait()

    def store(side, h, i, source):
        if side:
            target = outs[-heads + h].at[place[1] if scatter else 0, i]
        elif split:
            target = outs[1].at[h, i - 1] if i else outs[0].at[h]
        else:
            target = outs[0].at[h, i]
        copy = pltpu.make_async_copy(source, target, sems.at[1, side, h, i])
        copy.start()
        stores.append(copy)

    for side, h in places:
        for i in range(2):
            loads[side, h, i].wait()
            store(side, h, i, scr.at[side, h, i])
        loads[side, h, 2].wait()
        for tile in range(rows // HD):
            at = slice(tile * HD, (tile + 1) * HD)
            t_scr[side, h, at, :] = scr[side, h, 2, at, :].T
        store(side, h, 2, t_scr.at[side, h])
    for copy in stores:
        copy.wait()


def pack_call(place, queries, keys, values, heads, first, half, split, scatter, after=()):
    rows = queries.shape[0]
    hbm = pl.BlockSpec(memory_space=pltpu.HBM)
    bf16 = jnp.bfloat16
    queries, keys, values = (
        pltpu.with_memory_space_constraint(array, pltpu.HBM) for array in (queries, keys, values)
    )
    if split:
        outs = [
            jax.ShapeDtypeStruct((heads, rows, HD), bf16),
            jax.ShapeDtypeStruct((heads, 2, rows, HD), bf16),
        ]
    else:
        outs = [jax.ShapeDtypeStruct((heads, 3, rows, HD), bf16)]
    outs += [jax.ShapeDtypeStruct((2 if scatter else 1, 3, rows, HD), bf16)] * heads
    return pl.pallas_call(
        ordered(partial(pack_kernel, (heads, first, half, rows, split, scatter)), len(after)),
        out_shape=outs,
        in_specs=[hbm] * len(after) + [pl.BlockSpec(memory_space=pltpu.SMEM)] + [hbm] * 3,
        out_specs=[hbm] * len(outs),
        scratch_shapes=[
            pltpu.VMEM((2, heads, 3, rows, HD), bf16),
            pltpu.VMEM((2, heads, rows, HD), bf16),
            pltpu.SemaphoreType.DMA((3, 2, heads, 3)),
        ],
        compiler_params=pltpu.CompilerParams(vmem_limit_bytes=VMEM_LIMIT),
        cost_estimate=cost("pack"),
        name="pack",
    )(*after, place, queries, keys, values)


def cut_kernel(rows, note_ref, ref, q_ref, kv_ref, scr, note_scr, sems):
    loads = [
        pltpu.make_async_copy(ref, scr, sems.at[0]),
        pltpu.make_async_copy(note_ref, note_scr, sems.at[1]),
    ]
    for load in loads:
        load.start()
    for load in loads:
        load.wait()
    stores = [
        pltpu.make_async_copy(scr.at[0, 0], q_ref.at[0, pl.ds(0, rows)], sems.at[2]),
        pltpu.make_async_copy(note_scr, q_ref.at[0, pl.ds(rows, NOTE_ROWS)], sems.at[3]),
        pltpu.make_async_copy(scr.at[0, pl.ds(1, 2)], kv_ref.at[0], sems.at[4]),
    ]
    for store in stores:
        store.start()
    for store in stores:
        store.wait()


def cut_call(packed, note, after=()):
    _, _, rows, _ = packed.shape
    hbm = pl.BlockSpec(memory_space=pltpu.HBM)
    return pl.pallas_call(
        ordered(partial(cut_kernel, rows), len(after)),
        out_shape=(
            jax.ShapeDtypeStruct((1, rows + NOTE_ROWS, HD), jnp.bfloat16),
            jax.ShapeDtypeStruct((1, 2, rows, HD), jnp.bfloat16),
        ),
        in_specs=[hbm] * (len(after) + 2),
        out_specs=(hbm, hbm),
        scratch_shapes=[
            pltpu.VMEM(packed.shape, jnp.bfloat16),
            pltpu.VMEM((NOTE_ROWS, HD), jnp.bfloat16),
            pltpu.SemaphoreType.DMA((5,)),
        ],
        compiler_params=pltpu.CompilerParams(vmem_limit_bytes=VMEM_LIMIT),
        cost_estimate=cost("join"),
        name="join",
    )(*after, note, packed)


def join_kernel(heads, keep_ref, swap_ref, q_ref, kv_ref, scr, sems):
    loads, stores = [], []
    for side, ref in enumerate((keep_ref, swap_ref)):
        for h in range(heads):
            loads.append(pltpu.make_async_copy(ref.at[h], scr.at[side, h], sems.at[0, side, h]))
            stores.append(
                (
                    pltpu.make_async_copy(scr.at[side, h, 0], q_ref.at[side, h], sems.at[1, side, h]),
                    pltpu.make_async_copy(
                        scr.at[side, h, pl.ds(1, 2)], kv_ref.at[side, h], sems.at[2, side, h]
                    ),
                )
            )
    for load in loads:
        load.start()
    for load, pair in zip(loads, stores):
        load.wait()
        for store in pair:
            store.start()
    for pair in stores:
        for store in pair:
            store.wait()


def join_call(keep, swapped, after=()):
    heads, _, rows, _ = keep.shape
    hbm = pl.BlockSpec(memory_space=pltpu.HBM)
    return pl.pallas_call(
        ordered(partial(join_kernel, heads), len(after)),
        out_shape=(
            jax.ShapeDtypeStruct((2, heads, rows, HD), jnp.bfloat16),
            jax.ShapeDtypeStruct((2, heads, 2, rows, HD), jnp.bfloat16),
        ),
        in_specs=[hbm] * (len(after) + 2),
        out_specs=(hbm, hbm),
        scratch_shapes=[
            pltpu.VMEM((2, heads, 3, rows, HD), jnp.bfloat16),
            pltpu.SemaphoreType.DMA((3, 2, heads)),
        ],
        compiler_params=pltpu.CompilerParams(vmem_limit_bytes=VMEM_LIMIT),
        cost_estimate=cost("join"),
        name="join",
    )(*after, keep, swapped)


def merge_kernel(per_dev, block_rows, sizes, valid, sofar_ref, *refs):
    inputs, (keep_ref, send_ref, squares_ref) = refs[:-3], refs[-3:]
    spans = 2 * per_dev
    squares_ref[...] = sofar_ref[...]
    at = 0
    for c, size in enumerate(sizes):
        own_ref, own_lse_ref, near_ref, far_ref = inputs[4 * c : 4 * c + 4]
        for h in range(size):
            lses = [own_lse_ref[h]]
            for i, ref in enumerate((near_ref, far_ref)):
                lses.append(jnp.where(valid[i] > 0, unpacked_lse(ref, h, spans), -1e30))
            top = jnp.maximum(jnp.maximum(lses[0], lses[1]), lses[2])
            weights = [jnp.exp2(lse - top) for lse in lses]
            scale = 1.0 / (weights[0] + weights[1] + weights[2])
            weights = [weight * scale for weight in weights]
            for span in range(spans):
                rows = slice(span, span + 1)
                tile = slice(span * HD, (span + 1) * HD)
                mixed = weights[0][rows, :] * own_ref[h, span]
                mixed = mixed + weights[1][rows, :] * near_ref[h, tile, :].astype(jnp.float32)
                mixed = mixed + weights[2][rows, :] * far_ref[h, tile, :].astype(jnp.float32)
                squares_ref[rows, :] = squares_ref[rows, :] + jnp.sum(mixed * mixed, axis=0, keepdims=True)
                target = keep_ref if span < per_dev else send_ref
                start = (span % per_dev) * block_rows
                target[at, start : start + block_rows, :] = mixed.T.astype(target.dtype)
            at += 1


def merge_call(valid, sofar, parts, per_dev, after=()):
    block_rows = sofar.shape[1]
    sizes = [own[0].shape[0] for own, _, _ in parts]
    arrays = [array for own, near, far in parts for array in (*own, near, far)]
    vmem = pl.BlockSpec(memory_space=pltpu.VMEM)
    hbm = pl.BlockSpec(memory_space=pltpu.HBM)
    packed = jax.ShapeDtypeStruct((sum(sizes), per_dev * block_rows, HD), jnp.bfloat16)
    return pl.pallas_call(
        ordered(partial(merge_kernel, per_dev, block_rows, sizes), len(after)),
        out_shape=(packed, packed, jax.ShapeDtypeStruct(sofar.shape, jnp.float32)),
        in_specs=[hbm] * len(after)
        + [pl.BlockSpec(memory_space=pltpu.SMEM)]
        + [vmem] * (1 + len(arrays)),
        out_specs=(vmem, vmem, vmem),
        compiler_params=pltpu.CompilerParams(vmem_limit_bytes=VMEM_LIMIT),
        cost_estimate=cost("merge"),
        name="merge",
    )(*after, valid, sofar, *arrays)


def own_merge_kernel(per_dev, block_rows, valid, sofar_ref, squares_in_ref, own_ref, own_lse_ref, *refs):
    other_ref, packs, outs, squares_ref = refs[0], refs[1:5], refs[5:7], refs[7]
    squares_ref[...] = sofar_ref[:per_dev, :] + squares_in_ref[...]
    for side in range(2):
        arrivals = (packs[side], packs[2 + side])
        lses = [unpacked_lse(other_ref, 0, per_dev) if side else own_lse_ref[0]]
        for i, ref in enumerate(arrivals):
            lses.append(jnp.where(valid[i] > 0, unpacked_lse(ref, 0, per_dev), -1e30))
        top = jnp.maximum(jnp.maximum(lses[0], lses[1]), lses[2])
        weights = [jnp.exp2(lse - top) for lse in lses]
        scale = 1.0 / (weights[0] + weights[1] + weights[2])
        weights = [weight * scale for weight in weights]
        for span in range(per_dev):
            rows = slice(span, span + 1)
            tile = slice(span * HD, (span + 1) * HD)
            mixed = other_ref[0, tile, :].astype(jnp.float32) if side else own_ref[0, span]
            mixed = weights[0][rows, :] * mixed
            for weight, ref in zip(weights[1:], arrivals):
                mixed = mixed + weight[rows, :] * ref[0, tile, :].astype(jnp.float32)
            squares_ref[rows, :] = squares_ref[rows, :] + jnp.sum(mixed * mixed, axis=0, keepdims=True)
            at = slice(span * block_rows, (span + 1) * block_rows)
            outs[side][0, at, :] = mixed.T.astype(jnp.bfloat16)


def own_merge_call(valid, sofar, squares_in, own, other, packs, per_dev, after=()):
    block_rows = sofar.shape[1]
    vmem = pl.BlockSpec(memory_space=pltpu.VMEM)
    hbm = pl.BlockSpec(memory_space=pltpu.HBM)
    packed = jax.ShapeDtypeStruct((1, per_dev * block_rows, HD), jnp.bfloat16)
    return pl.pallas_call(
        ordered(partial(own_merge_kernel, per_dev, block_rows), len(after)),
        out_shape=(packed, packed, jax.ShapeDtypeStruct((per_dev, block_rows), jnp.float32)),
        in_specs=[hbm] * len(after) + [pl.BlockSpec(memory_space=pltpu.SMEM)] + [vmem] * 9,
        out_specs=(vmem, vmem, vmem),
        compiler_params=pltpu.CompilerParams(vmem_limit_bytes=VMEM_LIMIT),
        cost_estimate=cost("merge"),
        name="merge",
    )(*after, valid, sofar, squares_in, *own, other, *packs)


def finish_kernel(per_dev, sizes, place, *refs):
    n = len(sizes)
    kept, returned = refs[:n], refs[n : 2 * n]
    squares_ref, gain_ref, out_ref = refs[2 * n :]
    block_rows = squares_ref.shape[1]
    half = sum(sizes)
    factor = lax.rsqrt(squares_ref[...] / (HEADS * HD) + 1e-06)
    for b in range(per_dev):
        column = jnp.broadcast_to(factor[b : b + 1, :], (HD, block_rows)).T
        rows = slice(b * block_rows, (b + 1) * block_rows)
        for side, pieces in enumerate((kept, returned)):
            head = 0
            for piece, size in zip(pieces, sizes):
                for h in range(size):
                    start = pl.multiple_of((place[side] * half + head) * HD, HD)
                    gain = gain_ref[:, pl.ds(start, HD)].astype(jnp.float32)
                    value = piece[h, rows, :].astype(jnp.float32) * column * gain
                    out_ref[rows, pl.ds(start, HD)] = value.astype(out_ref.dtype)
                    head += 1


def finish_call(place, kept, returned, squares, gain, per_dev):
    vmem = pl.BlockSpec(memory_space=pltpu.VMEM)
    rows, width = kept[0].shape[1], gain.shape[0]
    return pl.pallas_call(
        partial(finish_kernel, per_dev, [k.shape[0] for k in kept]),
        out_shape=jax.ShapeDtypeStruct((rows, width), jnp.bfloat16),
        in_specs=[pl.BlockSpec(memory_space=pltpu.SMEM)] + [vmem] * (2 * len(kept) + 2),
        out_specs=vmem,
        compiler_params=pltpu.CompilerParams(vmem_limit_bytes=VMEM_LIMIT),
        cost_estimate=cost("finish"),
        name="finish",
    )(place, *kept, *returned, squares, gain.reshape(1, width))


def plan_of(live, slot, diagonal, dump):
    spans, entries = live.shape
    t = jnp.arange(entries)
    earlier = jnp.sum((t[None, None, :] < t[None, :, None]) & live[:, None, :], axis=2)
    span = lax.broadcasted_iota(jnp.int32, live.shape, 0)
    code = unit_code(slot, span, span, (earlier == 0).astype(jnp.int32), diagonal)
    code, live = code.reshape(-1), live.reshape(-1)
    n = spans * entries
    i = jnp.arange(n)
    rank = jnp.sum((i[None, :] < i[:, None]) & live[None, :], axis=1)
    at = jnp.arange(n + 8 * UNROLL)
    hit = live[None, :] & (rank[None, :] + 2 * UNROLL == at[:, None])
    idle = unit_code(0, 0, dump, 1, 0)
    codes = jnp.sum(jnp.where(hit, code[None, :] - idle, 0), axis=1) + idle
    total = jnp.sum(live.astype(jnp.int32))
    steps = jnp.where(total > 0, (total + UNROLL - 1) // UNROLL + 2, 0)
    return jnp.concatenate([steps[None], codes]).astype(jnp.int32)


def level_shards(queries, keys, values, selection, norm_gain):
    device = lax.axis_index("ctx")
    level, x = device // 2, device % 2
    rows, width = queries.shape
    per_dev, topk = selection.shape
    block_rows = rows // per_dev
    spans = 2 * per_dev
    half = width // HD // 2

    sent = {}

    def to(array, pairs, name):
        with jax.named_scope(name):
            sent[name] = lax.ppermute(array, "ctx", pairs)
        return sent[name]

    def exchange(array, name):
        pairs = [[d, d + 1] for d in range(0, 8, 2)]
        with jax.named_scope(name):
            sent[name] = lax.psum_scatter(
                array, "ctx", scatter_dimension=0, axis_index_groups=pairs, tiled=True
            )
        return sent[name]

    swap = [(d, d ^ 1) for d in range(8)]
    lift = [(0, 2), (1, 3)]
    near_down, far_down = [(4, 2), (5, 3), (6, 4), (7, 5)], [(6, 2), (7, 3)]

    def crossed(pairs):
        return [(source, target ^ 1) for source, target in pairs]

    near_up, far_up = [(2, 4), (3, 5), (4, 6), (5, 7)], [(2, 6), (3, 7)]
    valid = jnp.stack([level >= 2, level >= 3]).astype(jnp.int32)
    place = jnp.stack([x, 1 - x]).astype(jnp.int32)

    own_selection = jnp.concatenate([selection, to(selection, swap, "selection_swap")], axis=0)
    note = jnp.zeros((NOTE_ROWS, HD), jnp.bfloat16)
    note = lax.dynamic_update_slice(note, own_selection.astype(jnp.bfloat16), (0, 0))

    def ids(at):
        first = jnp.stack([(at * 2 + x) * per_dev, (at * 2 + 1 - x) * per_dev])
        return (first[:, None] + jnp.arange(per_dev)[None, :]).reshape(-1, 1)

    def slots(blocks):
        owner = blocks // per_dev
        slot = jnp.where(owner // 2 == level, 0, spans) + jnp.where(owner % 2 == x, 0, per_dev)
        return owner // 2, slot + blocks % per_dev

    others = own_selection[:, 1:]
    block_level, slot = slots(others)
    live = (others != ids(level)) & ((block_level == level) | ((level == 1) & (block_level == 0)))
    first = jnp.ones((spans, 1), jnp.int32)
    own_plan = plan_of(
        jnp.concatenate([first > 0, live], axis=1),
        jnp.concatenate([jnp.arange(spans, dtype=jnp.int32)[:, None], slot], axis=1),
        jnp.concatenate([first, jnp.zeros_like(others)], axis=1),
        spans,
    )
    def served_lists(*noted):
        near_selection, far_selection = (
            array[0, rows : rows + spans, :topk].astype(jnp.int32) for array in noted
        )
        others = jnp.concatenate([near_selection, far_selection], axis=0)[:, 1:]
        block_level, slot = slots(others)
        is_near = lax.broadcasted_iota(jnp.int32, others.shape, 0) < spans
        mine = ((level == 1) & (block_level <= 1)) | ((level == 2) & (block_level == 2) & is_near)
        live = (others != jnp.concatenate([ids(level + 1), ids(level + 2)], axis=0)) & mine
        return plan_of(live, slot, jnp.zeros_like(others), 2 * spans)

    n, split, order = half, SPLIT, ORDER
    own_pieces, z_arrays, served_pieces, downs_of = {}, {}, {}, {}
    ups, owns, others, squares_in, kept, returned = {}, {}, {}, [], [], []
    squares = [jnp.zeros((spans, block_rows), jnp.float32)]
    last, served_plan = [], []

    def downs(q, kv, name):
        low = to(kv, lift, f"lift_{name}")
        far = to(q, far_down, f"far_down_{name}")
        return to(q, near_down, f"near_down_{name}"), far, low

    def pack(*chunks):
        c = chunks[0]
        packed = pack_call(
            place, queries, keys, values, len(chunks), c, half, split[c], SCATTER[c], last
        )
        last[:] = [packed[0]]
        if SCATTER[c]:
            swapped = [exchange(p, f"swap_c{d}") for d, p in zip(chunks, packed[-len(chunks) :])]
        else:
            swapped = [to(p, swap, f"swap_c{d}") for d, p in zip(chunks, packed[-len(chunks) :])]
        if split[c]:
            keeps = downs(packed[0], packed[1], f"keep_c{c}")
            for d, kind, swap_d in zip(chunks, ("head", "next head"), swapped):
                downs_of[d] = [(array, kind) for array in keeps]
                z_arrays[d] = (swap_d,)
                own_pieces[d] = (
                    [(packed[0], kind), (swap_d, "queries")],
                    [(packed[1], kind), (swap_d, "keys_values")],
                )
        else:
            z_arrays[c] = (packed[0], swapped[0])
            own_pieces[c] = (
                [(array, "queries") for array in z_arrays[c]],
                [(array, "keys_values") for array in z_arrays[c]],
            )

    def join(c):
        if split[c]:
            q_swap, kv_swap = cut_call(*z_arrays[c], note, last)
            last[:] = [q_swap]
            swaps = downs(q_swap, kv_swap, f"recv_c{c}")
            if not served_plan:
                served_plan.append(served_lists(*swaps[:2]))
            near, far, low = [
                [k, (r, kind)]
                for k, r, kind in zip(downs_of[c], swaps, ("top rows", "top rows", "head"))
            ]
        else:
            level_q, level_kv = join_call(*z_arrays[c], last)
            last[:] = [level_q]
            near, far, low = [
                [(array, "first"), (array, "second")] for array in downs(level_q, level_kv, f"c{c}")
            ]
        served_pieces[c] = (near + far, own_pieces[c][1] + low)

    def is_direct(c):
        return DIRECT and c == n - 1

    def serve(c):
        packs = attention_call(
            served_plan[0], *served_pieces[c], False, is_direct(c), 1, per_dev, block_rows, last
        )
        last[:] = [packs[0]]
        if is_direct(c):
            near_same, near_cross, far_same, far_cross = packs
            far = (
                to(far_same, far_up, f"far_up_same_c{c}"),
                to(far_cross, crossed(far_up), f"far_up_cross_c{c}"),
            )
            near = (
                to(near_same, near_up, f"near_up_same_c{c}"),
                to(near_cross, crossed(near_up), f"near_up_cross_c{c}"),
            )
            ups[c] = (*near, *far)
        else:
            near, far = packs
            far = to(far, far_up, f"far_up_c{c}")
            ups[c] = (to(near, near_up, f"near_up_c{c}"), far)

    def attend(c):
        state = attention_call(
            own_plan,
            own_pieces[c][0],
            served_pieces[c][1],
            True,
            is_direct(c),
            1,
            per_dev,
            block_rows,
            last,
        )
        last[:] = [state[1]]
        owns[c] = state[:2]
        if is_direct(c):
            others[c] = to(state[2], swap, f"back_own_c{c}")

    def merge(*chunks):
        if is_direct(chunks[0]):
            c = chunks[0]
            keep, back, squares[0] = own_merge_call(
                valid, squares[0], squares_in[0], owns[c], others[c], ups[c], per_dev, last
            )
            kept.append(keep)
            returned.append(back)
            return
        parts = [(owns[c], *ups[c]) for c in chunks]
        keep, send, squares[0] = merge_call(valid, squares[0], parts, per_dev, last)
        last[:] = [keep]
        kept.append(keep)
        returned.append(to(send, swap, f"back_c{chunks[0]}"))
        if DIRECT and chunks[-1] == n - 2:
            squares_in.append(to(squares[0][per_dev:], swap, "squares_swap"))

    steps = {"p": pack, "j": join, "s": serve, "a": attend, "m": merge}
    for what, *args in order:
        if what == "w":
            last.append(own_plan if args[0] == "plan" else sent[args[0]])
        else:
            steps[what](*args)
    square = squares[0]
    if not DIRECT:
        square = square[:per_dev] + to(square[per_dev:], swap, "squares_swap")
    n_head = lax.axis_size("head")
    hop = 1
    while hop < n_head:
        square = square + lax.ppermute(square, "head", [(i, i ^ hop) for i in range(n_head)])
        hop *= 2
    return finish_call(place, kept, returned, square, norm_gain, per_dev)


def solution(mesh):
    placed = (P("ctx", "head"), P("ctx", "head"), P("ctx", "head"), P("ctx", None), P("head"))
    body = level_shards if mesh.shape["ctx"] == 8 else shards
    return jax.shard_map(
        body, mesh=mesh, in_specs=placed, out_specs=P("ctx", "head"), check_vma=False
    )
```

```python
from functools import partial
import math

import jax
import jax.numpy as jnp
from jax import lax
from jax.experimental import pallas as pl
from jax.experimental.pallas import tpu as pltpu
from jax.sharding import PartitionSpec as P

HEADS = 32
HD = 128
CAP = 2
LOG2E = math.log2(math.e)
EXP_SCALE = HD ** (-0.5) * LOG2E


def partial_state(query_rows, key_block, value_block, causal):
    scores = jnp.einsum(
        "sqhd,skhd->shqk", query_rows, key_block, preferred_element_type=jnp.float32
    ) * query_rows.shape[3] ** (-0.5)
    if causal:
        query_pos = lax.broadcasted_iota(jnp.int32, scores.shape, 2)
        key_pos = lax.broadcasted_iota(jnp.int32, scores.shape, 3)
        scores = jnp.where(key_pos <= query_pos, scores, -1e30)
    row_peak = jnp.max(scores, axis=3)
    exponentials = jnp.exp(scores - row_peak[..., None])
    row_sum = jnp.sum(exponentials, axis=3)
    weights = exponentials.astype(jnp.bfloat16)
    blended = jnp.einsum(
        "shqk,skhd->sqhd", weights, value_block, preferred_element_type=jnp.float32
    )
    blended = blended / jnp.transpose(row_sum, (0, 2, 1))[..., None]
    return (blended, row_peak + jnp.log(row_sum))


def slot_plan(selected, first_span, per_dev, capacity):
    own_span = first_span + lax.broadcasted_iota(jnp.int32, selected.shape, 0)
    is_live = (selected != own_span).reshape(-1)
    owner_dev = (selected // per_dev).reshape(-1)
    pair_count = owner_dev.shape[0]
    is_later = lax.broadcasted_iota(jnp.int32, (pair_count, pair_count), 0) > lax.broadcasted_iota(
        jnp.int32, (pair_count, pair_count), 1
    )
    earlier = is_later & (owner_dev[:, None] == owner_dev[None, :]) & is_live[None, :]
    slot_rank = jnp.sum(earlier.astype(jnp.int32), axis=1)
    slot_index = jnp.where(is_live, owner_dev * capacity + slot_rank, 0)
    return (slot_index, is_live, (selected % per_dev).reshape(-1))


def shards(queries, keys, values, selection, norm_gain):
    n_ctx = lax.axis_size("ctx")
    device = lax.axis_index("ctx")
    rows, width = queries.shape
    per_dev, topk_count = selection.shape
    block_rows = rows // per_dev
    heads_dev = width // HD
    slot_count = n_ctx * CAP
    group_size = math.gcd(slot_count, 4)
    query_blocks = queries.reshape(per_dev, block_rows, heads_dev, HD)
    key_blocks = keys.reshape(per_dev, block_rows, heads_dev, HD)
    value_blocks = values.reshape(per_dev, block_rows, heads_dev, HD)
    slot_index, is_live, local_block = slot_plan(selection[:, 1:], device * per_dev, per_dev, CAP)
    pair_count = slot_index.shape[0]
    pair_span = lax.broadcasted_iota(jnp.int32, (pair_count,), 0) // (topk_count - 1)
    slot_ids = lax.broadcasted_iota(jnp.int32, (slot_count, pair_count), 0)
    placed = (slot_ids == slot_index[None, :]) & is_live[None, :]
    slot_span = jnp.sum(jnp.where(placed, pair_span[None, :], 0), axis=1)
    everyone = lax.all_gather(selection, "ctx", axis=0, tiled=True)
    requests = everyone[:, 1:].reshape(n_ctx, per_dev, topk_count - 1)
    first_spans = lax.broadcasted_iota(jnp.int32, (n_ctx,), 0) * per_dev
    all_slots, all_live, all_local = jax.vmap(partial(slot_plan, per_dev=per_dev, capacity=CAP))(
        requests, first_spans
    )
    owner_devs = requests.reshape(n_ctx, -1) // per_dev
    served = all_live & (owner_devs == device)
    capacity_ids = lax.broadcasted_iota(jnp.int32, (1, CAP, 1), 1)
    matched = served[:, None, :] & (all_slots[:, None, :] == device * CAP + capacity_ids)
    send_block = jnp.sum(jnp.where(matched, all_local[:, None, :], 0), axis=2)
    key_out = key_blocks[send_block].reshape(n_ctx, CAP, block_rows, width)
    value_out = value_blocks[send_block].reshape(n_ctx, CAP, block_rows, width)
    key_in, value_in = (
        lax.all_to_all(key_out, "ctx", split_axis=0, concat_axis=0, tiled=True),
        lax.all_to_all(value_out, "ctx", split_axis=0, concat_axis=0, tiled=True),
    )

    def one_group(packed):
        group_keys, group_values, group_span = packed
        blended, log_sums = partial_state(query_blocks[group_span], group_keys, group_values, False)
        return (blended.astype(jnp.bfloat16), log_sums)

    slot_out, slot_lse = lax.map(
        one_group,
        (
            key_in.reshape(-1, group_size, block_rows, heads_dev, HD),
            value_in.reshape(-1, group_size, block_rows, heads_dev, HD),
            slot_span.reshape(-1, group_size),
        ),
    )
    slot_out = slot_out.reshape(slot_count, block_rows, heads_dev, HD)
    slot_lse = slot_lse.reshape(slot_count, heads_dev, block_rows)
    own_out, own_lse = partial_state(query_blocks, key_blocks, value_blocks, True)
    live_pairs = is_live.reshape(per_dev, topk_count - 1)
    pair_out = (
        slot_out[slot_index]
        .reshape(per_dev, topk_count - 1, block_rows, heads_dev, HD)
        .astype(jnp.float32)
    )
    pair_lse = jnp.where(
        live_pairs[:, :, None, None],
        slot_lse[slot_index].reshape(per_dev, topk_count - 1, heads_dev, block_rows),
        -1e30,
    )
    highest = jnp.maximum(own_lse, jnp.max(pair_lse, axis=1))
    own_weight = jnp.exp(own_lse - highest)
    pair_weight = jnp.where(live_pairs[:, :, None, None], jnp.exp(pair_lse - highest[:, None]), 0.0)
    numerator = jnp.transpose(own_weight, (0, 2, 1))[..., None] * own_out
    numerator = numerator + jnp.sum(
        jnp.transpose(pair_weight, (0, 1, 3, 2))[..., None] * pair_out, axis=1
    )
    denominator = own_weight + jnp.sum(pair_weight, axis=1)
    attended = (numerator / jnp.transpose(denominator, (0, 2, 1))[..., None]).reshape(rows, width)
    squares = jnp.sum(attended * attended, axis=1)
    summed = lax.psum(squares, "head")
    factor = lax.rsqrt(summed / (HEADS * HD) + 1e-06)
    return (attended * factor[:, None] * norm_gain.astype(jnp.float32)[None, :]).astype(
        jnp.bfloat16
    )


SPLIT = (True, False, False, False)
SCATTER = (False, False, False, False)
ORDER = (
    ("p", 0),
    ("w", "plan"),
    ("p", 1),
    ("w", "near_down_keep_c0"),
    ("w", "far_down_keep_c0"),
    ("w", "lift_keep_c0"),
    ("w", "served"),
    ("j", 0),
    ("p", 2),
    ("j", 1),
    ("s", 0),
    ("j", 2),
    ("a", 0),
    ("p", 3),
    ("s", 1),
    ("m", 0),
    ("a", 1),
    ("j", 3),
    ("s", 2),
    ("m", 1),
    ("a", 2),
    ("w", "back_c0"),
    ("s", 3),
    ("a", 3),
    ("m", 2),
    ("m", 3),
)
COSTS = {"pack": 2, "join": 1, "served": 6, "own": 5, "merge": 1, "finish": 3}
DIRECT = True
NOTE_ROWS = 16
UNROLL = 2
VMEM_LIMIT = 10 * 1024 * 1024


def unit_fields(code):
    return code & 31, (code >> 5) & 31, (code >> 10) & 63, (code >> 16) & 1, (code >> 17) & 1


def unit_code(slot, span, out, first, diagonal):
    return slot + span * 32 + out * 1024 + first * 65536 + diagonal * 131072


PIECES = {
    "head": lambda ref, h, rows: ref.at[h],
    "top rows": lambda ref, h, rows: ref.at[h, pl.ds(0, rows)],
    "queries": lambda ref, h, rows: ref.at[h, 0],
    "keys_values": lambda ref, h, rows: ref.at[h, pl.ds(1, 2)],
    "first": lambda ref, h, rows: ref.at[0, h],
    "second": lambda ref, h, rows: ref.at[1, h],
}


def attention_kernel(shape, own, groups, q_pieces, kv_pieces, n_in, plan, *refs):
    heads, per_dev, block_rows = shape
    n_q, n_kv = len(q_pieces), len(kv_pieces)
    inputs, refs = refs[:n_in], refs[n_in:]
    n_out = len(groups) + 2 * own
    outs, refs = refs[:n_out], refs[n_out:]
    (q_scr, kv_scr, s0, s1, p0, p1, d0, d1, acc_scr, top_scr, sum_scr, o_scr, lse_scr, sems) = refs[:14]
    s_scr, p_scr, decay_scr = (s0, s1), (p0, p1), (d0, d1)
    spans = n_q * per_dev
    copies = []
    for h in range(heads):
        for i, (n, kind) in enumerate(q_pieces):
            copies.append((PIECES[kind](inputs[n], h, per_dev * block_rows), q_scr.at[h, i], sems.at[h, i]))
        for i, (n, kind) in enumerate(kv_pieces):
            copies.append((PIECES[kind](inputs[n], h, per_dev * block_rows), kv_scr.at[h, i], sems.at[h, n_q + i]))
    copies = [pltpu.make_async_copy(*copy) for copy in copies]
    for copy in copies:
        copy.start()
    s1[...] = jnp.zeros_like(s1)
    p0[...] = jnp.zeros_like(p0)
    d0[...] = jnp.zeros_like(d0)
    d1[...] = jnp.zeros_like(d1)
    acc_scr[...] = jnp.zeros_like(acc_scr)
    top_scr[...] = jnp.zeros_like(top_scr)
    sum_scr[...] = jnp.ones_like(sum_scr)
    if own:
        bias_scr = refs[14]
        key_pos = lax.broadcasted_iota(jnp.int32, (block_rows, block_rows), 0)
        query_pos = lax.broadcasted_iota(jnp.int32, (block_rows, block_rows), 1)
        bias_scr[0] = jnp.zeros((block_rows, block_rows), jnp.float32)
        bias_scr[1] = jnp.where(key_pos <= query_pos, 0.0, -1e30)
    for copy in copies:
        copy.wait()

    def rows_of(i):
        return pl.ds(pl.multiple_of((i % per_dev) * block_rows, block_rows), block_rows)

    def step(h, at, now, acc, top, total):
        before = 1 - now
        for u in range(UNROLL):
            slot, _, out, _, _ = unit_fields(plan[at + u])
            vt = kv_scr[h, slot // per_dev, 1, rows_of(slot), :]
            vt = jnp.concatenate([vt[:HD], vt[HD:]], axis=1)
            mixed = jnp.dot(vt, p_scr[now][u], preferred_element_type=jnp.float32)
            acc = acc * decay_scr[now][u, 0:1, :] + mixed
            o_scr[out] = (acc * decay_scr[now][u, 1:2, :]).astype(o_scr.dtype)
        for u in range(UNROLL):
            _, _, out, first, _ = unit_fields(plan[at + UNROLL + u])
            s = s_scr[before][u]
            old = jnp.where(first == 1, -1e30, top)
            top = jnp.maximum(old, decay_scr[before][u, 2:3, :])
            decay = jnp.exp2((old - top) * EXP_SCALE)
            p = jnp.exp2((s - top) * EXP_SCALE)
            total = total * decay + jnp.sum(p, axis=0, keepdims=True)
            p_scr[before][u] = p.astype(jnp.bfloat16)
            decay_scr[before][u, 0:1, :] = decay
            decay_scr[before][u, 1:2, :] = 1.0 / total
            lse_scr[pl.ds(out, 1), :] = top * EXP_SCALE + jnp.log(total) * LOG2E
        for u in range(UNROLL):
            slot, span, _, _, diagonal = unit_fields(plan[at + 2 * UNROLL + u])
            k = kv_scr[h, slot // per_dev, 0, rows_of(slot), :]
            q = q_scr[h, span // per_dev, rows_of(span), :]
            s = lax.dot_general(k, q, (((1,), (1,)), ((), ())), preferred_element_type=jnp.float32)
            if own:
                s = s + bias_scr[diagonal]
            s_scr[now][u] = s
            decay_scr[now][u, 2:3, :] = jnp.max(s, axis=0, keepdims=True)
        return acc, top, total

    for h in range(heads):
        o_scr[...] = jnp.zeros_like(o_scr)
        lse_scr[...] = jnp.full_like(lse_scr, -1e30)

        def two_steps(i, carry):
            state = (acc_scr[...], top_scr[...], sum_scr[...])
            state = step(h, 1 + 2 * i * UNROLL, 0, *state)
            state = step(h, 1 + (2 * i + 1) * UNROLL, 1, *state)
            acc_scr[...], top_scr[...], sum_scr[...] = state
            return carry

        lax.fori_loop(0, (plan[0] + 1) // 2, two_steps, 0)
        if own:
            kept = outs[0].shape[1]
            outs[0][h] = o_scr[:kept]
            outs[1][h] = lse_scr[:kept, :]
        for out, (start, stop) in zip(outs[2 if own else 0 :], groups):
            n = stop - start
            for span in range(n):
                out[h, span * HD : (span + 1) * HD, :] = o_scr[start + span].astype(jnp.bfloat16)
            lse = lse_scr[start:stop, :]
            high = lse.astype(jnp.bfloat16).astype(jnp.float32)
            middle = (lse - high).astype(jnp.bfloat16).astype(jnp.float32)
            rest = jnp.zeros((lse_rows(n) - 3 * n, block_rows), jnp.float32)
            parts = jnp.concatenate([high, middle, lse - high - middle, rest], axis=0)
            out[h, n * HD :, :] = parts.astype(jnp.bfloat16)


def lse_rows(spans):
    return -(-3 * spans // 16) * 16


def unpacked_lse(ref, h, spans):
    parts = ref[h, spans * HD :, :].astype(jnp.float32)
    return parts[:spans] + parts[spans : 2 * spans] + parts[2 * spans : 3 * spans]


def cost(name):
    us = COSTS[name]
    return pl.CostEstimate(flops=int(us * 1e9) + 1, bytes_accessed=int(us * 3.4e6) + 1, transcendentals=0)


def ordered(kernel, n_after):
    def body(*refs):
        kernel(*refs[n_after:])

    return body


def attention_call(plan, q_pieces, kv_pieces, own, direct, heads, per_dev, block_rows, after=()):
    inputs = []

    def numbered(pieces):
        out = []
        for array, kind in pieces:
            if not any(array is known for known in inputs):
                inputs.append(array)
            out.append(([array is known for known in inputs].index(True), kind))
        return out

    q_pieces, kv_pieces = numbered(q_pieces), numbered(kv_pieces)
    n_q, n_kv = len(q_pieces), len(kv_pieces)
    spans = n_q * per_dev
    vmem, hbm = pl.BlockSpec(memory_space=pltpu.VMEM), pl.BlockSpec(memory_space=pltpu.HBM)
    f32, bf16 = jnp.float32, jnp.bfloat16
    if own:
        kept = per_dev if direct else spans
        groups = ((per_dev, spans),) if direct else ()
        out_shape = [
            jax.ShapeDtypeStruct((heads, kept, HD, block_rows), f32),
            jax.ShapeDtypeStruct((heads, kept, block_rows), f32),
        ]
    else:
        size = per_dev if direct else 2 * per_dev
        groups = tuple((start, start + size) for start in range(0, spans, size))
        out_shape = []
    for start, stop in groups:
        packed_rows = (stop - start) * HD + lse_rows(stop - start)
        out_shape.append(jax.ShapeDtypeStruct((heads, packed_rows, block_rows), bf16))
    scratch = [
        pltpu.VMEM((heads, n_q, per_dev * block_rows, HD), bf16),
        pltpu.VMEM((heads, n_kv, 2, per_dev * block_rows, HD), bf16),
        pltpu.VMEM((UNROLL, block_rows, block_rows), f32),
        pltpu.VMEM((UNROLL, block_rows, block_rows), f32),
        pltpu.VMEM((UNROLL, block_rows, block_rows), bf16),
        pltpu.VMEM((UNROLL, block_rows, block_rows), bf16),
        pltpu.VMEM((UNROLL, 8, block_rows), f32),
        pltpu.VMEM((UNROLL, 8, block_rows), f32),
        pltpu.VMEM((HD, block_rows), f32),
        pltpu.VMEM((1, block_rows), f32),
        pltpu.VMEM((1, block_rows), f32),
        pltpu.VMEM((spans + 1, HD, block_rows), f32 if own else bf16),
        pltpu.VMEM((spans + 8, block_rows), f32),
        pltpu.SemaphoreType.DMA((heads, n_q + n_kv)),
    ]
    if own:
        scratch.append(pltpu.VMEM((2, block_rows, block_rows), f32))
    return pl.pallas_call(
        ordered(
            partial(
                attention_kernel,
                (heads, per_dev, block_rows),
                own,
                groups,
                q_pieces,
                kv_pieces,
                len(inputs),
            ),
            len(after),
        ),
        out_shape=out_shape,
        in_specs=[hbm] * len(after) + [pl.BlockSpec(memory_space=pltpu.SMEM)] + [hbm] * len(inputs),
        out_specs=[vmem] * len(out_shape),
        scratch_shapes=scratch,
        compiler_params=pltpu.CompilerParams(vmem_limit_bytes=VMEM_LIMIT),
        cost_estimate=cost("own" if own else "served"),
        name="own_attention" if own else "served_attention",
    )(*after, plan, *inputs)


def pack_kernel(shape, place, q_ref, k_ref, v_ref, *refs):
    sides, head, half, rows, noted = shape
    n_out = len(sides) + noted
    note_ref, refs = (refs[0], refs[1:]) if noted else (None, refs)
    outs, (scr, t_scr, note_scr, sems) = refs[:n_out], refs[n_out:]
    loads, stores = {}, []
    for side in sides:
        start = pl.multiple_of((place[side] * half + head) * HD, HD)
        for i, ref in enumerate((q_ref, k_ref, v_ref)):
            loads[side, i] = pltpu.make_async_copy(
                ref.at[:, pl.ds(start, HD)], scr.at[side, i], sems.at[0, side, i]
            )
            loads[side, i].start()

    def store(source, target, side, i):
        copy = pltpu.make_async_copy(source, target, sems.at[1, side, i])
        copy.start()
        stores.append(copy)

    if noted:
        load = pltpu.make_async_copy(note_ref, note_scr, sems.at[0, 0, 3])
        load.start()
        load.wait()
        store(note_scr, outs[0].at[0, pl.ds(rows, NOTE_ROWS)], 0, 3)
    for side, out in zip(sides, outs[noted:]):
        targets = [out.at[0, i] for i in range(3)]
        if noted:
            targets = [outs[0].at[0, pl.ds(0, rows)], out.at[0, 0], out.at[0, 1]]
        for i in range(2):
            loads[side, i].wait()
            store(scr.at[side, i], targets[i], side, i)
        loads[side, 2].wait()
        for tile in range(rows // HD):
            at = slice(tile * HD, (tile + 1) * HD)
            t_scr[side, at, :] = scr[side, 2, at, :].T
        store(t_scr.at[side], targets[2], side, 2)
    for copy in stores:
        copy.wait()


def pack_call(place, queries, keys, values, head, half, sides=(1, 0), note=None, after=()):
    rows = queries.shape[0]
    hbm = pl.BlockSpec(memory_space=pltpu.HBM)
    bf16 = jnp.bfloat16
    queries, keys, values = (
        pltpu.with_memory_space_constraint(array, pltpu.HBM) for array in (queries, keys, values)
    )
    noted = note is not None
    if noted:
        shapes, notes = [(1, rows + NOTE_ROWS, HD), (1, 2, rows, HD)], [note]
    else:
        shapes, notes = [(1, 3, rows, HD)] * len(sides), []
    return pl.pallas_call(
        ordered(partial(pack_kernel, (sides, head, half, rows, noted)), len(after)),
        out_shape=[jax.ShapeDtypeStruct(shape, bf16) for shape in shapes],
        in_specs=[hbm] * len(after) + [pl.BlockSpec(memory_space=pltpu.SMEM)] + [hbm] * (3 + noted),
        out_specs=[hbm] * len(shapes),
        scratch_shapes=[
            pltpu.VMEM((2, 3, rows, HD), bf16),
            pltpu.VMEM((2, rows, HD), bf16),
            pltpu.VMEM((NOTE_ROWS, HD), bf16),
            pltpu.SemaphoreType.DMA((2, 2, 4)),
        ],
        compiler_params=pltpu.CompilerParams(vmem_limit_bytes=VMEM_LIMIT),
        cost_estimate=cost("pack"),
        name="pack",
    )(*after, place, queries, keys, values, *notes)


def cut_kernel(ref, q_ref, kv_ref, scr, sems):
    load = pltpu.make_async_copy(ref, scr, sems.at[0])
    load.start()
    load.wait()
    stores = [
        pltpu.make_async_copy(scr.at[0, 0], q_ref.at[0], sems.at[1]),
        pltpu.make_async_copy(scr.at[0, pl.ds(1, 2)], kv_ref.at[0], sems.at[2]),
    ]
    for store in stores:
        store.start()
    for store in stores:
        store.wait()


def cut_call(packed, after=()):
    _, _, rows, _ = packed.shape
    hbm = pl.BlockSpec(memory_space=pltpu.HBM)
    return pl.pallas_call(
        ordered(cut_kernel, len(after)),
        out_shape=(
            jax.ShapeDtypeStruct((1, rows, HD), jnp.bfloat16),
            jax.ShapeDtypeStruct((1, 2, rows, HD), jnp.bfloat16),
        ),
        in_specs=[hbm] * (len(after) + 1),
        out_specs=(hbm, hbm),
        scratch_shapes=[
            pltpu.VMEM(packed.shape, jnp.bfloat16),
            pltpu.SemaphoreType.DMA((3,)),
        ],
        compiler_params=pltpu.CompilerParams(vmem_limit_bytes=VMEM_LIMIT),
        cost_estimate=cost("join"),
        name="join",
    )(*after, packed)


def join_kernel(heads, keep_ref, swap_ref, q_ref, kv_ref, scr, sems):
    loads, stores = [], []
    for side, ref in enumerate((keep_ref, swap_ref)):
        for h in range(heads):
            loads.append(pltpu.make_async_copy(ref.at[h], scr.at[side, h], sems.at[0, side, h]))
            stores.append(
                (
                    pltpu.make_async_copy(scr.at[side, h, 0], q_ref.at[side, h], sems.at[1, side, h]),
                    pltpu.make_async_copy(
                        scr.at[side, h, pl.ds(1, 2)], kv_ref.at[side, h], sems.at[2, side, h]
                    ),
                )
            )
    for load in loads:
        load.start()
    for load, pair in zip(loads, stores):
        load.wait()
        for store in pair:
            store.start()
    for pair in stores:
        for store in pair:
            store.wait()


def join_call(keep, swapped, after=()):
    heads, _, rows, _ = keep.shape
    hbm = pl.BlockSpec(memory_space=pltpu.HBM)
    return pl.pallas_call(
        ordered(partial(join_kernel, heads), len(after)),
        out_shape=(
            jax.ShapeDtypeStruct((2, heads, rows, HD), jnp.bfloat16),
            jax.ShapeDtypeStruct((2, heads, 2, rows, HD), jnp.bfloat16),
        ),
        in_specs=[hbm] * (len(after) + 2),
        out_specs=(hbm, hbm),
        scratch_shapes=[
            pltpu.VMEM((2, heads, 3, rows, HD), jnp.bfloat16),
            pltpu.SemaphoreType.DMA((3, 2, heads)),
        ],
        compiler_params=pltpu.CompilerParams(vmem_limit_bytes=VMEM_LIMIT),
        cost_estimate=cost("join"),
        name="join",
    )(*after, keep, swapped)


def merge_kernel(per_dev, block_rows, sizes, valid, sofar_ref, *refs):
    inputs, (keep_ref, send_ref, squares_ref) = refs[:-3], refs[-3:]
    spans = 2 * per_dev
    squares_ref[...] = sofar_ref[...]
    at = 0
    for c, size in enumerate(sizes):
        own_ref, own_lse_ref, near_ref, far_ref = inputs[4 * c : 4 * c + 4]
        for h in range(size):
            lses = [own_lse_ref[h]]
            for i, ref in enumerate((near_ref, far_ref)):
                lses.append(jnp.where(valid[i] > 0, unpacked_lse(ref, h, spans), -1e30))
            top = jnp.maximum(jnp.maximum(lses[0], lses[1]), lses[2])
            weights = [jnp.exp2(lse - top) for lse in lses]
            scale = 1.0 / (weights[0] + weights[1] + weights[2])
            weights = [weight * scale for weight in weights]
            for span in range(spans):
                rows = slice(span, span + 1)
                tile = slice(span * HD, (span + 1) * HD)
                mixed = weights[0][rows, :] * own_ref[h, span]
                mixed = mixed + weights[1][rows, :] * near_ref[h, tile, :].astype(jnp.float32)
                mixed = mixed + weights[2][rows, :] * far_ref[h, tile, :].astype(jnp.float32)
                squares_ref[rows, :] = squares_ref[rows, :] + jnp.sum(mixed * mixed, axis=0, keepdims=True)
                target = keep_ref if span < per_dev else send_ref
                start = (span % per_dev) * block_rows
                target[at, start : start + block_rows, :] = mixed.T.astype(target.dtype)
            at += 1


def merge_call(valid, sofar, parts, per_dev, after=()):
    block_rows = sofar.shape[1]
    sizes = [own[0].shape[0] for own, _, _ in parts]
    arrays = [array for own, near, far in parts for array in (*own, near, far)]
    vmem = pl.BlockSpec(memory_space=pltpu.VMEM)
    hbm = pl.BlockSpec(memory_space=pltpu.HBM)
    packed = jax.ShapeDtypeStruct((sum(sizes), per_dev * block_rows, HD), jnp.bfloat16)
    return pl.pallas_call(
        ordered(partial(merge_kernel, per_dev, block_rows, sizes), len(after)),
        out_shape=(packed, packed, jax.ShapeDtypeStruct(sofar.shape, jnp.float32)),
        in_specs=[hbm] * len(after)
        + [pl.BlockSpec(memory_space=pltpu.SMEM)]
        + [vmem] * (1 + len(arrays)),
        out_specs=(vmem, vmem, vmem),
        compiler_params=pltpu.CompilerParams(vmem_limit_bytes=VMEM_LIMIT),
        cost_estimate=cost("merge"),
        name="merge",
    )(*after, valid, sofar, *arrays)


def own_merge_kernel(per_dev, block_rows, valid, sofar_ref, squares_in_ref, own_ref, own_lse_ref, *refs):
    other_ref, packs, outs, squares_ref = refs[0], refs[1:5], refs[5:7], refs[7]
    squares_ref[...] = sofar_ref[:per_dev, :] + squares_in_ref[...]
    for side in range(2):
        arrivals = (packs[side], packs[2 + side])
        lses = [unpacked_lse(other_ref, 0, per_dev) if side else own_lse_ref[0]]
        for i, ref in enumerate(arrivals):
            lses.append(jnp.where(valid[i] > 0, unpacked_lse(ref, 0, per_dev), -1e30))
        top = jnp.maximum(jnp.maximum(lses[0], lses[1]), lses[2])
        weights = [jnp.exp2(lse - top) for lse in lses]
        scale = 1.0 / (weights[0] + weights[1] + weights[2])
        weights = [weight * scale for weight in weights]
        for span in range(per_dev):
            rows = slice(span, span + 1)
            tile = slice(span * HD, (span + 1) * HD)
            mixed = other_ref[0, tile, :].astype(jnp.float32) if side else own_ref[0, span]
            mixed = weights[0][rows, :] * mixed
            for weight, ref in zip(weights[1:], arrivals):
                mixed = mixed + weight[rows, :] * ref[0, tile, :].astype(jnp.float32)
            squares_ref[rows, :] = squares_ref[rows, :] + jnp.sum(mixed * mixed, axis=0, keepdims=True)
            at = slice(span * block_rows, (span + 1) * block_rows)
            outs[side][0, at, :] = mixed.T.astype(jnp.bfloat16)


def own_merge_call(valid, sofar, squares_in, own, other, packs, per_dev, after=()):
    block_rows = sofar.shape[1]
    vmem = pl.BlockSpec(memory_space=pltpu.VMEM)
    hbm = pl.BlockSpec(memory_space=pltpu.HBM)
    packed = jax.ShapeDtypeStruct((1, per_dev * block_rows, HD), jnp.bfloat16)
    return pl.pallas_call(
        ordered(partial(own_merge_kernel, per_dev, block_rows), len(after)),
        out_shape=(packed, packed, jax.ShapeDtypeStruct((per_dev, block_rows), jnp.float32)),
        in_specs=[hbm] * len(after) + [pl.BlockSpec(memory_space=pltpu.SMEM)] + [vmem] * 9,
        out_specs=(vmem, vmem, vmem),
        compiler_params=pltpu.CompilerParams(vmem_limit_bytes=VMEM_LIMIT),
        cost_estimate=cost("merge"),
        name="merge",
    )(*after, valid, sofar, squares_in, *own, other, *packs)


def finish_kernel(per_dev, sizes, place, *refs):
    n = len(sizes)
    kept, returned = refs[:n], refs[n : 2 * n]
    squares_ref, gain_ref, out_ref = refs[2 * n :]
    block_rows = squares_ref.shape[1]
    half = sum(sizes)
    factor = lax.rsqrt(squares_ref[...] / (HEADS * HD) + 1e-06)
    for b in range(per_dev):
        column = jnp.broadcast_to(factor[b : b + 1, :], (HD, block_rows)).T
        rows = slice(b * block_rows, (b + 1) * block_rows)
        for side, pieces in enumerate((kept, returned)):
            head = 0
            for piece, size in zip(pieces, sizes):
                for h in range(size):
                    start = pl.multiple_of((place[side] * half + head) * HD, HD)
                    gain = gain_ref[:, pl.ds(start, HD)].astype(jnp.float32)
                    value = piece[h, rows, :].astype(jnp.float32) * column * gain
                    out_ref[rows, pl.ds(start, HD)] = value.astype(out_ref.dtype)
                    head += 1


def finish_call(place, kept, returned, squares, gain, per_dev):
    vmem = pl.BlockSpec(memory_space=pltpu.VMEM)
    rows, width = kept[0].shape[1], gain.shape[0]
    return pl.pallas_call(
        partial(finish_kernel, per_dev, [k.shape[0] for k in kept]),
        out_shape=jax.ShapeDtypeStruct((rows, width), jnp.bfloat16),
        in_specs=[pl.BlockSpec(memory_space=pltpu.SMEM)] + [vmem] * (2 * len(kept) + 2),
        out_specs=vmem,
        compiler_params=pltpu.CompilerParams(vmem_limit_bytes=VMEM_LIMIT),
        cost_estimate=cost("finish"),
        name="finish",
    )(place, *kept, *returned, squares, gain.reshape(1, width))


def plan_of(live, slot, diagonal, dump):
    spans, entries = live.shape
    t = jnp.arange(entries)
    earlier = jnp.sum((t[None, None, :] < t[None, :, None]) & live[:, None, :], axis=2)
    span = lax.broadcasted_iota(jnp.int32, live.shape, 0)
    code = unit_code(slot, span, span, (earlier == 0).astype(jnp.int32), diagonal)
    code, live = code.reshape(-1), live.reshape(-1)
    n = spans * entries
    i = jnp.arange(n)
    rank = jnp.sum((i[None, :] < i[:, None]) & live[None, :], axis=1)
    at = jnp.arange(n + 8 * UNROLL)
    hit = live[None, :] & (rank[None, :] + 2 * UNROLL == at[:, None])
    idle = unit_code(0, 0, dump, 1, 0)
    codes = jnp.sum(jnp.where(hit, code[None, :] - idle, 0), axis=1) + idle
    total = jnp.sum(live.astype(jnp.int32))
    steps = jnp.where(total > 0, (total + UNROLL - 1) // UNROLL + 2, 0)
    return jnp.concatenate([steps[None], codes]).astype(jnp.int32)


def level_shards(queries, keys, values, selection, norm_gain):
    device = lax.axis_index("ctx")
    level, x = device // 2, device % 2
    rows, width = queries.shape
    per_dev, topk = selection.shape
    block_rows = rows // per_dev
    spans = 2 * per_dev
    half = width // HD // 2

    sent = {}

    def to(array, pairs, name):
        with jax.named_scope(name):
            sent[name] = lax.ppermute(array, "ctx", pairs)
        return sent[name]

    def exchange(array, name):
        pairs = [[d, d + 1] for d in range(0, 8, 2)]
        with jax.named_scope(name):
            sent[name] = lax.psum_scatter(
                array, "ctx", scatter_dimension=0, axis_index_groups=pairs, tiled=True
            )
        return sent[name]

    swap = [(d, d ^ 1) for d in range(8)]
    lift = [(0, 2), (1, 3)]
    near_down, far_down = [(4, 2), (5, 3), (6, 4), (7, 5)], [(6, 2), (7, 3)]

    def crossed(pairs):
        return [(source, target ^ 1) for source, target in pairs]

    near_up, far_up = [(2, 4), (3, 5), (4, 6), (5, 7)], [(2, 6), (3, 7)]
    valid = jnp.stack([level >= 2, level >= 3]).astype(jnp.int32)
    place = jnp.stack([x, 1 - x]).astype(jnp.int32)

    own_selection = jnp.concatenate([selection, to(selection, swap, "selection_swap")], axis=0)
    note = jnp.zeros((NOTE_ROWS, HD), jnp.bfloat16)
    note = lax.dynamic_update_slice(note, own_selection.astype(jnp.bfloat16), (0, 0))

    def ids(at):
        first = jnp.stack([(at * 2 + x) * per_dev, (at * 2 + 1 - x) * per_dev])
        return (first[:, None] + jnp.arange(per_dev)[None, :]).reshape(-1, 1)

    def slots(blocks):
        owner = blocks // per_dev
        slot = jnp.where(owner // 2 == level, 0, spans) + jnp.where(owner % 2 == x, 0, per_dev)
        return owner // 2, slot + blocks % per_dev

    others = own_selection[:, 1:]
    block_level, slot = slots(others)
    live = (others != ids(level)) & ((block_level == level) | ((level == 1) & (block_level == 0)))
    first = jnp.ones((spans, 1), jnp.int32)
    own_plan = plan_of(
        jnp.concatenate([first > 0, live], axis=1),
        jnp.concatenate([jnp.arange(spans, dtype=jnp.int32)[:, None], slot], axis=1),
        jnp.concatenate([first, jnp.zeros_like(others)], axis=1),
        spans,
    )
    def served_lists(*noted):
        near_selection, far_selection = (
            array[0, rows : rows + spans, :topk].astype(jnp.int32) for array in noted
        )
        others = jnp.concatenate([near_selection, far_selection], axis=0)[:, 1:]
        block_level, slot = slots(others)
        is_near = lax.broadcasted_iota(jnp.int32, others.shape, 0) < spans
        mine = ((level == 1) & (block_level <= 1)) | ((level == 2) & (block_level == 2) & is_near)
        live = (others != jnp.concatenate([ids(level + 1), ids(level + 2)], axis=0)) & mine
        return plan_of(live, slot, jnp.zeros_like(others), 2 * spans)

    n, split, order = half, SPLIT, ORDER
    own_pieces, z_arrays, served_pieces, downs_of = {}, {}, {}, {}
    ups, owns, others, squares_in, kept, returned = {}, {}, {}, [], [], []
    squares = [jnp.zeros((spans, block_rows), jnp.float32)]
    last, served_plan = [], []

    def downs(q, kv, name):
        low = to(kv, lift, f"lift_{name}")
        far = to(q, far_down, f"far_down_{name}")
        return to(q, near_down, f"near_down_{name}"), far, low

    def pack(c):
        if split[c]:
            (send,) = pack_call(place, queries, keys, values, c, half, (1,), None, last)
            swapped = to(send, swap, f"swap_c{c}")
            q_keep, kv_keep = pack_call(
                place, queries, keys, values, c, half, (0,), note, (*last, send)
            )
            last[:] = [q_keep]
            downs_of[c] = downs(q_keep, kv_keep, f"keep_c{c}")
            served_plan.append(served_lists(*downs_of[c][:2]))
            z_arrays[c] = (swapped,)
            own_pieces[c] = (
                [(q_keep, "top rows"), (swapped, "queries")],
                [(kv_keep, "head"), (swapped, "keys_values")],
            )
        else:
            send, keep = pack_call(place, queries, keys, values, c, half, (1, 0), None, last)
            last[:] = [keep]
            z_arrays[c] = (keep, to(send, swap, f"swap_c{c}"))
            own_pieces[c] = (
                [(array, "queries") for array in z_arrays[c]],
                [(array, "keys_values") for array in z_arrays[c]],
            )

    def join(c):
        if split[c]:
            q_swap, kv_swap = cut_call(*z_arrays[c], last)
            last[:] = [q_swap]
            swaps = downs(q_swap, kv_swap, f"recv_c{c}")
            near, far, low = [
                [(k, kind), (r, "head")]
                for k, r, kind in zip(downs_of[c], swaps, ("top rows", "top rows", "head"))
            ]
        else:
            level_q, level_kv = join_call(*z_arrays[c], last)
            last[:] = [level_q]
            near, far, low = [
                [(array, "first"), (array, "second")] for array in downs(level_q, level_kv, f"c{c}")
            ]
        served_pieces[c] = (near + far, own_pieces[c][1] + low)

    def is_direct(c):
        return DIRECT and c == n - 1

    def serve(c):
        packs = attention_call(
            served_plan[0], *served_pieces[c], False, is_direct(c), 1, per_dev, block_rows, last
        )
        last[:] = [packs[0]]
        if is_direct(c):
            near_same, near_cross, far_same, far_cross = packs
            far = (
                to(far_same, far_up, f"far_up_same_c{c}"),
                to(far_cross, crossed(far_up), f"far_up_cross_c{c}"),
            )
            near = (
                to(near_same, near_up, f"near_up_same_c{c}"),
                to(near_cross, crossed(near_up), f"near_up_cross_c{c}"),
            )
            ups[c] = (*near, *far)
        else:
            near, far = packs
            far = to(far, far_up, f"far_up_c{c}")
            ups[c] = (to(near, near_up, f"near_up_c{c}"), far)

    def attend(c):
        state = attention_call(
            own_plan,
            own_pieces[c][0],
            served_pieces[c][1],
            True,
            is_direct(c),
            1,
            per_dev,
            block_rows,
            last,
        )
        last[:] = [state[1]]
        owns[c] = state[:2]
        if is_direct(c):
            others[c] = to(state[2], swap, f"back_own_c{c}")

    def merge(*chunks):
        if is_direct(chunks[0]):
            c = chunks[0]
            keep, back, squares[0] = own_merge_call(
                valid, squares[0], squares_in[0], owns[c], others[c], ups[c], per_dev, last
            )
            kept.append(keep)
            returned.append(back)
            return
        parts = [(owns[c], *ups[c]) for c in chunks]
        keep, send, squares[0] = merge_call(valid, squares[0], parts, per_dev, last)
        last[:] = [keep]
        kept.append(keep)
        returned.append(to(send, swap, f"back_c{chunks[0]}"))
        if DIRECT and chunks[-1] == n - 2:
            squares_in.append(to(squares[0][per_dev:], swap, "squares_swap"))

    steps = {"p": pack, "j": join, "s": serve, "a": attend, "m": merge}
    for what, *args in order:
        if what == "w":
            tokens = {"plan": own_plan, "served": served_plan and served_plan[0], **sent}
            last.append(tokens[args[0]])
        else:
            steps[what](*args)
    square = squares[0]
    if not DIRECT:
        square = square[:per_dev] + to(square[per_dev:], swap, "squares_swap")
    n_head = lax.axis_size("head")
    hop = 1
    while hop < n_head:
        square = square + lax.ppermute(square, "head", [(i, i ^ hop) for i in range(n_head)])
        hop *= 2
    return finish_call(place, kept, returned, square, norm_gain, per_dev)


def solution(mesh):
    placed = (P("ctx", "head"), P("ctx", "head"), P("ctx", "head"), P("ctx", None), P("head"))
    body = level_shards if mesh.shape["ctx"] == 8 else shards
    return jax.shard_map(
        body, mesh=mesh, in_specs=placed, out_specs=P("ctx", "head"), check_vma=False
    )
```

```python
from functools import partial
import math

import jax
import jax.numpy as jnp
from jax import lax
from jax.experimental import pallas as pl
from jax.experimental.pallas import tpu as pltpu
from jax.sharding import PartitionSpec as P

HEADS = 32
HD = 128
CAP = 2
LOG2E = math.log2(math.e)
EXP_SCALE = HD ** (-0.5) * LOG2E


def partial_state(query_rows, key_block, value_block, causal):
    scores = jnp.einsum(
        "sqhd,skhd->shqk", query_rows, key_block, preferred_element_type=jnp.float32
    ) * query_rows.shape[3] ** (-0.5)
    if causal:
        query_pos = lax.broadcasted_iota(jnp.int32, scores.shape, 2)
        key_pos = lax.broadcasted_iota(jnp.int32, scores.shape, 3)
        scores = jnp.where(key_pos <= query_pos, scores, -1e30)
    row_peak = jnp.max(scores, axis=3)
    exponentials = jnp.exp(scores - row_peak[..., None])
    row_sum = jnp.sum(exponentials, axis=3)
    weights = exponentials.astype(jnp.bfloat16)
    blended = jnp.einsum(
        "shqk,skhd->sqhd", weights, value_block, preferred_element_type=jnp.float32
    )
    blended = blended / jnp.transpose(row_sum, (0, 2, 1))[..., None]
    return (blended, row_peak + jnp.log(row_sum))


def slot_plan(selected, first_span, per_dev, capacity):
    own_span = first_span + lax.broadcasted_iota(jnp.int32, selected.shape, 0)
    is_live = (selected != own_span).reshape(-1)
    owner_dev = (selected // per_dev).reshape(-1)
    pair_count = owner_dev.shape[0]
    is_later = lax.broadcasted_iota(jnp.int32, (pair_count, pair_count), 0) > lax.broadcasted_iota(
        jnp.int32, (pair_count, pair_count), 1
    )
    earlier = is_later & (owner_dev[:, None] == owner_dev[None, :]) & is_live[None, :]
    slot_rank = jnp.sum(earlier.astype(jnp.int32), axis=1)
    slot_index = jnp.where(is_live, owner_dev * capacity + slot_rank, 0)
    return (slot_index, is_live, (selected % per_dev).reshape(-1))


def shards(queries, keys, values, selection, norm_gain):
    n_ctx = lax.axis_size("ctx")
    device = lax.axis_index("ctx")
    rows, width = queries.shape
    per_dev, topk_count = selection.shape
    block_rows = rows // per_dev
    heads_dev = width // HD
    slot_count = n_ctx * CAP
    group_size = math.gcd(slot_count, 4)
    query_blocks = queries.reshape(per_dev, block_rows, heads_dev, HD)
    key_blocks = keys.reshape(per_dev, block_rows, heads_dev, HD)
    value_blocks = values.reshape(per_dev, block_rows, heads_dev, HD)
    slot_index, is_live, local_block = slot_plan(selection[:, 1:], device * per_dev, per_dev, CAP)
    pair_count = slot_index.shape[0]
    pair_span = lax.broadcasted_iota(jnp.int32, (pair_count,), 0) // (topk_count - 1)
    slot_ids = lax.broadcasted_iota(jnp.int32, (slot_count, pair_count), 0)
    placed = (slot_ids == slot_index[None, :]) & is_live[None, :]
    slot_span = jnp.sum(jnp.where(placed, pair_span[None, :], 0), axis=1)
    everyone = lax.all_gather(selection, "ctx", axis=0, tiled=True)
    requests = everyone[:, 1:].reshape(n_ctx, per_dev, topk_count - 1)
    first_spans = lax.broadcasted_iota(jnp.int32, (n_ctx,), 0) * per_dev
    all_slots, all_live, all_local = jax.vmap(partial(slot_plan, per_dev=per_dev, capacity=CAP))(
        requests, first_spans
    )
    owner_devs = requests.reshape(n_ctx, -1) // per_dev
    served = all_live & (owner_devs == device)
    capacity_ids = lax.broadcasted_iota(jnp.int32, (1, CAP, 1), 1)
    matched = served[:, None, :] & (all_slots[:, None, :] == device * CAP + capacity_ids)
    send_block = jnp.sum(jnp.where(matched, all_local[:, None, :], 0), axis=2)
    key_out = key_blocks[send_block].reshape(n_ctx, CAP, block_rows, width)
    value_out = value_blocks[send_block].reshape(n_ctx, CAP, block_rows, width)
    key_in, value_in = (
        lax.all_to_all(key_out, "ctx", split_axis=0, concat_axis=0, tiled=True),
        lax.all_to_all(value_out, "ctx", split_axis=0, concat_axis=0, tiled=True),
    )

    def one_group(packed):
        group_keys, group_values, group_span = packed
        blended, log_sums = partial_state(query_blocks[group_span], group_keys, group_values, False)
        return (blended.astype(jnp.bfloat16), log_sums)

    slot_out, slot_lse = lax.map(
        one_group,
        (
            key_in.reshape(-1, group_size, block_rows, heads_dev, HD),
            value_in.reshape(-1, group_size, block_rows, heads_dev, HD),
            slot_span.reshape(-1, group_size),
        ),
    )
    slot_out = slot_out.reshape(slot_count, block_rows, heads_dev, HD)
    slot_lse = slot_lse.reshape(slot_count, heads_dev, block_rows)
    own_out, own_lse = partial_state(query_blocks, key_blocks, value_blocks, True)
    live_pairs = is_live.reshape(per_dev, topk_count - 1)
    pair_out = (
        slot_out[slot_index]
        .reshape(per_dev, topk_count - 1, block_rows, heads_dev, HD)
        .astype(jnp.float32)
    )
    pair_lse = jnp.where(
        live_pairs[:, :, None, None],
        slot_lse[slot_index].reshape(per_dev, topk_count - 1, heads_dev, block_rows),
        -1e30,
    )
    highest = jnp.maximum(own_lse, jnp.max(pair_lse, axis=1))
    own_weight = jnp.exp(own_lse - highest)
    pair_weight = jnp.where(live_pairs[:, :, None, None], jnp.exp(pair_lse - highest[:, None]), 0.0)
    numerator = jnp.transpose(own_weight, (0, 2, 1))[..., None] * own_out
    numerator = numerator + jnp.sum(
        jnp.transpose(pair_weight, (0, 1, 3, 2))[..., None] * pair_out, axis=1
    )
    denominator = own_weight + jnp.sum(pair_weight, axis=1)
    attended = (numerator / jnp.transpose(denominator, (0, 2, 1))[..., None]).reshape(rows, width)
    squares = jnp.sum(attended * attended, axis=1)
    summed = lax.psum(squares, "head")
    factor = lax.rsqrt(summed / (HEADS * HD) + 1e-06)
    return (attended * factor[:, None] * norm_gain.astype(jnp.float32)[None, :]).astype(
        jnp.bfloat16
    )


SPLIT = (True, False, False, False)
ORDER = (
    ("p", 0),
    ("w", "plan"),
    ("p", 1),
    ("w", "near_down_keep_c0"),
    ("w", "far_down_keep_c0"),
    ("j", 0),
    ("w", "lift_keep_c0"),
    ("w", "served"),
    ("p", 2),
    ("j", 1),
    ("s", 0),
    ("j", 2),
    ("a", 0),
    ("p", 3),
    ("s", 1),
    ("m", 0),
    ("a", 1),
    ("j", 3),
    ("s", 2),
    ("m", 1),
    ("a", 2),
    ("w", "back_c0"),
    ("s", 3),
    ("a", 3),
    ("m", 2),
    ("m", 3),
)
COSTS = {"pack": 2, "join": 1, "served": 6, "own": 5, "merge": 1, "finish": 3}
DIRECT = True
NOTE_ROWS = 16
UNROLL = 2
VMEM_LIMIT = 10 * 1024 * 1024


def unit_fields(code):
    return code & 31, (code >> 5) & 31, (code >> 10) & 63, (code >> 16) & 1, (code >> 17) & 1


def unit_code(slot, span, out, first, diagonal):
    return slot + span * 32 + out * 1024 + first * 65536 + diagonal * 131072


PIECES = {
    "head": lambda ref, h, rows: ref.at[h],
    "top rows": lambda ref, h, rows: ref.at[h, pl.ds(0, rows)],
    "queries": lambda ref, h, rows: ref.at[h, 0],
    "keys_values": lambda ref, h, rows: ref.at[h, pl.ds(1, 2)],
    "first": lambda ref, h, rows: ref.at[0, h],
    "second": lambda ref, h, rows: ref.at[1, h],
}


def attention_kernel(shape, own, groups, q_pieces, kv_pieces, n_in, plan, *refs):
    heads, per_dev, block_rows = shape
    n_q, n_kv = len(q_pieces), len(kv_pieces)
    inputs, refs = refs[:n_in], refs[n_in:]
    n_out = len(groups) + 2 * own
    outs, refs = refs[:n_out], refs[n_out:]
    (q_scr, kv_scr, s0, s1, p0, p1, d0, d1, acc_scr, top_scr, sum_scr, o_scr, lse_scr, sems) = refs[:14]
    s_scr, p_scr, decay_scr = (s0, s1), (p0, p1), (d0, d1)
    spans = n_q * per_dev
    copies = []
    for h in range(heads):
        for i, (n, kind) in enumerate(q_pieces):
            copies.append((PIECES[kind](inputs[n], h, per_dev * block_rows), q_scr.at[h, i], sems.at[h, i]))
        for i, (n, kind) in enumerate(kv_pieces):
            copies.append((PIECES[kind](inputs[n], h, per_dev * block_rows), kv_scr.at[h, i], sems.at[h, n_q + i]))
    copies = [pltpu.make_async_copy(*copy) for copy in copies]
    for copy in copies:
        copy.start()
    s1[...] = jnp.zeros_like(s1)
    p0[...] = jnp.zeros_like(p0)
    d0[...] = jnp.zeros_like(d0)
    d1[...] = jnp.zeros_like(d1)
    acc_scr[...] = jnp.zeros_like(acc_scr)
    top_scr[...] = jnp.zeros_like(top_scr)
    sum_scr[...] = jnp.ones_like(sum_scr)
    if own:
        bias_scr = refs[14]
        key_pos = lax.broadcasted_iota(jnp.int32, (block_rows, block_rows), 0)
        query_pos = lax.broadcasted_iota(jnp.int32, (block_rows, block_rows), 1)
        bias_scr[0] = jnp.zeros((block_rows, block_rows), jnp.float32)
        bias_scr[1] = jnp.where(key_pos <= query_pos, 0.0, -1e30)
    for copy in copies:
        copy.wait()

    def rows_of(i):
        return pl.ds(pl.multiple_of((i % per_dev) * block_rows, block_rows), block_rows)

    def step(h, at, now, acc, top, total):
        before = 1 - now
        for u in range(UNROLL):
            slot, _, out, _, _ = unit_fields(plan[at + u])
            vt = kv_scr[h, slot // per_dev, 1, rows_of(slot), :]
            vt = jnp.concatenate([vt[:HD], vt[HD:]], axis=1)
            mixed = jnp.dot(vt, p_scr[now][u], preferred_element_type=jnp.float32)
            acc = acc * decay_scr[now][u, 0:1, :] + mixed
            o_scr[out] = (acc * decay_scr[now][u, 1:2, :]).astype(o_scr.dtype)
        for u in range(UNROLL):
            _, _, out, first, _ = unit_fields(plan[at + UNROLL + u])
            s = s_scr[before][u]
            old = jnp.where(first == 1, -1e30, top)
            top = jnp.maximum(old, decay_scr[before][u, 2:3, :])
            decay = jnp.exp2((old - top) * EXP_SCALE)
            p = jnp.exp2((s - top) * EXP_SCALE)
            total = total * decay + jnp.sum(p, axis=0, keepdims=True)
            p_scr[before][u] = p.astype(jnp.bfloat16)
            decay_scr[before][u, 0:1, :] = decay
            decay_scr[before][u, 1:2, :] = 1.0 / total
            lse_scr[pl.ds(out, 1), :] = top * EXP_SCALE + jnp.log(total) * LOG2E
        for u in range(UNROLL):
            slot, span, _, _, diagonal = unit_fields(plan[at + 2 * UNROLL + u])
            k = kv_scr[h, slot // per_dev, 0, rows_of(slot), :]
            q = q_scr[h, span // per_dev, rows_of(span), :]
            s = lax.dot_general(k, q, (((1,), (1,)), ((), ())), preferred_element_type=jnp.float32)
            if own:
                s = s + bias_scr[diagonal]
            s_scr[now][u] = s
            decay_scr[now][u, 2:3, :] = jnp.max(s, axis=0, keepdims=True)
        return acc, top, total

    for h in range(heads):
        o_scr[...] = jnp.zeros_like(o_scr)
        lse_scr[...] = jnp.full_like(lse_scr, -1e30)

        def two_steps(i, carry):
            state = (acc_scr[...], top_scr[...], sum_scr[...])
            state = step(h, 1 + 2 * i * UNROLL, 0, *state)
            state = step(h, 1 + (2 * i + 1) * UNROLL, 1, *state)
            acc_scr[...], top_scr[...], sum_scr[...] = state
            return carry

        lax.fori_loop(0, (plan[0] + 1) // 2, two_steps, 0)
        if own:
            kept = outs[0].shape[1]
            outs[0][h] = o_scr[:kept]
            outs[1][h] = lse_scr[:kept, :]
        for out, (start, stop) in zip(outs[2 if own else 0 :], groups):
            n = stop - start
            for span in range(n):
                out[h, span * HD : (span + 1) * HD, :] = o_scr[start + span].astype(jnp.bfloat16)
            lse = lse_scr[start:stop, :]
            high = lse.astype(jnp.bfloat16).astype(jnp.float32)
            middle = (lse - high).astype(jnp.bfloat16).astype(jnp.float32)
            rest = jnp.zeros((lse_rows(n) - 3 * n, block_rows), jnp.float32)
            parts = jnp.concatenate([high, middle, lse - high - middle, rest], axis=0)
            out[h, n * HD :, :] = parts.astype(jnp.bfloat16)


def lse_rows(spans):
    return -(-3 * spans // 16) * 16


def unpacked_lse(ref, h, spans):
    parts = ref[h, spans * HD :, :].astype(jnp.float32)
    return parts[:spans] + parts[spans : 2 * spans] + parts[2 * spans : 3 * spans]


def cost(name):
    us = COSTS[name]
    return pl.CostEstimate(flops=int(us * 1e9) + 1, bytes_accessed=int(us * 3.4e6) + 1, transcendentals=0)


def ordered(kernel, n_after):
    def body(*refs):
        kernel(*refs[n_after:])

    return body


def attention_call(plan, q_pieces, kv_pieces, own, direct, heads, per_dev, block_rows, after=()):
    inputs = []

    def numbered(pieces):
        out = []
        for array, kind in pieces:
            if not any(array is known for known in inputs):
                inputs.append(array)
            out.append(([array is known for known in inputs].index(True), kind))
        return out

    q_pieces, kv_pieces = numbered(q_pieces), numbered(kv_pieces)
    n_q, n_kv = len(q_pieces), len(kv_pieces)
    spans = n_q * per_dev
    vmem, hbm = pl.BlockSpec(memory_space=pltpu.VMEM), pl.BlockSpec(memory_space=pltpu.HBM)
    f32, bf16 = jnp.float32, jnp.bfloat16
    if own:
        kept = per_dev if direct else spans
        groups = ((per_dev, spans),) if direct else ()
        out_shape = [
            jax.ShapeDtypeStruct((heads, kept, HD, block_rows), f32),
            jax.ShapeDtypeStruct((heads, kept, block_rows), f32),
        ]
    else:
        size = per_dev if direct else 2 * per_dev
        groups = tuple((start, start + size) for start in range(0, spans, size))
        out_shape = []
    for start, stop in groups:
        packed_rows = (stop - start) * HD + lse_rows(stop - start)
        out_shape.append(jax.ShapeDtypeStruct((heads, packed_rows, block_rows), bf16))
    scratch = [
        pltpu.VMEM((heads, n_q, per_dev * block_rows, HD), bf16),
        pltpu.VMEM((heads, n_kv, 2, per_dev * block_rows, HD), bf16),
        pltpu.VMEM((UNROLL, block_rows, block_rows), f32),
        pltpu.VMEM((UNROLL, block_rows, block_rows), f32),
        pltpu.VMEM((UNROLL, block_rows, block_rows), bf16),
        pltpu.VMEM((UNROLL, block_rows, block_rows), bf16),
        pltpu.VMEM((UNROLL, 8, block_rows), f32),
        pltpu.VMEM((UNROLL, 8, block_rows), f32),
        pltpu.VMEM((HD, block_rows), f32),
        pltpu.VMEM((1, block_rows), f32),
        pltpu.VMEM((1, block_rows), f32),
        pltpu.VMEM((spans + 1, HD, block_rows), f32 if own else bf16),
        pltpu.VMEM((spans + 8, block_rows), f32),
        pltpu.SemaphoreType.DMA((heads, n_q + n_kv)),
    ]
    if own:
        scratch.append(pltpu.VMEM((2, block_rows, block_rows), f32))
    return pl.pallas_call(
        ordered(
            partial(
                attention_kernel,
                (heads, per_dev, block_rows),
                own,
                groups,
                q_pieces,
                kv_pieces,
                len(inputs),
            ),
            len(after),
        ),
        out_shape=out_shape,
        in_specs=[hbm] * len(after) + [pl.BlockSpec(memory_space=pltpu.SMEM)] + [hbm] * len(inputs),
        out_specs=[vmem] * len(out_shape),
        scratch_shapes=scratch,
        compiler_params=pltpu.CompilerParams(vmem_limit_bytes=VMEM_LIMIT),
        cost_estimate=cost("own" if own else "served"),
        name="own_attention" if own else "served_attention",
    )(*after, plan, *inputs)


def pack_kernel(shape, place, q_ref, k_ref, v_ref, *refs):
    sides, head, half, rows, noted = shape
    n_out = len(sides) + noted
    note_ref, refs = (refs[0], refs[1:]) if noted else (None, refs)
    outs, (scr, t_scr, note_scr, sems) = refs[:n_out], refs[n_out:]
    loads, stores = {}, []
    for side in sides:
        start = pl.multiple_of((place[side] * half + head) * HD, HD)
        for i, ref in enumerate((q_ref, k_ref, v_ref)):
            loads[side, i] = pltpu.make_async_copy(
                ref.at[:, pl.ds(start, HD)], scr.at[side, i], sems.at[0, side, i]
            )
            loads[side, i].start()

    def store(source, target, side, i):
        copy = pltpu.make_async_copy(source, target, sems.at[1, side, i])
        copy.start()
        stores.append(copy)

    if noted:
        load = pltpu.make_async_copy(note_ref, note_scr, sems.at[0, 0, 3])
        load.start()
        load.wait()
        store(note_scr, outs[0].at[0, pl.ds(rows, NOTE_ROWS)], 0, 3)
    for side, out in zip(sides, outs[noted:]):
        targets = [out.at[0, i] for i in range(3)]
        if noted:
            targets = [outs[0].at[0, pl.ds(0, rows)], out.at[0, 0], out.at[0, 1]]
        for i in range(2):
            loads[side, i].wait()
            store(scr.at[side, i], targets[i], side, i)
        loads[side, 2].wait()
        for tile in range(rows // HD):
            at = slice(tile * HD, (tile + 1) * HD)
            t_scr[side, at, :] = scr[side, 2, at, :].T
        store(t_scr.at[side], targets[2], side, 2)
    for copy in stores:
        copy.wait()


def pack_call(place, queries, keys, values, head, half, sides=(1, 0), note=None, after=()):
    rows = queries.shape[0]
    hbm = pl.BlockSpec(memory_space=pltpu.HBM)
    bf16 = jnp.bfloat16
    queries, keys, values = (
        pltpu.with_memory_space_constraint(array, pltpu.HBM) for array in (queries, keys, values)
    )
    noted = note is not None
    if noted:
        shapes, notes = [(1, rows + NOTE_ROWS, HD), (1, 2, rows, HD)], [note]
    else:
        shapes, notes = [(1, 3, rows, HD)] * len(sides), []
    return pl.pallas_call(
        ordered(partial(pack_kernel, (sides, head, half, rows, noted)), len(after)),
        out_shape=[jax.ShapeDtypeStruct(shape, bf16) for shape in shapes],
        in_specs=[hbm] * len(after) + [pl.BlockSpec(memory_space=pltpu.SMEM)] + [hbm] * (3 + noted),
        out_specs=[hbm] * len(shapes),
        scratch_shapes=[
            pltpu.VMEM((2, 3, rows, HD), bf16),
            pltpu.VMEM((2, rows, HD), bf16),
            pltpu.VMEM((NOTE_ROWS, HD), bf16),
            pltpu.SemaphoreType.DMA((2, 2, 4)),
        ],
        compiler_params=pltpu.CompilerParams(vmem_limit_bytes=VMEM_LIMIT),
        cost_estimate=cost("pack"),
        name="pack",
    )(*after, place, queries, keys, values, *notes)


def cut_kernel(ref, q_ref, kv_ref, scr, sems):
    load = pltpu.make_async_copy(ref, scr, sems.at[0])
    load.start()
    load.wait()
    stores = [
        pltpu.make_async_copy(scr.at[0, 0], q_ref.at[0], sems.at[1]),
        pltpu.make_async_copy(scr.at[0, pl.ds(1, 2)], kv_ref.at[0], sems.at[2]),
    ]
    for store in stores:
        store.start()
    for store in stores:
        store.wait()


def cut_call(packed, after=()):
    _, _, rows, _ = packed.shape
    hbm = pl.BlockSpec(memory_space=pltpu.HBM)
    return pl.pallas_call(
        ordered(cut_kernel, len(after)),
        out_shape=(
            jax.ShapeDtypeStruct((1, rows, HD), jnp.bfloat16),
            jax.ShapeDtypeStruct((1, 2, rows, HD), jnp.bfloat16),
        ),
        in_specs=[hbm] * (len(after) + 1),
        out_specs=(hbm, hbm),
        scratch_shapes=[
            pltpu.VMEM(packed.shape, jnp.bfloat16),
            pltpu.SemaphoreType.DMA((3,)),
        ],
        compiler_params=pltpu.CompilerParams(vmem_limit_bytes=VMEM_LIMIT),
        cost_estimate=cost("join"),
        name="join",
    )(*after, packed)


def join_kernel(heads, keep_ref, swap_ref, q_ref, kv_ref, scr, sems):
    loads, stores = [], []
    for side, ref in enumerate((keep_ref, swap_ref)):
        for h in range(heads):
            loads.append(pltpu.make_async_copy(ref.at[h], scr.at[side, h], sems.at[0, side, h]))
            stores.append(
                (
                    pltpu.make_async_copy(scr.at[side, h, 0], q_ref.at[side, h], sems.at[1, side, h]),
                    pltpu.make_async_copy(
                        scr.at[side, h, pl.ds(1, 2)], kv_ref.at[side, h], sems.at[2, side, h]
                    ),
                )
            )
    for load in loads:
        load.start()
    for load, pair in zip(loads, stores):
        load.wait()
        for store in pair:
            store.start()
    for pair in stores:
        for store in pair:
            store.wait()


def join_call(keep, swapped, after=()):
    heads, _, rows, _ = keep.shape
    hbm = pl.BlockSpec(memory_space=pltpu.HBM)
    return pl.pallas_call(
        ordered(partial(join_kernel, heads), len(after)),
        out_shape=(
            jax.ShapeDtypeStruct((2, heads, rows, HD), jnp.bfloat16),
            jax.ShapeDtypeStruct((2, heads, 2, rows, HD), jnp.bfloat16),
        ),
        in_specs=[hbm] * (len(after) + 2),
        out_specs=(hbm, hbm),
        scratch_shapes=[
            pltpu.VMEM((2, heads, 3, rows, HD), jnp.bfloat16),
            pltpu.SemaphoreType.DMA((3, 2, heads)),
        ],
        compiler_params=pltpu.CompilerParams(vmem_limit_bytes=VMEM_LIMIT),
        cost_estimate=cost("join"),
        name="join",
    )(*after, keep, swapped)


def merge_kernel(per_dev, block_rows, sizes, valid, sofar_ref, *refs):
    inputs, (keep_ref, send_ref, squares_ref) = refs[:-3], refs[-3:]
    spans = 2 * per_dev
    squares_ref[...] = sofar_ref[...]
    at = 0
    for c, size in enumerate(sizes):
        own_ref, own_lse_ref, near_ref, far_ref = inputs[4 * c : 4 * c + 4]
        for h in range(size):
            lses = [own_lse_ref[h]]
            for i, ref in enumerate((near_ref, far_ref)):
                lses.append(jnp.where(valid[i] > 0, unpacked_lse(ref, h, spans), -1e30))
            top = jnp.maximum(jnp.maximum(lses[0], lses[1]), lses[2])
            weights = [jnp.exp2(lse - top) for lse in lses]
            scale = 1.0 / (weights[0] + weights[1] + weights[2])
            weights = [weight * scale for weight in weights]
            for span in range(spans):
                rows = slice(span, span + 1)
                tile = slice(span * HD, (span + 1) * HD)
                mixed = weights[0][rows, :] * own_ref[h, span]
                mixed = mixed + weights[1][rows, :] * near_ref[h, tile, :].astype(jnp.float32)
                mixed = mixed + weights[2][rows, :] * far_ref[h, tile, :].astype(jnp.float32)
                squares_ref[rows, :] = squares_ref[rows, :] + jnp.sum(mixed * mixed, axis=0, keepdims=True)
                target = keep_ref if span < per_dev else send_ref
                start = (span % per_dev) * block_rows
                target[at, start : start + block_rows, :] = mixed.T.astype(target.dtype)
            at += 1


def merge_call(valid, sofar, parts, per_dev, after=()):
    block_rows = sofar.shape[1]
    sizes = [own[0].shape[0] for own, _, _ in parts]
    arrays = [array for own, near, far in parts for array in (*own, near, far)]
    vmem = pl.BlockSpec(memory_space=pltpu.VMEM)
    hbm = pl.BlockSpec(memory_space=pltpu.HBM)
    packed = jax.ShapeDtypeStruct((sum(sizes), per_dev * block_rows, HD), jnp.bfloat16)
    return pl.pallas_call(
        ordered(partial(merge_kernel, per_dev, block_rows, sizes), len(after)),
        out_shape=(packed, packed, jax.ShapeDtypeStruct(sofar.shape, jnp.float32)),
        in_specs=[hbm] * len(after)
        + [pl.BlockSpec(memory_space=pltpu.SMEM)]
        + [vmem] * (1 + len(arrays)),
        out_specs=(vmem, vmem, vmem),
        compiler_params=pltpu.CompilerParams(vmem_limit_bytes=VMEM_LIMIT),
        cost_estimate=cost("merge"),
        name="merge",
    )(*after, valid, sofar, *arrays)


def own_merge_kernel(per_dev, block_rows, valid, sofar_ref, squares_in_ref, own_ref, own_lse_ref, *refs):
    other_ref, packs, outs, squares_ref = refs[0], refs[1:5], refs[5:7], refs[7]
    squares_ref[...] = sofar_ref[:per_dev, :] + squares_in_ref[...]
    for side in range(2):
        arrivals = (packs[side], packs[2 + side])
        lses = [unpacked_lse(other_ref, 0, per_dev) if side else own_lse_ref[0]]
        for i, ref in enumerate(arrivals):
            lses.append(jnp.where(valid[i] > 0, unpacked_lse(ref, 0, per_dev), -1e30))
        top = jnp.maximum(jnp.maximum(lses[0], lses[1]), lses[2])
        weights = [jnp.exp2(lse - top) for lse in lses]
        scale = 1.0 / (weights[0] + weights[1] + weights[2])
        weights = [weight * scale for weight in weights]
        for span in range(per_dev):
            rows = slice(span, span + 1)
            tile = slice(span * HD, (span + 1) * HD)
            mixed = other_ref[0, tile, :].astype(jnp.float32) if side else own_ref[0, span]
            mixed = weights[0][rows, :] * mixed
            for weight, ref in zip(weights[1:], arrivals):
                mixed = mixed + weight[rows, :] * ref[0, tile, :].astype(jnp.float32)
            squares_ref[rows, :] = squares_ref[rows, :] + jnp.sum(mixed * mixed, axis=0, keepdims=True)
            at = slice(span * block_rows, (span + 1) * block_rows)
            outs[side][0, at, :] = mixed.T.astype(jnp.bfloat16)


def own_merge_call(valid, sofar, squares_in, own, other, packs, per_dev, after=()):
    block_rows = sofar.shape[1]
    vmem = pl.BlockSpec(memory_space=pltpu.VMEM)
    hbm = pl.BlockSpec(memory_space=pltpu.HBM)
    packed = jax.ShapeDtypeStruct((1, per_dev * block_rows, HD), jnp.bfloat16)
    return pl.pallas_call(
        ordered(partial(own_merge_kernel, per_dev, block_rows), len(after)),
        out_shape=(packed, packed, jax.ShapeDtypeStruct((per_dev, block_rows), jnp.float32)),
        in_specs=[hbm] * len(after) + [pl.BlockSpec(memory_space=pltpu.SMEM)] + [vmem] * 9,
        out_specs=(vmem, vmem, vmem),
        compiler_params=pltpu.CompilerParams(vmem_limit_bytes=VMEM_LIMIT),
        cost_estimate=cost("merge"),
        name="merge",
    )(*after, valid, sofar, squares_in, *own, other, *packs)


def finish_kernel(per_dev, sizes, place, *refs):
    n = len(sizes)
    kept, returned = refs[:n], refs[n : 2 * n]
    squares_ref, gain_ref, out_ref = refs[2 * n :]
    block_rows = squares_ref.shape[1]
    half = sum(sizes)
    factor = lax.rsqrt(squares_ref[...] / (HEADS * HD) + 1e-06)
    for b in range(per_dev):
        column = jnp.broadcast_to(factor[b : b + 1, :], (HD, block_rows)).T
        rows = slice(b * block_rows, (b + 1) * block_rows)
        for side, pieces in enumerate((kept, returned)):
            head = 0
            for piece, size in zip(pieces, sizes):
                for h in range(size):
                    start = pl.multiple_of((place[side] * half + head) * HD, HD)
                    gain = gain_ref[:, pl.ds(start, HD)].astype(jnp.float32)
                    value = piece[h, rows, :].astype(jnp.float32) * column * gain
                    out_ref[rows, pl.ds(start, HD)] = value.astype(out_ref.dtype)
                    head += 1


def finish_call(place, kept, returned, squares, gain, per_dev):
    vmem = pl.BlockSpec(memory_space=pltpu.VMEM)
    rows, width = kept[0].shape[1], gain.shape[0]
    return pl.pallas_call(
        partial(finish_kernel, per_dev, [k.shape[0] for k in kept]),
        out_shape=jax.ShapeDtypeStruct((rows, width), jnp.bfloat16),
        in_specs=[pl.BlockSpec(memory_space=pltpu.SMEM)] + [vmem] * (2 * len(kept) + 2),
        out_specs=vmem,
        compiler_params=pltpu.CompilerParams(vmem_limit_bytes=VMEM_LIMIT),
        cost_estimate=cost("finish"),
        name="finish",
    )(place, *kept, *returned, squares, gain.reshape(1, width))


def plan_of(live, slot, diagonal, dump):
    spans, entries = live.shape
    t = jnp.arange(entries)
    earlier = jnp.sum((t[None, None, :] < t[None, :, None]) & live[:, None, :], axis=2)
    span = lax.broadcasted_iota(jnp.int32, live.shape, 0)
    code = unit_code(slot, span, span, (earlier == 0).astype(jnp.int32), diagonal)
    code, live = code.reshape(-1), live.reshape(-1)
    n = spans * entries
    i = jnp.arange(n)
    rank = jnp.sum((i[None, :] < i[:, None]) & live[None, :], axis=1)
    at = jnp.arange(n + 8 * UNROLL)
    hit = live[None, :] & (rank[None, :] + 2 * UNROLL == at[:, None])
    idle = unit_code(0, 0, dump, 1, 0)
    codes = jnp.sum(jnp.where(hit, code[None, :] - idle, 0), axis=1) + idle
    total = jnp.sum(live.astype(jnp.int32))
    steps = jnp.where(total > 0, (total + UNROLL - 1) // UNROLL + 2, 0)
    return jnp.concatenate([steps[None], codes]).astype(jnp.int32)


def level_shards(queries, keys, values, selection, norm_gain):
    device = lax.axis_index("ctx")
    level, x = device // 2, device % 2
    rows, width = queries.shape
    per_dev, topk = selection.shape
    block_rows = rows // per_dev
    spans = 2 * per_dev
    half = width // HD // 2

    sent = {}

    def to(array, pairs, name):
        with jax.named_scope(name):
            sent[name] = lax.ppermute(array, "ctx", pairs)
        return sent[name]

    swap = [(d, d ^ 1) for d in range(8)]
    lift = [(0, 2), (1, 3)]
    near_down, far_down = [(4, 2), (5, 3), (6, 4), (7, 5)], [(6, 2), (7, 3)]

    def crossed(pairs):
        return [(source, target ^ 1) for source, target in pairs]

    near_up, far_up = [(2, 4), (3, 5), (4, 6), (5, 7)], [(2, 6), (3, 7)]
    valid = jnp.stack([level >= 2, level >= 3]).astype(jnp.int32)
    place = jnp.stack([x, 1 - x]).astype(jnp.int32)

    own_selection = jnp.concatenate([selection, to(selection, swap, "selection_swap")], axis=0)
    note = jnp.zeros((NOTE_ROWS, HD), jnp.bfloat16)
    note = lax.dynamic_update_slice(note, own_selection.astype(jnp.bfloat16), (0, 0))

    def ids(at):
        first = jnp.stack([(at * 2 + x) * per_dev, (at * 2 + 1 - x) * per_dev])
        return (first[:, None] + jnp.arange(per_dev)[None, :]).reshape(-1, 1)

    def slots(blocks):
        owner = blocks // per_dev
        slot = jnp.where(owner // 2 == level, 0, spans) + jnp.where(owner % 2 == x, 0, per_dev)
        return owner // 2, slot + blocks % per_dev

    others = own_selection[:, 1:]
    block_level, slot = slots(others)
    live = (others != ids(level)) & ((block_level == level) | ((level == 1) & (block_level == 0)))
    first = jnp.ones((spans, 1), jnp.int32)
    own_plan = plan_of(
        jnp.concatenate([first > 0, live], axis=1),
        jnp.concatenate([jnp.arange(spans, dtype=jnp.int32)[:, None], slot], axis=1),
        jnp.concatenate([first, jnp.zeros_like(others)], axis=1),
        spans,
    )
    def served_lists(*noted):
        near_selection, far_selection = (
            array[0, rows : rows + spans, :topk].astype(jnp.int32) for array in noted
        )
        others = jnp.concatenate([near_selection, far_selection], axis=0)[:, 1:]
        block_level, slot = slots(others)
        is_near = lax.broadcasted_iota(jnp.int32, others.shape, 0) < spans
        mine = ((level == 1) & (block_level <= 1)) | ((level == 2) & (block_level == 2) & is_near)
        live = (others != jnp.concatenate([ids(level + 1), ids(level + 2)], axis=0)) & mine
        return plan_of(live, slot, jnp.zeros_like(others), 2 * spans)

    n, split, order = half, SPLIT, ORDER
    own_pieces, z_arrays, served_pieces, downs_of = {}, {}, {}, {}
    ups, owns, others, squares_in, kept, returned = {}, {}, {}, [], [], []
    squares = [jnp.zeros((spans, block_rows), jnp.float32)]
    last, served_plan = [], []

    def downs(q, kv, name):
        low = to(kv, lift, f"lift_{name}")
        far = to(q, far_down, f"far_down_{name}")
        return to(q, near_down, f"near_down_{name}"), far, low

    def pack(c):
        if split[c]:
            (send,) = pack_call(place, queries, keys, values, c, half, (1,), None, last)
            swapped = to(send, swap, f"swap_c{c}")
            q_keep, kv_keep = pack_call(
                place, queries, keys, values, c, half, (0,), note, (*last, send)
            )
            last[:] = [q_keep]
            downs_of[c] = downs(q_keep, kv_keep, f"keep_c{c}")
            served_plan.append(served_lists(*downs_of[c][:2]))
            z_arrays[c] = (swapped,)
            own_pieces[c] = (
                [(q_keep, "top rows"), (swapped, "queries")],
                [(kv_keep, "head"), (swapped, "keys_values")],
            )
        else:
            send, keep = pack_call(place, queries, keys, values, c, half, (1, 0), None, last)
            last[:] = [keep]
            z_arrays[c] = (keep, to(send, swap, f"swap_c{c}"))
            own_pieces[c] = (
                [(array, "queries") for array in z_arrays[c]],
                [(array, "keys_values") for array in z_arrays[c]],
            )

    def join(c):
        if split[c]:
            q_swap, kv_swap = cut_call(*z_arrays[c], last)
            last[:] = [q_swap]
            swaps = downs(q_swap, kv_swap, f"recv_c{c}")
            near, far, low = [
                [(k, kind), (r, "head")]
                for k, r, kind in zip(downs_of[c], swaps, ("top rows", "top rows", "head"))
            ]
        else:
            level_q, level_kv = join_call(*z_arrays[c], last)
            last[:] = [level_q]
            near, far, low = [
                [(array, "first"), (array, "second")] for array in downs(level_q, level_kv, f"c{c}")
            ]
        served_pieces[c] = (near + far, own_pieces[c][1] + low)

    def is_direct(c):
        return DIRECT and c == n - 1

    def serve(c):
        packs = attention_call(
            served_plan[0], *served_pieces[c], False, is_direct(c), 1, per_dev, block_rows, last
        )
        last[:] = [packs[0]]
        if is_direct(c):
            near_same, near_cross, far_same, far_cross = packs
            far = (
                to(far_same, far_up, f"far_up_same_c{c}"),
                to(far_cross, crossed(far_up), f"far_up_cross_c{c}"),
            )
            near = (
                to(near_same, near_up, f"near_up_same_c{c}"),
                to(near_cross, crossed(near_up), f"near_up_cross_c{c}"),
            )
            ups[c] = (*near, *far)
        else:
            near, far = packs
            far = to(far, far_up, f"far_up_c{c}")
            ups[c] = (to(near, near_up, f"near_up_c{c}"), far)

    def attend(c):
        state = attention_call(
            own_plan,
            own_pieces[c][0],
            served_pieces[c][1],
            True,
            is_direct(c),
            1,
            per_dev,
            block_rows,
            last,
        )
        last[:] = [state[1]]
        owns[c] = state[:2]
        if is_direct(c):
            others[c] = to(state[2], swap, f"back_own_c{c}")

    def merge(*chunks):
        if is_direct(chunks[0]):
            c = chunks[0]
            keep, back, squares[0] = own_merge_call(
                valid, squares[0], squares_in[0], owns[c], others[c], ups[c], per_dev, last
            )
            kept.append(keep)
            returned.append(back)
            return
        parts = [(owns[c], *ups[c]) for c in chunks]
        keep, send, squares[0] = merge_call(valid, squares[0], parts, per_dev, last)
        last[:] = [keep]
        kept.append(keep)
        returned.append(to(send, swap, f"back_c{chunks[0]}"))
        if DIRECT and chunks[-1] == n - 2:
            squares_in.append(to(squares[0][per_dev:], swap, "squares_swap"))

    steps = {"p": pack, "j": join, "s": serve, "a": attend, "m": merge}
    for what, *args in order:
        if what == "w":
            tokens = {"plan": own_plan, "served": served_plan and served_plan[0], **sent}
            last.append(tokens[args[0]])
        else:
            steps[what](*args)
    square = squares[0]
    if not DIRECT:
        square = square[:per_dev] + to(square[per_dev:], swap, "squares_swap")
    n_head = lax.axis_size("head")
    hop = 1
    while hop < n_head:
        square = square + lax.ppermute(square, "head", [(i, i ^ hop) for i in range(n_head)])
        hop *= 2
    return finish_call(place, kept, returned, square, norm_gain, per_dev)


def solution(mesh):
    placed = (P("ctx", "head"), P("ctx", "head"), P("ctx", "head"), P("ctx", None), P("head"))
    body = level_shards if mesh.shape["ctx"] == 8 else shards
    return jax.shard_map(
        body, mesh=mesh, in_specs=placed, out_specs=P("ctx", "head"), check_vma=False
    )
```

```python
from functools import partial
import math

import jax
import jax.numpy as jnp
from jax import lax
from jax.experimental import pallas as pl
from jax.experimental.pallas import tpu as pltpu
from jax.sharding import PartitionSpec as P

HEADS = 32
HD = 128
CAP = 2
LOG2E = math.log2(math.e)
EXP_SCALE = HD ** (-0.5) * LOG2E


def partial_state(query_rows, key_block, value_block, causal):
    scores = jnp.einsum(
        "sqhd,skhd->shqk", query_rows, key_block, preferred_element_type=jnp.float32
    ) * query_rows.shape[3] ** (-0.5)
    if causal:
        query_pos = lax.broadcasted_iota(jnp.int32, scores.shape, 2)
        key_pos = lax.broadcasted_iota(jnp.int32, scores.shape, 3)
        scores = jnp.where(key_pos <= query_pos, scores, -1e30)
    row_peak = jnp.max(scores, axis=3)
    exponentials = jnp.exp(scores - row_peak[..., None])
    row_sum = jnp.sum(exponentials, axis=3)
    weights = exponentials.astype(jnp.bfloat16)
    blended = jnp.einsum(
        "shqk,skhd->sqhd", weights, value_block, preferred_element_type=jnp.float32
    )
    blended = blended / jnp.transpose(row_sum, (0, 2, 1))[..., None]
    return (blended, row_peak + jnp.log(row_sum))


def slot_plan(selected, first_span, per_dev, capacity):
    own_span = first_span + lax.broadcasted_iota(jnp.int32, selected.shape, 0)
    is_live = (selected != own_span).reshape(-1)
    owner_dev = (selected // per_dev).reshape(-1)
    pair_count = owner_dev.shape[0]
    is_later = lax.broadcasted_iota(jnp.int32, (pair_count, pair_count), 0) > lax.broadcasted_iota(
        jnp.int32, (pair_count, pair_count), 1
    )
    earlier = is_later & (owner_dev[:, None] == owner_dev[None, :]) & is_live[None, :]
    slot_rank = jnp.sum(earlier.astype(jnp.int32), axis=1)
    slot_index = jnp.where(is_live, owner_dev * capacity + slot_rank, 0)
    return (slot_index, is_live, (selected % per_dev).reshape(-1))


def shards(queries, keys, values, selection, norm_gain):
    n_ctx = lax.axis_size("ctx")
    device = lax.axis_index("ctx")
    rows, width = queries.shape
    per_dev, topk_count = selection.shape
    block_rows = rows // per_dev
    heads_dev = width // HD
    slot_count = n_ctx * CAP
    group_size = math.gcd(slot_count, 4)
    query_blocks = queries.reshape(per_dev, block_rows, heads_dev, HD)
    key_blocks = keys.reshape(per_dev, block_rows, heads_dev, HD)
    value_blocks = values.reshape(per_dev, block_rows, heads_dev, HD)
    slot_index, is_live, local_block = slot_plan(selection[:, 1:], device * per_dev, per_dev, CAP)
    pair_count = slot_index.shape[0]
    pair_span = lax.broadcasted_iota(jnp.int32, (pair_count,), 0) // (topk_count - 1)
    slot_ids = lax.broadcasted_iota(jnp.int32, (slot_count, pair_count), 0)
    placed = (slot_ids == slot_index[None, :]) & is_live[None, :]
    slot_span = jnp.sum(jnp.where(placed, pair_span[None, :], 0), axis=1)
    everyone = lax.all_gather(selection, "ctx", axis=0, tiled=True)
    requests = everyone[:, 1:].reshape(n_ctx, per_dev, topk_count - 1)
    first_spans = lax.broadcasted_iota(jnp.int32, (n_ctx,), 0) * per_dev
    all_slots, all_live, all_local = jax.vmap(partial(slot_plan, per_dev=per_dev, capacity=CAP))(
        requests, first_spans
    )
    owner_devs = requests.reshape(n_ctx, -1) // per_dev
    served = all_live & (owner_devs == device)
    capacity_ids = lax.broadcasted_iota(jnp.int32, (1, CAP, 1), 1)
    matched = served[:, None, :] & (all_slots[:, None, :] == device * CAP + capacity_ids)
    send_block = jnp.sum(jnp.where(matched, all_local[:, None, :], 0), axis=2)
    key_out = key_blocks[send_block].reshape(n_ctx, CAP, block_rows, width)
    value_out = value_blocks[send_block].reshape(n_ctx, CAP, block_rows, width)
    key_in, value_in = (
        lax.all_to_all(key_out, "ctx", split_axis=0, concat_axis=0, tiled=True),
        lax.all_to_all(value_out, "ctx", split_axis=0, concat_axis=0, tiled=True),
    )

    def one_group(packed):
        group_keys, group_values, group_span = packed
        blended, log_sums = partial_state(query_blocks[group_span], group_keys, group_values, False)
        return (blended.astype(jnp.bfloat16), log_sums)

    slot_out, slot_lse = lax.map(
        one_group,
        (
            key_in.reshape(-1, group_size, block_rows, heads_dev, HD),
            value_in.reshape(-1, group_size, block_rows, heads_dev, HD),
            slot_span.reshape(-1, group_size),
        ),
    )
    slot_out = slot_out.reshape(slot_count, block_rows, heads_dev, HD)
    slot_lse = slot_lse.reshape(slot_count, heads_dev, block_rows)
    own_out, own_lse = partial_state(query_blocks, key_blocks, value_blocks, True)
    live_pairs = is_live.reshape(per_dev, topk_count - 1)
    pair_out = (
        slot_out[slot_index]
        .reshape(per_dev, topk_count - 1, block_rows, heads_dev, HD)
        .astype(jnp.float32)
    )
    pair_lse = jnp.where(
        live_pairs[:, :, None, None],
        slot_lse[slot_index].reshape(per_dev, topk_count - 1, heads_dev, block_rows),
        -1e30,
    )
    highest = jnp.maximum(own_lse, jnp.max(pair_lse, axis=1))
    own_weight = jnp.exp(own_lse - highest)
    pair_weight = jnp.where(live_pairs[:, :, None, None], jnp.exp(pair_lse - highest[:, None]), 0.0)
    numerator = jnp.transpose(own_weight, (0, 2, 1))[..., None] * own_out
    numerator = numerator + jnp.sum(
        jnp.transpose(pair_weight, (0, 1, 3, 2))[..., None] * pair_out, axis=1
    )
    denominator = own_weight + jnp.sum(pair_weight, axis=1)
    attended = (numerator / jnp.transpose(denominator, (0, 2, 1))[..., None]).reshape(rows, width)
    squares = jnp.sum(attended * attended, axis=1)
    summed = lax.psum(squares, "head")
    factor = lax.rsqrt(summed / (HEADS * HD) + 1e-06)
    return (attended * factor[:, None] * norm_gain.astype(jnp.float32)[None, :]).astype(
        jnp.bfloat16
    )


SPLIT = (True, False, False, False)
ORDER = (
    ("p", 0),
    ("p", 1),
    ("w", "plan"),
    ("w", "near_down_keep_c0"),
    ("w", "far_down_keep_c0"),
    ("j", 0),
    ("w", "lift_keep_c0"),
    ("w", "served"),
    ("p", 2),
    ("j", 1),
    ("s", 0),
    ("j", 2),
    ("a", 0),
    ("p", 3),
    ("s", 1),
    ("m", 0),
    ("a", 1),
    ("j", 3),
    ("s", 2),
    ("m", 1),
    ("a", 2),
    ("s", 3),
    ("a", 3),
    ("m", 2),
    ("m", 3),
)
COSTS = {"pack": 2, "join": 1, "served": 6, "own": 5, "merge": 1, "finish": 3}
DIRECT = True
NOTE_ROWS = 16
UNROLL = 2
VMEM_LIMIT = 10 * 1024 * 1024


def unit_fields(code):
    return code & 31, (code >> 5) & 31, (code >> 10) & 63, (code >> 16) & 1, (code >> 17) & 1


def unit_code(slot, span, out, first, diagonal):
    return slot + span * 32 + out * 1024 + first * 65536 + diagonal * 131072


PIECES = {
    "head": lambda ref, h, rows: ref.at[h],
    "top rows": lambda ref, h, rows: ref.at[h, pl.ds(0, rows)],
    "queries": lambda ref, h, rows: ref.at[h, 0],
    "keys_values": lambda ref, h, rows: ref.at[h, pl.ds(1, 2)],
    "first": lambda ref, h, rows: ref.at[0, h],
    "second": lambda ref, h, rows: ref.at[1, h],
}


def attention_kernel(shape, own, groups, q_pieces, kv_pieces, n_in, plan, *refs):
    heads, per_dev, block_rows = shape
    n_q, n_kv = len(q_pieces), len(kv_pieces)
    inputs, refs = refs[:n_in], refs[n_in:]
    n_out = len(groups) + 2 * own
    outs, refs = refs[:n_out], refs[n_out:]
    (q_scr, kv_scr, s0, s1, p0, p1, d0, d1, acc_scr, top_scr, sum_scr, o_scr, lse_scr, sems) = refs[:14]
    s_scr, p_scr, decay_scr = (s0, s1), (p0, p1), (d0, d1)
    spans = n_q * per_dev
    copies = []
    for h in range(heads):
        for i, (n, kind) in enumerate(q_pieces):
            copies.append((PIECES[kind](inputs[n], h, per_dev * block_rows), q_scr.at[h, i], sems.at[h, i]))
        for i, (n, kind) in enumerate(kv_pieces):
            copies.append((PIECES[kind](inputs[n], h, per_dev * block_rows), kv_scr.at[h, i], sems.at[h, n_q + i]))
    copies = [pltpu.make_async_copy(*copy) for copy in copies]
    for copy in copies:
        copy.start()
    s1[...] = jnp.zeros_like(s1)
    p0[...] = jnp.zeros_like(p0)
    d0[...] = jnp.zeros_like(d0)
    d1[...] = jnp.zeros_like(d1)
    acc_scr[...] = jnp.zeros_like(acc_scr)
    top_scr[...] = jnp.zeros_like(top_scr)
    sum_scr[...] = jnp.ones_like(sum_scr)
    if own:
        bias_scr = refs[14]
        key_pos = lax.broadcasted_iota(jnp.int32, (block_rows, block_rows), 0)
        query_pos = lax.broadcasted_iota(jnp.int32, (block_rows, block_rows), 1)
        bias_scr[0] = jnp.zeros((block_rows, block_rows), jnp.float32)
        bias_scr[1] = jnp.where(key_pos <= query_pos, 0.0, -1e30)
    for copy in copies:
        copy.wait()

    def rows_of(i):
        return pl.ds(pl.multiple_of((i % per_dev) * block_rows, block_rows), block_rows)

    def step(h, at, now, acc, top, total):
        before = 1 - now
        for u in range(UNROLL):
            slot, _, out, _, _ = unit_fields(plan[at + u])
            vt = kv_scr[h, slot // per_dev, 1, rows_of(slot), :]
            vt = jnp.concatenate([vt[:HD], vt[HD:]], axis=1)
            mixed = jnp.dot(vt, p_scr[now][u], preferred_element_type=jnp.float32)
            acc = acc * decay_scr[now][u, 0:1, :] + mixed
            o_scr[out] = (acc * decay_scr[now][u, 1:2, :]).astype(o_scr.dtype)
        for u in range(UNROLL):
            _, _, out, first, _ = unit_fields(plan[at + UNROLL + u])
            s = s_scr[before][u]
            old = jnp.where(first == 1, -1e30, top)
            top = jnp.maximum(old, decay_scr[before][u, 2:3, :])
            decay = jnp.exp2((old - top) * EXP_SCALE)
            p = jnp.exp2((s - top) * EXP_SCALE)
            total = total * decay + jnp.sum(p, axis=0, keepdims=True)
            p_scr[before][u] = p.astype(jnp.bfloat16)
            decay_scr[before][u, 0:1, :] = decay
            decay_scr[before][u, 1:2, :] = 1.0 / total
            lse_scr[pl.ds(out, 1), :] = top * EXP_SCALE + jnp.log(total) * LOG2E
        for u in range(UNROLL):
            slot, span, _, _, diagonal = unit_fields(plan[at + 2 * UNROLL + u])
            k = kv_scr[h, slot // per_dev, 0, rows_of(slot), :]
            q = q_scr[h, span // per_dev, rows_of(span), :]
            s = lax.dot_general(k, q, (((1,), (1,)), ((), ())), preferred_element_type=jnp.float32)
            if own:
                s = s + bias_scr[diagonal]
            s_scr[now][u] = s
            decay_scr[now][u, 2:3, :] = jnp.max(s, axis=0, keepdims=True)
        return acc, top, total

    for h in range(heads):
        o_scr[...] = jnp.zeros_like(o_scr)
        lse_scr[...] = jnp.full_like(lse_scr, -1e30)

        def two_steps(i, carry):
            state = (acc_scr[...], top_scr[...], sum_scr[...])
            state = step(h, 1 + 2 * i * UNROLL, 0, *state)
            state = step(h, 1 + (2 * i + 1) * UNROLL, 1, *state)
            acc_scr[...], top_scr[...], sum_scr[...] = state
            return carry

        lax.fori_loop(0, (plan[0] + 1) // 2, two_steps, 0)
        if own:
            kept = outs[0].shape[1]
            outs[0][h] = o_scr[:kept]
            outs[1][h] = lse_scr[:kept, :]
        for out, (start, stop) in zip(outs[2 if own else 0 :], groups):
            n = stop - start
            for span in range(n):
                out[h, span * HD : (span + 1) * HD, :] = o_scr[start + span].astype(jnp.bfloat16)
            lse = lse_scr[start:stop, :]
            high = lse.astype(jnp.bfloat16).astype(jnp.float32)
            middle = (lse - high).astype(jnp.bfloat16).astype(jnp.float32)
            rest = jnp.zeros((lse_rows(n) - 3 * n, block_rows), jnp.float32)
            parts = jnp.concatenate([high, middle, lse - high - middle, rest], axis=0)
            out[h, n * HD :, :] = parts.astype(jnp.bfloat16)


def lse_rows(spans):
    return -(-3 * spans // 16) * 16


def unpacked_lse(ref, h, spans):
    parts = ref[h, spans * HD :, :].astype(jnp.float32)
    return parts[:spans] + parts[spans : 2 * spans] + parts[2 * spans : 3 * spans]


def cost(name):
    us = COSTS[name]
    return pl.CostEstimate(flops=int(us * 1e9) + 1, bytes_accessed=int(us * 3.4e6) + 1, transcendentals=0)


def ordered(kernel, n_after):
    def body(*refs):
        kernel(*refs[n_after:])

    return body


def attention_call(plan, q_pieces, kv_pieces, own, direct, heads, per_dev, block_rows, after=()):
    inputs = []

    def numbered(pieces):
        out = []
        for array, kind in pieces:
            if not any(array is known for known in inputs):
                inputs.append(array)
            out.append(([array is known for known in inputs].index(True), kind))
        return out

    q_pieces, kv_pieces = numbered(q_pieces), numbered(kv_pieces)
    n_q, n_kv = len(q_pieces), len(kv_pieces)
    spans = n_q * per_dev
    vmem, hbm = pl.BlockSpec(memory_space=pltpu.VMEM), pl.BlockSpec(memory_space=pltpu.HBM)
    f32, bf16 = jnp.float32, jnp.bfloat16
    if own:
        kept = per_dev if direct else spans
        groups = ((per_dev, spans),) if direct else ()
        out_shape = [
            jax.ShapeDtypeStruct((heads, kept, HD, block_rows), f32),
            jax.ShapeDtypeStruct((heads, kept, block_rows), f32),
        ]
    else:
        size = per_dev if direct else 2 * per_dev
        groups = tuple((start, start + size) for start in range(0, spans, size))
        out_shape = []
    for start, stop in groups:
        packed_rows = (stop - start) * HD + lse_rows(stop - start)
        out_shape.append(jax.ShapeDtypeStruct((heads, packed_rows, block_rows), bf16))
    scratch = [
        pltpu.VMEM((heads, n_q, per_dev * block_rows, HD), bf16),
        pltpu.VMEM((heads, n_kv, 2, per_dev * block_rows, HD), bf16),
        pltpu.VMEM((UNROLL, block_rows, block_rows), f32),
        pltpu.VMEM((UNROLL, block_rows, block_rows), f32),
        pltpu.VMEM((UNROLL, block_rows, block_rows), bf16),
        pltpu.VMEM((UNROLL, block_rows, block_rows), bf16),
        pltpu.VMEM((UNROLL, 8, block_rows), f32),
        pltpu.VMEM((UNROLL, 8, block_rows), f32),
        pltpu.VMEM((HD, block_rows), f32),
        pltpu.VMEM((1, block_rows), f32),
        pltpu.VMEM((1, block_rows), f32),
        pltpu.VMEM((spans + 1, HD, block_rows), f32 if own else bf16),
        pltpu.VMEM((spans + 8, block_rows), f32),
        pltpu.SemaphoreType.DMA((heads, n_q + n_kv)),
    ]
    if own:
        scratch.append(pltpu.VMEM((2, block_rows, block_rows), f32))
    return pl.pallas_call(
        ordered(
            partial(
                attention_kernel,
                (heads, per_dev, block_rows),
                own,
                groups,
                q_pieces,
                kv_pieces,
                len(inputs),
            ),
            len(after),
        ),
        out_shape=out_shape,
        in_specs=[hbm] * len(after) + [pl.BlockSpec(memory_space=pltpu.SMEM)] + [hbm] * len(inputs),
        out_specs=[vmem] * len(out_shape),
        scratch_shapes=scratch,
        compiler_params=pltpu.CompilerParams(vmem_limit_bytes=VMEM_LIMIT),
        cost_estimate=cost("own" if own else "served"),
        name="own_attention" if own else "served_attention",
    )(*after, plan, *inputs)


def pack_kernel(shape, place, q_ref, k_ref, v_ref, *refs):
    sides, head, half, rows, noted = shape
    n_out = len(sides) + noted
    note_ref, refs = (refs[0], refs[1:]) if noted else (None, refs)
    outs, (scr, t_scr, note_scr, sems) = refs[:n_out], refs[n_out:]
    loads, stores = {}, []
    for side in sides:
        start = pl.multiple_of((place[side] * half + head) * HD, HD)
        for i, ref in enumerate((q_ref, k_ref, v_ref)):
            loads[side, i] = pltpu.make_async_copy(
                ref.at[:, pl.ds(start, HD)], scr.at[side, i], sems.at[0, side, i]
            )
            loads[side, i].start()

    def store(source, target, side, i):
        copy = pltpu.make_async_copy(source, target, sems.at[1, side, i])
        copy.start()
        stores.append(copy)

    if noted:
        load = pltpu.make_async_copy(note_ref, note_scr, sems.at[0, 0, 3])
        load.start()
        load.wait()
        store(note_scr, outs[0].at[0, pl.ds(rows, NOTE_ROWS)], 0, 3)
    for side, out in zip(sides, outs[noted:]):
        targets = [out.at[0, i] for i in range(3)]
        if noted:
            targets = [outs[0].at[0, pl.ds(0, rows)], out.at[0, 0], out.at[0, 1]]
        for i in range(2):
            loads[side, i].wait()
            store(scr.at[side, i], targets[i], side, i)
        loads[side, 2].wait()
        for tile in range(rows // HD):
            at = slice(tile * HD, (tile + 1) * HD)
            t_scr[side, at, :] = scr[side, 2, at, :].T
        store(t_scr.at[side], targets[2], side, 2)
    for copy in stores:
        copy.wait()


def pack_call(place, queries, keys, values, head, half, sides=(1, 0), note=None, after=()):
    rows = queries.shape[0]
    hbm = pl.BlockSpec(memory_space=pltpu.HBM)
    bf16 = jnp.bfloat16
    queries, keys, values = (
        pltpu.with_memory_space_constraint(array, pltpu.HBM) for array in (queries, keys, values)
    )
    noted = note is not None
    if noted:
        shapes, notes = [(1, rows + NOTE_ROWS, HD), (1, 2, rows, HD)], [note]
    else:
        shapes, notes = [(1, 3, rows, HD)] * len(sides), []
    return pl.pallas_call(
        ordered(partial(pack_kernel, (sides, head, half, rows, noted)), len(after)),
        out_shape=[jax.ShapeDtypeStruct(shape, bf16) for shape in shapes],
        in_specs=[hbm] * len(after) + [pl.BlockSpec(memory_space=pltpu.SMEM)] + [hbm] * (3 + noted),
        out_specs=[hbm] * len(shapes),
        scratch_shapes=[
            pltpu.VMEM((2, 3, rows, HD), bf16),
            pltpu.VMEM((2, rows, HD), bf16),
            pltpu.VMEM((NOTE_ROWS, HD), bf16),
            pltpu.SemaphoreType.DMA((2, 2, 4)),
        ],
        compiler_params=pltpu.CompilerParams(vmem_limit_bytes=VMEM_LIMIT),
        cost_estimate=cost("pack"),
        name="pack",
    )(*after, place, queries, keys, values, *notes)


def cut_kernel(ref, q_ref, kv_ref, scr, sems):
    load = pltpu.make_async_copy(ref, scr, sems.at[0])
    load.start()
    load.wait()
    stores = [
        pltpu.make_async_copy(scr.at[0, 0], q_ref.at[0], sems.at[1]),
        pltpu.make_async_copy(scr.at[0, pl.ds(1, 2)], kv_ref.at[0], sems.at[2]),
    ]
    for store in stores:
        store.start()
    for store in stores:
        store.wait()


def cut_call(packed, after=()):
    _, _, rows, _ = packed.shape
    hbm = pl.BlockSpec(memory_space=pltpu.HBM)
    return pl.pallas_call(
        ordered(cut_kernel, len(after)),
        out_shape=(
            jax.ShapeDtypeStruct((1, rows, HD), jnp.bfloat16),
            jax.ShapeDtypeStruct((1, 2, rows, HD), jnp.bfloat16),
        ),
        in_specs=[hbm] * (len(after) + 1),
        out_specs=(hbm, hbm),
        scratch_shapes=[
            pltpu.VMEM(packed.shape, jnp.bfloat16),
            pltpu.SemaphoreType.DMA((3,)),
        ],
        compiler_params=pltpu.CompilerParams(vmem_limit_bytes=VMEM_LIMIT),
        cost_estimate=cost("join"),
        name="join",
    )(*after, packed)


def join_kernel(heads, keep_ref, swap_ref, q_ref, kv_ref, scr, sems):
    loads, stores = [], []
    for side, ref in enumerate((keep_ref, swap_ref)):
        for h in range(heads):
            loads.append(pltpu.make_async_copy(ref.at[h], scr.at[side, h], sems.at[0, side, h]))
            stores.append(
                (
                    pltpu.make_async_copy(scr.at[side, h, 0], q_ref.at[side, h], sems.at[1, side, h]),
                    pltpu.make_async_copy(
                        scr.at[side, h, pl.ds(1, 2)], kv_ref.at[side, h], sems.at[2, side, h]
                    ),
                )
            )
    for load in loads:
        load.start()
    for load, pair in zip(loads, stores):
        load.wait()
        for store in pair:
            store.start()
    for pair in stores:
        for store in pair:
            store.wait()


def join_call(keep, swapped, after=()):
    heads, _, rows, _ = keep.shape
    hbm = pl.BlockSpec(memory_space=pltpu.HBM)
    return pl.pallas_call(
        ordered(partial(join_kernel, heads), len(after)),
        out_shape=(
            jax.ShapeDtypeStruct((2, heads, rows, HD), jnp.bfloat16),
            jax.ShapeDtypeStruct((2, heads, 2, rows, HD), jnp.bfloat16),
        ),
        in_specs=[hbm] * (len(after) + 2),
        out_specs=(hbm, hbm),
        scratch_shapes=[
            pltpu.VMEM((2, heads, 3, rows, HD), jnp.bfloat16),
            pltpu.SemaphoreType.DMA((3, 2, heads)),
        ],
        compiler_params=pltpu.CompilerParams(vmem_limit_bytes=VMEM_LIMIT),
        cost_estimate=cost("join"),
        name="join",
    )(*after, keep, swapped)


def merge_kernel(per_dev, block_rows, sizes, valid, sofar_ref, *refs):
    inputs, (keep_ref, send_ref, squares_ref) = refs[:-3], refs[-3:]
    spans = 2 * per_dev
    squares_ref[...] = sofar_ref[...]
    at = 0
    for c, size in enumerate(sizes):
        own_ref, own_lse_ref, near_ref, far_ref = inputs[4 * c : 4 * c + 4]
        for h in range(size):
            lses = [own_lse_ref[h]]
            for i, ref in enumerate((near_ref, far_ref)):
                lses.append(jnp.where(valid[i] > 0, unpacked_lse(ref, h, spans), -1e30))
            top = jnp.maximum(jnp.maximum(lses[0], lses[1]), lses[2])
            weights = [jnp.exp2(lse - top) for lse in lses]
            scale = 1.0 / (weights[0] + weights[1] + weights[2])
            weights = [weight * scale for weight in weights]
            for span in range(spans):
                rows = slice(span, span + 1)
                tile = slice(span * HD, (span + 1) * HD)
                mixed = weights[0][rows, :] * own_ref[h, span]
                mixed = mixed + weights[1][rows, :] * near_ref[h, tile, :].astype(jnp.float32)
                mixed = mixed + weights[2][rows, :] * far_ref[h, tile, :].astype(jnp.float32)
                squares_ref[rows, :] = squares_ref[rows, :] + jnp.sum(mixed * mixed, axis=0, keepdims=True)
                target = keep_ref if span < per_dev else send_ref
                start = (span % per_dev) * block_rows
                target[at, start : start + block_rows, :] = mixed.T.astype(target.dtype)
            at += 1


def merge_call(valid, sofar, parts, per_dev, after=()):
    block_rows = sofar.shape[1]
    sizes = [own[0].shape[0] for own, _, _ in parts]
    arrays = [array for own, near, far in parts for array in (*own, near, far)]
    vmem = pl.BlockSpec(memory_space=pltpu.VMEM)
    hbm = pl.BlockSpec(memory_space=pltpu.HBM)
    packed = jax.ShapeDtypeStruct((sum(sizes), per_dev * block_rows, HD), jnp.bfloat16)
    return pl.pallas_call(
        ordered(partial(merge_kernel, per_dev, block_rows, sizes), len(after)),
        out_shape=(packed, packed, jax.ShapeDtypeStruct(sofar.shape, jnp.float32)),
        in_specs=[hbm] * len(after)
        + [pl.BlockSpec(memory_space=pltpu.SMEM)]
        + [vmem] * (1 + len(arrays)),
        out_specs=(vmem, vmem, vmem),
        compiler_params=pltpu.CompilerParams(vmem_limit_bytes=VMEM_LIMIT),
        cost_estimate=cost("merge"),
        name="merge",
    )(*after, valid, sofar, *arrays)


def own_merge_kernel(per_dev, block_rows, valid, sofar_ref, squares_in_ref, own_ref, own_lse_ref, *refs):
    other_ref, packs, outs, squares_ref = refs[0], refs[1:5], refs[5:7], refs[7]
    squares_ref[...] = sofar_ref[:per_dev, :] + squares_in_ref[...]
    for side in range(2):
        arrivals = (packs[side], packs[2 + side])
        lses = [unpacked_lse(other_ref, 0, per_dev) if side else own_lse_ref[0]]
        for i, ref in enumerate(arrivals):
            lses.append(jnp.where(valid[i] > 0, unpacked_lse(ref, 0, per_dev), -1e30))
        top = jnp.maximum(jnp.maximum(lses[0], lses[1]), lses[2])
        weights = [jnp.exp2(lse - top) for lse in lses]
        scale = 1.0 / (weights[0] + weights[1] + weights[2])
        weights = [weight * scale for weight in weights]
        for span in range(per_dev):
            rows = slice(span, span + 1)
            tile = slice(span * HD, (span + 1) * HD)
            mixed = other_ref[0, tile, :].astype(jnp.float32) if side else own_ref[0, span]
            mixed = weights[0][rows, :] * mixed
            for weight, ref in zip(weights[1:], arrivals):
                mixed = mixed + weight[rows, :] * ref[0, tile, :].astype(jnp.float32)
            squares_ref[rows, :] = squares_ref[rows, :] + jnp.sum(mixed * mixed, axis=0, keepdims=True)
            at = slice(span * block_rows, (span + 1) * block_rows)
            outs[side][0, at, :] = mixed.T.astype(jnp.bfloat16)


def own_merge_call(valid, sofar, squares_in, own, other, packs, per_dev, after=()):
    block_rows = sofar.shape[1]
    vmem = pl.BlockSpec(memory_space=pltpu.VMEM)
    hbm = pl.BlockSpec(memory_space=pltpu.HBM)
    packed = jax.ShapeDtypeStruct((1, per_dev * block_rows, HD), jnp.bfloat16)
    return pl.pallas_call(
        ordered(partial(own_merge_kernel, per_dev, block_rows), len(after)),
        out_shape=(packed, packed, jax.ShapeDtypeStruct((per_dev, block_rows), jnp.float32)),
        in_specs=[hbm] * len(after) + [pl.BlockSpec(memory_space=pltpu.SMEM)] + [vmem] * 9,
        out_specs=(vmem, vmem, vmem),
        compiler_params=pltpu.CompilerParams(vmem_limit_bytes=VMEM_LIMIT),
        cost_estimate=cost("merge"),
        name="merge",
    )(*after, valid, sofar, squares_in, *own, other, *packs)


def finish_kernel(per_dev, sizes, place, *refs):
    n = len(sizes)
    kept, returned = refs[:n], refs[n : 2 * n]
    squares_ref, gain_ref, out_ref, scr, sems = refs[2 * n :]
    copies = []
    block_rows = squares_ref.shape[1]
    half = sum(sizes)
    factor = lax.rsqrt(squares_ref[...] / (HEADS * HD) + 1e-06)
    for b in range(per_dev):
        column = jnp.broadcast_to(factor[b : b + 1, :], (HD, block_rows)).T
        rows = slice(b * block_rows, (b + 1) * block_rows)
        for side, pieces in enumerate((kept, returned)):
            head = 0
            for piece, size in zip(pieces, sizes):
                for h in range(size):
                    start = pl.multiple_of((place[side] * half + head) * HD, HD)
                    gain = gain_ref[:, pl.ds(start, HD)].astype(jnp.float32)
                    value = piece[h, rows, :].astype(jnp.float32) * column * gain
                    scr[rows, pl.ds(start, HD)] = value.astype(out_ref.dtype)
                    head += 1
        copy = pltpu.make_async_copy(scr.at[rows], out_ref.at[rows], sems.at[b])
        copy.start()
        copies.append(copy)
    for copy in copies:
        copy.wait()


def finish_call(place, kept, returned, squares, gain, per_dev):
    vmem = pl.BlockSpec(memory_space=pltpu.VMEM)
    rows, width = kept[0].shape[1], gain.shape[0]
    return pl.pallas_call(
        partial(finish_kernel, per_dev, [k.shape[0] for k in kept]),
        out_shape=jax.ShapeDtypeStruct((rows, width), jnp.bfloat16),
        in_specs=[pl.BlockSpec(memory_space=pltpu.SMEM)] + [vmem] * (2 * len(kept) + 2),
        out_specs=pl.BlockSpec(memory_space=pltpu.HBM),
        scratch_shapes=[
            pltpu.VMEM((rows, width), jnp.bfloat16),
            pltpu.SemaphoreType.DMA((per_dev,)),
        ],
        compiler_params=pltpu.CompilerParams(vmem_limit_bytes=VMEM_LIMIT),
        cost_estimate=cost("finish"),
        name="finish",
    )(place, *kept, *returned, squares, gain.reshape(1, width))


def plan_of(live, slot, diagonal, dump):
    spans, entries = live.shape
    t = jnp.arange(entries)
    earlier = jnp.sum((t[None, None, :] < t[None, :, None]) & live[:, None, :], axis=2)
    span = lax.broadcasted_iota(jnp.int32, live.shape, 0)
    code = unit_code(slot, span, span, (earlier == 0).astype(jnp.int32), diagonal)
    code, live = code.reshape(-1), live.reshape(-1)
    n = spans * entries
    i = jnp.arange(n)
    rank = jnp.sum((i[None, :] < i[:, None]) & live[None, :], axis=1)
    at = jnp.arange(n + 8 * UNROLL)
    hit = live[None, :] & (rank[None, :] + 2 * UNROLL == at[:, None])
    idle = unit_code(0, 0, dump, 1, 0)
    codes = jnp.sum(jnp.where(hit, code[None, :] - idle, 0), axis=1) + idle
    total = jnp.sum(live.astype(jnp.int32))
    steps = jnp.where(total > 0, (total + UNROLL - 1) // UNROLL + 2, 0)
    return jnp.concatenate([steps[None], codes]).astype(jnp.int32)


def level_shards(queries, keys, values, selection, norm_gain):
    device = lax.axis_index("ctx")
    level, x = device // 2, device % 2
    rows, width = queries.shape
    per_dev, topk = selection.shape
    block_rows = rows // per_dev
    spans = 2 * per_dev
    half = width // HD // 2

    sent = {}

    def to(array, pairs, name):
        with jax.named_scope(name):
            sent[name] = lax.ppermute(array, "ctx", pairs)
        return sent[name]

    swap = [(d, d ^ 1) for d in range(8)]
    lift = [(0, 2), (1, 3)]
    near_down, far_down = [(4, 2), (5, 3), (6, 4), (7, 5)], [(6, 2), (7, 3)]

    def crossed(pairs):
        return [(source, target ^ 1) for source, target in pairs]

    near_up, far_up = [(2, 4), (3, 5), (4, 6), (5, 7)], [(2, 6), (3, 7)]
    valid = jnp.stack([level >= 2, level >= 3]).astype(jnp.int32)
    place = jnp.stack([x, 1 - x]).astype(jnp.int32)

    own_selection = jnp.concatenate([selection, to(selection, swap, "selection_swap")], axis=0)
    note = jnp.zeros((NOTE_ROWS, HD), jnp.bfloat16)
    note = lax.dynamic_update_slice(note, own_selection.astype(jnp.bfloat16), (0, 0))

    def ids(at):
        first = jnp.stack([(at * 2 + x) * per_dev, (at * 2 + 1 - x) * per_dev])
        return (first[:, None] + jnp.arange(per_dev)[None, :]).reshape(-1, 1)

    def slots(blocks):
        owner = blocks // per_dev
        slot = jnp.where(owner // 2 == level, 0, spans) + jnp.where(owner % 2 == x, 0, per_dev)
        return owner // 2, slot + blocks % per_dev

    others = own_selection[:, 1:]
    block_level, slot = slots(others)
    live = (others != ids(level)) & ((block_level == level) | ((level == 1) & (block_level == 0)))
    first = jnp.ones((spans, 1), jnp.int32)
    own_plan = plan_of(
        jnp.concatenate([first > 0, live], axis=1),
        jnp.concatenate([jnp.arange(spans, dtype=jnp.int32)[:, None], slot], axis=1),
        jnp.concatenate([first, jnp.zeros_like(others)], axis=1),
        spans,
    )
    def served_lists(*noted):
        near_selection, far_selection = (
            array[0, rows : rows + spans, :topk].astype(jnp.int32) for array in noted
        )
        others = jnp.concatenate([near_selection, far_selection], axis=0)[:, 1:]
        block_level, slot = slots(others)
        is_near = lax.broadcasted_iota(jnp.int32, others.shape, 0) < spans
        mine = ((level == 1) & (block_level <= 1)) | ((level == 2) & (block_level == 2) & is_near)
        live = (others != jnp.concatenate([ids(level + 1), ids(level + 2)], axis=0)) & mine
        return plan_of(live, slot, jnp.zeros_like(others), 2 * spans)

    n, split, order = half, SPLIT, ORDER
    own_pieces, z_arrays, served_pieces, downs_of = {}, {}, {}, {}
    ups, owns, others, squares_in, kept, returned = {}, {}, {}, [], [], []
    squares = [jnp.zeros((spans, block_rows), jnp.float32)]
    last, served_plan = [], []

    def downs(q, kv, name):
        low = to(kv, lift, f"lift_{name}")
        far = to(q, far_down, f"far_down_{name}")
        return to(q, near_down, f"near_down_{name}"), far, low

    def pack(c):
        if split[c]:
            (send,) = pack_call(place, queries, keys, values, c, half, (1,), None, last)
            swapped = to(send, swap, f"swap_c{c}")
            q_keep, kv_keep = pack_call(
                place, queries, keys, values, c, half, (0,), note, (*last, send)
            )
            last[:] = [q_keep]
            downs_of[c] = downs(q_keep, kv_keep, f"keep_c{c}")
            served_plan.append(served_lists(*downs_of[c][:2]))
            z_arrays[c] = (swapped,)
            own_pieces[c] = (
                [(q_keep, "top rows"), (swapped, "queries")],
                [(kv_keep, "head"), (swapped, "keys_values")],
            )
        else:
            send, keep = pack_call(place, queries, keys, values, c, half, (1, 0), None, last)
            last[:] = [keep]
            z_arrays[c] = (keep, to(send, swap, f"swap_c{c}"))
            own_pieces[c] = (
                [(array, "queries") for array in z_arrays[c]],
                [(array, "keys_values") for array in z_arrays[c]],
            )

    def join(c):
        if split[c]:
            q_swap, kv_swap = cut_call(*z_arrays[c], last)
            last[:] = [q_swap]
            swaps = downs(q_swap, kv_swap, f"recv_c{c}")
            near, far, low = [
                [(k, kind), (r, "head")]
                for k, r, kind in zip(downs_of[c], swaps, ("top rows", "top rows", "head"))
            ]
        else:
            level_q, level_kv = join_call(*z_arrays[c], last)
            last[:] = [level_q]
            near, far, low = [
                [(array, "first"), (array, "second")] for array in downs(level_q, level_kv, f"c{c}")
            ]
        served_pieces[c] = (near + far, own_pieces[c][1] + low)

    def is_direct(c):
        return DIRECT and c == n - 1

    def serve(c):
        packs = attention_call(
            served_plan[0], *served_pieces[c], False, is_direct(c), 1, per_dev, block_rows, last
        )
        last[:] = [packs[0]]
        if is_direct(c):
            near_same, near_cross, far_same, far_cross = packs
            far = (
                to(far_same, far_up, f"far_up_same_c{c}"),
                to(far_cross, crossed(far_up), f"far_up_cross_c{c}"),
            )
            near = (
                to(near_same, near_up, f"near_up_same_c{c}"),
                to(near_cross, crossed(near_up), f"near_up_cross_c{c}"),
            )
            ups[c] = (*near, *far)
        else:
            near, far = packs
            far = to(far, far_up, f"far_up_c{c}")
            ups[c] = (to(near, near_up, f"near_up_c{c}"), far)

    def attend(c):
        state = attention_call(
            own_plan,
            own_pieces[c][0],
            served_pieces[c][1],
            True,
            is_direct(c),
            1,
            per_dev,
            block_rows,
            last,
        )
        last[:] = [state[1]]
        owns[c] = state[:2]
        if is_direct(c):
            others[c] = to(state[2], swap, f"back_own_c{c}")

    def merge(*chunks):
        if is_direct(chunks[0]):
            c = chunks[0]
            keep, back, squares[0] = own_merge_call(
                valid, squares[0], squares_in[0], owns[c], others[c], ups[c], per_dev, last
            )
            kept.append(keep)
            returned.append(back)
            return
        parts = [(owns[c], *ups[c]) for c in chunks]
        keep, send, squares[0] = merge_call(valid, squares[0], parts, per_dev, last)
        last[:] = [keep]
        kept.append(keep)
        returned.append(to(send, swap, f"back_c{chunks[0]}"))
        if DIRECT and chunks[-1] == n - 2:
            squares_in.append(to(squares[0][per_dev:], swap, "squares_swap"))

    steps = {"p": pack, "j": join, "s": serve, "a": attend, "m": merge}
    for what, *args in order:
        if what == "w":
            tokens = {"plan": own_plan, "served": served_plan and served_plan[0], **sent}
            last.append(tokens[args[0]])
        else:
            steps[what](*args)
    square = squares[0]
    if not DIRECT:
        square = square[:per_dev] + to(square[per_dev:], swap, "squares_swap")
    n_head = lax.axis_size("head")
    hop = 1
    while hop < n_head:
        square = square + lax.ppermute(square, "head", [(i, i ^ hop) for i in range(n_head)])
        hop *= 2
    return finish_call(place, kept, returned, square, norm_gain, per_dev)


def solution(mesh):
    placed = (P("ctx", "head"), P("ctx", "head"), P("ctx", "head"), P("ctx", None), P("head"))
    body = level_shards if mesh.shape["ctx"] == 8 else shards
    return jax.shard_map(
        body, mesh=mesh, in_specs=placed, out_specs=P("ctx", "head"), check_vma=False
    )
```

```python
from functools import partial
import math

import jax
import jax.numpy as jnp
from jax import lax
from jax.experimental import pallas as pl
from jax.experimental.pallas import tpu as pltpu
from jax.sharding import PartitionSpec as P

HEADS = 32
HD = 128
CAP = 2
LOG2E = math.log2(math.e)
EXP_SCALE = HD ** (-0.5) * LOG2E


def partial_state(query_rows, key_block, value_block, causal):
    scores = jnp.einsum(
        "sqhd,skhd->shqk", query_rows, key_block, preferred_element_type=jnp.float32
    ) * query_rows.shape[3] ** (-0.5)
    if causal:
        query_pos = lax.broadcasted_iota(jnp.int32, scores.shape, 2)
        key_pos = lax.broadcasted_iota(jnp.int32, scores.shape, 3)
        scores = jnp.where(key_pos <= query_pos, scores, -1e30)
    row_peak = jnp.max(scores, axis=3)
    exponentials = jnp.exp(scores - row_peak[..., None])
    row_sum = jnp.sum(exponentials, axis=3)
    weights = exponentials.astype(jnp.bfloat16)
    blended = jnp.einsum(
        "shqk,skhd->sqhd", weights, value_block, preferred_element_type=jnp.float32
    )
    blended = blended / jnp.transpose(row_sum, (0, 2, 1))[..., None]
    return (blended, row_peak + jnp.log(row_sum))


def slot_plan(selected, first_span, per_dev, capacity):
    own_span = first_span + lax.broadcasted_iota(jnp.int32, selected.shape, 0)
    is_live = (selected != own_span).reshape(-1)
    owner_dev = (selected // per_dev).reshape(-1)
    pair_count = owner_dev.shape[0]
    is_later = lax.broadcasted_iota(jnp.int32, (pair_count, pair_count), 0) > lax.broadcasted_iota(
        jnp.int32, (pair_count, pair_count), 1
    )
    earlier = is_later & (owner_dev[:, None] == owner_dev[None, :]) & is_live[None, :]
    slot_rank = jnp.sum(earlier.astype(jnp.int32), axis=1)
    slot_index = jnp.where(is_live, owner_dev * capacity + slot_rank, 0)
    return (slot_index, is_live, (selected % per_dev).reshape(-1))


def shards(queries, keys, values, selection, norm_gain):
    n_ctx = lax.axis_size("ctx")
    device = lax.axis_index("ctx")
    rows, width = queries.shape
    per_dev, topk_count = selection.shape
    block_rows = rows // per_dev
    heads_dev = width // HD
    slot_count = n_ctx * CAP
    group_size = math.gcd(slot_count, 4)
    query_blocks = queries.reshape(per_dev, block_rows, heads_dev, HD)
    key_blocks = keys.reshape(per_dev, block_rows, heads_dev, HD)
    value_blocks = values.reshape(per_dev, block_rows, heads_dev, HD)
    slot_index, is_live, local_block = slot_plan(selection[:, 1:], device * per_dev, per_dev, CAP)
    pair_count = slot_index.shape[0]
    pair_span = lax.broadcasted_iota(jnp.int32, (pair_count,), 0) // (topk_count - 1)
    slot_ids = lax.broadcasted_iota(jnp.int32, (slot_count, pair_count), 0)
    placed = (slot_ids == slot_index[None, :]) & is_live[None, :]
    slot_span = jnp.sum(jnp.where(placed, pair_span[None, :], 0), axis=1)
    everyone = lax.all_gather(selection, "ctx", axis=0, tiled=True)
    requests = everyone[:, 1:].reshape(n_ctx, per_dev, topk_count - 1)
    first_spans = lax.broadcasted_iota(jnp.int32, (n_ctx,), 0) * per_dev
    all_slots, all_live, all_local = jax.vmap(partial(slot_plan, per_dev=per_dev, capacity=CAP))(
        requests, first_spans
    )
    owner_devs = requests.reshape(n_ctx, -1) // per_dev
    served = all_live & (owner_devs == device)
    capacity_ids = lax.broadcasted_iota(jnp.int32, (1, CAP, 1), 1)
    matched = served[:, None, :] & (all_slots[:, None, :] == device * CAP + capacity_ids)
    send_block = jnp.sum(jnp.where(matched, all_local[:, None, :], 0), axis=2)
    key_out = key_blocks[send_block].reshape(n_ctx, CAP, block_rows, width)
    value_out = value_blocks[send_block].reshape(n_ctx, CAP, block_rows, width)
    key_in, value_in = (
        lax.all_to_all(key_out, "ctx", split_axis=0, concat_axis=0, tiled=True),
        lax.all_to_all(value_out, "ctx", split_axis=0, concat_axis=0, tiled=True),
    )

    def one_group(packed):
        group_keys, group_values, group_span = packed
        blended, log_sums = partial_state(query_blocks[group_span], group_keys, group_values, False)
        return (blended.astype(jnp.bfloat16), log_sums)

    slot_out, slot_lse = lax.map(
        one_group,
        (
            key_in.reshape(-1, group_size, block_rows, heads_dev, HD),
            value_in.reshape(-1, group_size, block_rows, heads_dev, HD),
            slot_span.reshape(-1, group_size),
        ),
    )
    slot_out = slot_out.reshape(slot_count, block_rows, heads_dev, HD)
    slot_lse = slot_lse.reshape(slot_count, heads_dev, block_rows)
    own_out, own_lse = partial_state(query_blocks, key_blocks, value_blocks, True)
    live_pairs = is_live.reshape(per_dev, topk_count - 1)
    pair_out = (
        slot_out[slot_index]
        .reshape(per_dev, topk_count - 1, block_rows, heads_dev, HD)
        .astype(jnp.float32)
    )
    pair_lse = jnp.where(
        live_pairs[:, :, None, None],
        slot_lse[slot_index].reshape(per_dev, topk_count - 1, heads_dev, block_rows),
        -1e30,
    )
    highest = jnp.maximum(own_lse, jnp.max(pair_lse, axis=1))
    own_weight = jnp.exp(own_lse - highest)
    pair_weight = jnp.where(live_pairs[:, :, None, None], jnp.exp(pair_lse - highest[:, None]), 0.0)
    numerator = jnp.transpose(own_weight, (0, 2, 1))[..., None] * own_out
    numerator = numerator + jnp.sum(
        jnp.transpose(pair_weight, (0, 1, 3, 2))[..., None] * pair_out, axis=1
    )
    denominator = own_weight + jnp.sum(pair_weight, axis=1)
    attended = (numerator / jnp.transpose(denominator, (0, 2, 1))[..., None]).reshape(rows, width)
    squares = jnp.sum(attended * attended, axis=1)
    summed = lax.psum(squares, "head")
    factor = lax.rsqrt(summed / (HEADS * HD) + 1e-06)
    return (attended * factor[:, None] * norm_gain.astype(jnp.float32)[None, :]).astype(
        jnp.bfloat16
    )


SPLIT = (True, False, False, False)
ORDER = (
    ("p", 0),
    ("p", 1),
    ("w", "plan"),
    ("w", "near_down_keep_c0"),
    ("w", "far_down_keep_c0"),
    ("j", 0),
    ("w", "lift_keep_c0"),
    ("w", "served"),
    ("p", 2),
    ("j", 1),
    ("s", 0),
    ("j", 2),
    ("a", 0),
    ("p", 3),
    ("s", 1),
    ("m", 0),
    ("a", 1),
    ("j", 3),
    ("s", 2),
    ("m", 1),
    ("a", 2),
    ("s", 3),
    ("a", 3),
    ("m", 2),
    ("m", 3),
)
COSTS = {"pack": 2, "join": 1, "served": 6, "own": 5, "merge": 1, "finish": 3}
DIRECT = True
NOTE_ROWS = 16
UNROLL = 2
VMEM_LIMIT = 10 * 1024 * 1024


def unit_fields(code):
    return code & 31, (code >> 5) & 31, (code >> 10) & 63, (code >> 16) & 1, (code >> 17) & 1


def unit_code(slot, span, out, first, diagonal):
    return slot + span * 32 + out * 1024 + first * 65536 + diagonal * 131072


PIECES = {
    "head": lambda ref, h, rows: ref.at[h],
    "top rows": lambda ref, h, rows: ref.at[h, pl.ds(0, rows)],
    "queries": lambda ref, h, rows: ref.at[h, 0],
    "keys_values": lambda ref, h, rows: ref.at[h, pl.ds(1, 2)],
    "first": lambda ref, h, rows: ref.at[0, h],
    "second": lambda ref, h, rows: ref.at[1, h],
}


def attention_kernel(shape, own, groups, q_pieces, kv_pieces, n_in, plan, *refs):
    heads, per_dev, block_rows = shape
    n_q, n_kv = len(q_pieces), len(kv_pieces)
    inputs, refs = refs[:n_in], refs[n_in:]
    n_out = len(groups) + 2 * own
    outs, refs = refs[:n_out], refs[n_out:]
    (q_scr, kv_scr, s0, s1, p0, p1, d0, d1, acc_scr, top_scr, sum_scr, o_scr, lse_scr, sems) = refs[:14]
    s_scr, p_scr, decay_scr = (s0, s1), (p0, p1), (d0, d1)
    spans = n_q * per_dev
    copies = []
    for h in range(heads):
        for i, (n, kind) in enumerate(q_pieces):
            copies.append((PIECES[kind](inputs[n], h, per_dev * block_rows), q_scr.at[h, i], sems.at[h, i]))
        for i, (n, kind) in enumerate(kv_pieces):
            copies.append((PIECES[kind](inputs[n], h, per_dev * block_rows), kv_scr.at[h, i], sems.at[h, n_q + i]))
    copies = [pltpu.make_async_copy(*copy) for copy in copies]
    for copy in copies:
        copy.start()
    s1[...] = jnp.zeros_like(s1)
    p0[...] = jnp.zeros_like(p0)
    d0[...] = jnp.zeros_like(d0)
    d1[...] = jnp.zeros_like(d1)
    acc_scr[...] = jnp.zeros_like(acc_scr)
    top_scr[...] = jnp.zeros_like(top_scr)
    sum_scr[...] = jnp.ones_like(sum_scr)
    if own:
        bias_scr = refs[14]
        key_pos = lax.broadcasted_iota(jnp.int32, (block_rows, block_rows), 0)
        query_pos = lax.broadcasted_iota(jnp.int32, (block_rows, block_rows), 1)
        bias_scr[0] = jnp.zeros((block_rows, block_rows), jnp.float32)
        bias_scr[1] = jnp.where(key_pos <= query_pos, 0.0, -1e30)
    def clear():
        if not own:
            o_scr[...] = jnp.zeros_like(o_scr)
            lse_scr[...] = jnp.full_like(lse_scr, -1e30)

    clear()
    for copy in copies:
        copy.wait()

    def rows_of(i):
        return pl.ds(pl.multiple_of((i % per_dev) * block_rows, block_rows), block_rows)

    def step(h, at, now, acc, top, total):
        before = 1 - now
        for u in range(UNROLL):
            slot, _, out, _, _ = unit_fields(plan[at + u])
            vt = kv_scr[h, slot // per_dev, 1, rows_of(slot), :]
            vt = jnp.concatenate([vt[:HD], vt[HD:]], axis=1)
            mixed = jnp.dot(vt, p_scr[now][u], preferred_element_type=jnp.float32)
            acc = acc * decay_scr[now][u, 0:1, :] + mixed
            o_scr[out] = (acc * decay_scr[now][u, 1:2, :]).astype(o_scr.dtype)
        for u in range(UNROLL):
            _, _, out, first, _ = unit_fields(plan[at + UNROLL + u])
            s = s_scr[before][u]
            old = jnp.where(first == 1, -1e30, top)
            top = jnp.maximum(old, decay_scr[before][u, 2:3, :])
            decay = jnp.exp2((old - top) * EXP_SCALE)
            p = jnp.exp2((s - top) * EXP_SCALE)
            total = total * decay + jnp.sum(p, axis=0, keepdims=True)
            p_scr[before][u] = p.astype(jnp.bfloat16)
            decay_scr[before][u, 0:1, :] = decay
            decay_scr[before][u, 1:2, :] = 1.0 / total
            lse_scr[pl.ds(out, 1), :] = top * EXP_SCALE + jnp.log(total) * LOG2E
        for u in range(UNROLL):
            slot, span, _, _, diagonal = unit_fields(plan[at + 2 * UNROLL + u])
            k = kv_scr[h, slot // per_dev, 0, rows_of(slot), :]
            q = q_scr[h, span // per_dev, rows_of(span), :]
            s = lax.dot_general(k, q, (((1,), (1,)), ((), ())), preferred_element_type=jnp.float32)
            if own:
                s = s + bias_scr[diagonal]
            s_scr[now][u] = s
            decay_scr[now][u, 2:3, :] = jnp.max(s, axis=0, keepdims=True)
        return acc, top, total

    for h in range(heads):
        if h:
            clear()

        def two_steps(i, carry):
            state = (acc_scr[...], top_scr[...], sum_scr[...])
            state = step(h, 1 + 2 * i * UNROLL, 0, *state)
            state = step(h, 1 + (2 * i + 1) * UNROLL, 1, *state)
            acc_scr[...], top_scr[...], sum_scr[...] = state
            return carry

        lax.fori_loop(0, (plan[0] + 1) // 2, two_steps, 0)
        if own:
            kept = outs[0].shape[1]
            outs[0][h] = o_scr[:kept]
            outs[1][h] = lse_scr[:kept, :]
        for out, (start, stop) in zip(outs[2 if own else 0 :], groups):
            n = stop - start
            for span in range(n):
                out[h, span * HD : (span + 1) * HD, :] = o_scr[start + span].astype(jnp.bfloat16)
            lse = lse_scr[start:stop, :]
            high = lse.astype(jnp.bfloat16).astype(jnp.float32)
            middle = (lse - high).astype(jnp.bfloat16).astype(jnp.float32)
            rest = jnp.zeros((lse_rows(n) - 3 * n, block_rows), jnp.float32)
            parts = jnp.concatenate([high, middle, lse - high - middle, rest], axis=0)
            out[h, n * HD :, :] = parts.astype(jnp.bfloat16)


def lse_rows(spans):
    return -(-3 * spans // 16) * 16


def unpacked_lse(ref, h, spans):
    parts = ref[h, spans * HD :, :].astype(jnp.float32)
    return parts[:spans] + parts[spans : 2 * spans] + parts[2 * spans : 3 * spans]


def cost(name):
    us = COSTS[name]
    return pl.CostEstimate(flops=int(us * 1e9) + 1, bytes_accessed=int(us * 3.4e6) + 1, transcendentals=0)


def ordered(kernel, n_after):
    def body(*refs):
        kernel(*refs[n_after:])

    return body


def attention_call(plan, q_pieces, kv_pieces, own, direct, heads, per_dev, block_rows, after=()):
    inputs = []

    def numbered(pieces):
        out = []
        for array, kind in pieces:
            if not any(array is known for known in inputs):
                inputs.append(array)
            out.append(([array is known for known in inputs].index(True), kind))
        return out

    q_pieces, kv_pieces = numbered(q_pieces), numbered(kv_pieces)
    n_q, n_kv = len(q_pieces), len(kv_pieces)
    spans = n_q * per_dev
    vmem, hbm = pl.BlockSpec(memory_space=pltpu.VMEM), pl.BlockSpec(memory_space=pltpu.HBM)
    f32, bf16 = jnp.float32, jnp.bfloat16
    if own:
        kept = per_dev if direct else spans
        groups = ((per_dev, spans),) if direct else ()
        out_shape = [
            jax.ShapeDtypeStruct((heads, kept, HD, block_rows), f32),
            jax.ShapeDtypeStruct((heads, kept, block_rows), f32),
        ]
    else:
        size = per_dev if direct else 2 * per_dev
        groups = tuple((start, start + size) for start in range(0, spans, size))
        out_shape = []
    for start, stop in groups:
        packed_rows = (stop - start) * HD + lse_rows(stop - start)
        out_shape.append(jax.ShapeDtypeStruct((heads, packed_rows, block_rows), bf16))
    scratch = [
        pltpu.VMEM((heads, n_q, per_dev * block_rows, HD), bf16),
        pltpu.VMEM((heads, n_kv, 2, per_dev * block_rows, HD), bf16),
        pltpu.VMEM((UNROLL, block_rows, block_rows), f32),
        pltpu.VMEM((UNROLL, block_rows, block_rows), f32),
        pltpu.VMEM((UNROLL, block_rows, block_rows), bf16),
        pltpu.VMEM((UNROLL, block_rows, block_rows), bf16),
        pltpu.VMEM((UNROLL, 8, block_rows), f32),
        pltpu.VMEM((UNROLL, 8, block_rows), f32),
        pltpu.VMEM((HD, block_rows), f32),
        pltpu.VMEM((1, block_rows), f32),
        pltpu.VMEM((1, block_rows), f32),
        pltpu.VMEM((spans + 1, HD, block_rows), f32 if own else bf16),
        pltpu.VMEM((spans + 8, block_rows), f32),
        pltpu.SemaphoreType.DMA((heads, n_q + n_kv)),
    ]
    if own:
        scratch.append(pltpu.VMEM((2, block_rows, block_rows), f32))
    return pl.pallas_call(
        ordered(
            partial(
                attention_kernel,
                (heads, per_dev, block_rows),
                own,
                groups,
                q_pieces,
                kv_pieces,
                len(inputs),
            ),
            len(after),
        ),
        out_shape=out_shape,
        in_specs=[hbm] * len(after) + [pl.BlockSpec(memory_space=pltpu.SMEM)] + [hbm] * len(inputs),
        out_specs=[vmem] * len(out_shape),
        scratch_shapes=scratch,
        compiler_params=pltpu.CompilerParams(vmem_limit_bytes=VMEM_LIMIT),
        cost_estimate=cost("own" if own else "served"),
        name="own_attention" if own else "served_attention",
    )(*after, plan, *inputs)


def pack_kernel(shape, place, q_ref, k_ref, v_ref, *refs):
    sides, head, half, rows, noted = shape
    n_out = len(sides) + noted
    note_ref, refs = (refs[0], refs[1:]) if noted else (None, refs)
    outs, (scr, t_scr, note_scr, sems) = refs[:n_out], refs[n_out:]
    loads, stores = {}, []
    for side in sides:
        start = pl.multiple_of((place[side] * half + head) * HD, HD)
        for i, ref in enumerate((q_ref, k_ref, v_ref)):
            loads[side, i] = pltpu.make_async_copy(
                ref.at[:, pl.ds(start, HD)], scr.at[side, i], sems.at[0, side, i]
            )
            loads[side, i].start()

    def store(source, target, side, i):
        copy = pltpu.make_async_copy(source, target, sems.at[1, side, i])
        copy.start()
        stores.append(copy)

    if noted:
        load = pltpu.make_async_copy(note_ref, note_scr, sems.at[0, 0, 3])
        load.start()
        load.wait()
        store(note_scr, outs[0].at[0, pl.ds(rows, NOTE_ROWS)], 0, 3)
    for side, out in zip(sides, outs[noted:]):
        targets = [out.at[0, i] for i in range(3)]
        if noted:
            targets = [outs[0].at[0, pl.ds(0, rows)], out.at[0, 0], out.at[0, 1]]
        for i in range(2):
            loads[side, i].wait()
            store(scr.at[side, i], targets[i], side, i)
        loads[side, 2].wait()
        for tile in range(rows // HD):
            at = slice(tile * HD, (tile + 1) * HD)
            t_scr[side, at, :] = scr[side, 2, at, :].T
        store(t_scr.at[side], targets[2], side, 2)
    for copy in stores:
        copy.wait()


def pack_call(place, queries, keys, values, head, half, sides=(1, 0), note=None, after=()):
    rows = queries.shape[0]
    hbm = pl.BlockSpec(memory_space=pltpu.HBM)
    bf16 = jnp.bfloat16
    queries, keys, values = (
        pltpu.with_memory_space_constraint(array, pltpu.HBM) for array in (queries, keys, values)
    )
    noted = note is not None
    if noted:
        shapes, notes = [(1, rows + NOTE_ROWS, HD), (1, 2, rows, HD)], [note]
    else:
        shapes, notes = [(1, 3, rows, HD)] * len(sides), []
    return pl.pallas_call(
        ordered(partial(pack_kernel, (sides, head, half, rows, noted)), len(after)),
        out_shape=[jax.ShapeDtypeStruct(shape, bf16) for shape in shapes],
        in_specs=[hbm] * len(after) + [pl.BlockSpec(memory_space=pltpu.SMEM)] + [hbm] * (3 + noted),
        out_specs=[hbm] * len(shapes),
        scratch_shapes=[
            pltpu.VMEM((2, 3, rows, HD), bf16),
            pltpu.VMEM((2, rows, HD), bf16),
            pltpu.VMEM((NOTE_ROWS, HD), bf16),
            pltpu.SemaphoreType.DMA((2, 2, 4)),
        ],
        compiler_params=pltpu.CompilerParams(vmem_limit_bytes=VMEM_LIMIT),
        cost_estimate=cost("pack"),
        name="pack",
    )(*after, place, queries, keys, values, *notes)


def cut_kernel(ref, q_ref, kv_ref, scr, sems):
    load = pltpu.make_async_copy(ref, scr, sems.at[0])
    load.start()
    load.wait()
    stores = [
        pltpu.make_async_copy(scr.at[0, 0], q_ref.at[0], sems.at[1]),
        pltpu.make_async_copy(scr.at[0, pl.ds(1, 2)], kv_ref.at[0], sems.at[2]),
    ]
    for store in stores:
        store.start()
    for store in stores:
        store.wait()


def cut_call(packed, after=()):
    _, _, rows, _ = packed.shape
    hbm = pl.BlockSpec(memory_space=pltpu.HBM)
    return pl.pallas_call(
        ordered(cut_kernel, len(after)),
        out_shape=(
            jax.ShapeDtypeStruct((1, rows, HD), jnp.bfloat16),
            jax.ShapeDtypeStruct((1, 2, rows, HD), jnp.bfloat16),
        ),
        in_specs=[hbm] * (len(after) + 1),
        out_specs=(hbm, hbm),
        scratch_shapes=[
            pltpu.VMEM(packed.shape, jnp.bfloat16),
            pltpu.SemaphoreType.DMA((3,)),
        ],
        compiler_params=pltpu.CompilerParams(vmem_limit_bytes=VMEM_LIMIT),
        cost_estimate=cost("join"),
        name="join",
    )(*after, packed)


def join_kernel(heads, keep_ref, swap_ref, q_ref, kv_ref, scr, sems):
    loads, stores = [], []
    for side, ref in enumerate((keep_ref, swap_ref)):
        for h in range(heads):
            loads.append(pltpu.make_async_copy(ref.at[h], scr.at[side, h], sems.at[0, side, h]))
            stores.append(
                (
                    pltpu.make_async_copy(scr.at[side, h, 0], q_ref.at[side, h], sems.at[1, side, h]),
                    pltpu.make_async_copy(
                        scr.at[side, h, pl.ds(1, 2)], kv_ref.at[side, h], sems.at[2, side, h]
                    ),
                )
            )
    for load in loads:
        load.start()
    for load, pair in zip(loads, stores):
        load.wait()
        for store in pair:
            store.start()
    for pair in stores:
        for store in pair:
            store.wait()


def join_call(keep, swapped, after=()):
    heads, _, rows, _ = keep.shape
    hbm = pl.BlockSpec(memory_space=pltpu.HBM)
    return pl.pallas_call(
        ordered(partial(join_kernel, heads), len(after)),
        out_shape=(
            jax.ShapeDtypeStruct((2, heads, rows, HD), jnp.bfloat16),
            jax.ShapeDtypeStruct((2, heads, 2, rows, HD), jnp.bfloat16),
        ),
        in_specs=[hbm] * (len(after) + 2),
        out_specs=(hbm, hbm),
        scratch_shapes=[
            pltpu.VMEM((2, heads, 3, rows, HD), jnp.bfloat16),
            pltpu.SemaphoreType.DMA((3, 2, heads)),
        ],
        compiler_params=pltpu.CompilerParams(vmem_limit_bytes=VMEM_LIMIT),
        cost_estimate=cost("join"),
        name="join",
    )(*after, keep, swapped)


def merge_kernel(per_dev, block_rows, sizes, valid, sofar_ref, *refs):
    inputs, (keep_ref, send_ref, squares_ref) = refs[:-3], refs[-3:]
    spans = 2 * per_dev
    squares_ref[...] = sofar_ref[...]
    at = 0
    for c, size in enumerate(sizes):
        own_ref, own_lse_ref, near_ref, far_ref = inputs[4 * c : 4 * c + 4]
        for h in range(size):
            lses = [own_lse_ref[h]]
            for i, ref in enumerate((near_ref, far_ref)):
                lses.append(jnp.where(valid[i] > 0, unpacked_lse(ref, h, spans), -1e30))
            top = jnp.maximum(jnp.maximum(lses[0], lses[1]), lses[2])
            weights = [jnp.exp2(lse - top) for lse in lses]
            scale = 1.0 / (weights[0] + weights[1] + weights[2])
            weights = [weight * scale for weight in weights]
            for span in range(spans):
                rows = slice(span, span + 1)
                tile = slice(span * HD, (span + 1) * HD)
                mixed = weights[0][rows, :] * own_ref[h, span]
                mixed = mixed + weights[1][rows, :] * near_ref[h, tile, :].astype(jnp.float32)
                mixed = mixed + weights[2][rows, :] * far_ref[h, tile, :].astype(jnp.float32)
                squares_ref[rows, :] = squares_ref[rows, :] + jnp.sum(mixed * mixed, axis=0, keepdims=True)
                target = keep_ref if span < per_dev else send_ref
                start = (span % per_dev) * block_rows
                target[at, start : start + block_rows, :] = mixed.T.astype(target.dtype)
            at += 1


def merge_call(valid, sofar, parts, per_dev, after=()):
    block_rows = sofar.shape[1]
    sizes = [own[0].shape[0] for own, _, _ in parts]
    arrays = [array for own, near, far in parts for array in (*own, near, far)]
    vmem = pl.BlockSpec(memory_space=pltpu.VMEM)
    hbm = pl.BlockSpec(memory_space=pltpu.HBM)
    packed = jax.ShapeDtypeStruct((sum(sizes), per_dev * block_rows, HD), jnp.bfloat16)
    return pl.pallas_call(
        ordered(partial(merge_kernel, per_dev, block_rows, sizes), len(after)),
        out_shape=(packed, packed, jax.ShapeDtypeStruct(sofar.shape, jnp.float32)),
        in_specs=[hbm] * len(after)
        + [pl.BlockSpec(memory_space=pltpu.SMEM)]
        + [vmem] * (1 + len(arrays)),
        out_specs=(vmem, vmem, vmem),
        compiler_params=pltpu.CompilerParams(vmem_limit_bytes=VMEM_LIMIT),
        cost_estimate=cost("merge"),
        name="merge",
    )(*after, valid, sofar, *arrays)


def own_merge_kernel(per_dev, block_rows, valid, sofar_ref, squares_in_ref, own_ref, own_lse_ref, *refs):
    other_ref, packs, outs, squares_ref = refs[0], refs[1:5], refs[5:7], refs[7]
    squares_ref[...] = sofar_ref[:per_dev, :] + squares_in_ref[...]
    for side in range(2):
        arrivals = (packs[side], packs[2 + side])
        lses = [unpacked_lse(other_ref, 0, per_dev) if side else own_lse_ref[0]]
        for i, ref in enumerate(arrivals):
            lses.append(jnp.where(valid[i] > 0, unpacked_lse(ref, 0, per_dev), -1e30))
        top = jnp.maximum(jnp.maximum(lses[0], lses[1]), lses[2])
        weights = [jnp.exp2(lse - top) for lse in lses]
        scale = 1.0 / (weights[0] + weights[1] + weights[2])
        weights = [weight * scale for weight in weights]
        for span in range(per_dev):
            rows = slice(span, span + 1)
            tile = slice(span * HD, (span + 1) * HD)
            mixed = other_ref[0, tile, :].astype(jnp.float32) if side else own_ref[0, span]
            mixed = weights[0][rows, :] * mixed
            for weight, ref in zip(weights[1:], arrivals):
                mixed = mixed + weight[rows, :] * ref[0, tile, :].astype(jnp.float32)
            squares_ref[rows, :] = squares_ref[rows, :] + jnp.sum(mixed * mixed, axis=0, keepdims=True)
            at = slice(span * block_rows, (span + 1) * block_rows)
            outs[side][0, at, :] = mixed.T.astype(jnp.bfloat16)


def own_merge_call(valid, sofar, squares_in, own, other, packs, per_dev, after=()):
    block_rows = sofar.shape[1]
    vmem = pl.BlockSpec(memory_space=pltpu.VMEM)
    hbm = pl.BlockSpec(memory_space=pltpu.HBM)
    packed = jax.ShapeDtypeStruct((1, per_dev * block_rows, HD), jnp.bfloat16)
    return pl.pallas_call(
        ordered(partial(own_merge_kernel, per_dev, block_rows), len(after)),
        out_shape=(packed, packed, jax.ShapeDtypeStruct((per_dev, block_rows), jnp.float32)),
        in_specs=[hbm] * len(after) + [pl.BlockSpec(memory_space=pltpu.SMEM)] + [vmem] * 9,
        out_specs=(vmem, vmem, vmem),
        compiler_params=pltpu.CompilerParams(vmem_limit_bytes=VMEM_LIMIT),
        cost_estimate=cost("merge"),
        name="merge",
    )(*after, valid, sofar, squares_in, *own, other, *packs)


def finish_kernel(per_dev, sizes, place, *refs):
    n = len(sizes)
    kept, returned = refs[:n], refs[n : 2 * n]
    squares_ref, gain_ref, out_ref, scr, sems = refs[2 * n :]
    copies = []
    block_rows = squares_ref.shape[1]
    half = sum(sizes)
    factor = lax.rsqrt(squares_ref[...] / (HEADS * HD) + 1e-06)
    for b in range(per_dev):
        column = jnp.broadcast_to(factor[b : b + 1, :], (HD, block_rows)).T
        rows = slice(b * block_rows, (b + 1) * block_rows)
        for side, pieces in enumerate((kept, returned)):
            head = 0
            for piece, size in zip(pieces, sizes):
                for h in range(size):
                    start = pl.multiple_of((place[side] * half + head) * HD, HD)
                    gain = gain_ref[:, pl.ds(start, HD)].astype(jnp.float32)
                    value = piece[h, rows, :].astype(jnp.float32) * column * gain
                    scr[rows, pl.ds(start, HD)] = value.astype(out_ref.dtype)
                    head += 1
        copy = pltpu.make_async_copy(scr.at[rows], out_ref.at[rows], sems.at[b])
        copy.start()
        copies.append(copy)
    for copy in copies:
        copy.wait()


def finish_call(place, kept, returned, squares, gain, per_dev):
    vmem = pl.BlockSpec(memory_space=pltpu.VMEM)
    rows, width = kept[0].shape[1], gain.shape[0]
    return pl.pallas_call(
        partial(finish_kernel, per_dev, [k.shape[0] for k in kept]),
        out_shape=jax.ShapeDtypeStruct((rows, width), jnp.bfloat16),
        in_specs=[pl.BlockSpec(memory_space=pltpu.SMEM)] + [vmem] * (2 * len(kept) + 2),
        out_specs=pl.BlockSpec(memory_space=pltpu.HBM),
        scratch_shapes=[
            pltpu.VMEM((rows, width), jnp.bfloat16),
            pltpu.SemaphoreType.DMA((per_dev,)),
        ],
        compiler_params=pltpu.CompilerParams(vmem_limit_bytes=VMEM_LIMIT),
        cost_estimate=cost("finish"),
        name="finish",
    )(place, *kept, *returned, squares, gain.reshape(1, width))


def plan_of(live, slot, diagonal, dump):
    spans, entries = live.shape
    t = jnp.arange(entries)
    earlier = jnp.sum((t[None, None, :] < t[None, :, None]) & live[:, None, :], axis=2)
    span = lax.broadcasted_iota(jnp.int32, live.shape, 0)
    code = unit_code(slot, span, span, (earlier == 0).astype(jnp.int32), diagonal)
    code, live = code.reshape(-1), live.reshape(-1)
    n = spans * entries
    i = jnp.arange(n)
    rank = jnp.sum((i[None, :] < i[:, None]) & live[None, :], axis=1)
    at = jnp.arange(n + 8 * UNROLL)
    hit = live[None, :] & (rank[None, :] + 2 * UNROLL == at[:, None])
    idle = unit_code(0, 0, dump, 1, 0)
    codes = jnp.sum(jnp.where(hit, code[None, :] - idle, 0), axis=1) + idle
    total = jnp.sum(live.astype(jnp.int32))
    steps = jnp.where(total > 0, (total + UNROLL - 1) // UNROLL + 2, 0)
    return jnp.concatenate([steps[None], codes]).astype(jnp.int32)


def level_shards(queries, keys, values, selection, norm_gain):
    device = lax.axis_index("ctx")
    level, x = device // 2, device % 2
    rows, width = queries.shape
    per_dev, topk = selection.shape
    block_rows = rows // per_dev
    spans = 2 * per_dev
    half = width // HD // 2

    sent = {}

    def to(array, pairs, name):
        with jax.named_scope(name):
            sent[name] = lax.ppermute(array, "ctx", pairs)
        return sent[name]

    swap = [(d, d ^ 1) for d in range(8)]
    lift = [(0, 2), (1, 3)]
    near_down, far_down = [(4, 2), (5, 3), (6, 4), (7, 5)], [(6, 2), (7, 3)]

    def crossed(pairs):
        return [(source, target ^ 1) for source, target in pairs]

    near_up, far_up = [(2, 4), (3, 5), (4, 6), (5, 7)], [(2, 6), (3, 7)]
    valid = jnp.stack([level >= 2, level >= 3]).astype(jnp.int32)
    place = jnp.stack([x, 1 - x]).astype(jnp.int32)

    own_selection = jnp.concatenate([selection, to(selection, swap, "selection_swap")], axis=0)
    note = jnp.zeros((NOTE_ROWS, HD), jnp.bfloat16)
    note = lax.dynamic_update_slice(note, own_selection.astype(jnp.bfloat16), (0, 0))

    def ids(at):
        first = jnp.stack([(at * 2 + x) * per_dev, (at * 2 + 1 - x) * per_dev])
        return (first[:, None] + jnp.arange(per_dev)[None, :]).reshape(-1, 1)

    def slots(blocks):
        owner = blocks // per_dev
        slot = jnp.where(owner // 2 == level, 0, spans) + jnp.where(owner % 2 == x, 0, per_dev)
        return owner // 2, slot + blocks % per_dev

    others = own_selection[:, 1:]
    block_level, slot = slots(others)
    live = (others != ids(level)) & ((block_level == level) | ((level == 1) & (block_level == 0)))
    first = jnp.ones((spans, 1), jnp.int32)
    own_plan = plan_of(
        jnp.concatenate([first > 0, live], axis=1),
        jnp.concatenate([jnp.arange(spans, dtype=jnp.int32)[:, None], slot], axis=1),
        jnp.concatenate([first, jnp.zeros_like(others)], axis=1),
        spans,
    )
    def served_lists(*noted):
        near_selection, far_selection = (
            array[0, rows : rows + spans, :topk].astype(jnp.int32) for array in noted
        )
        others = jnp.concatenate([near_selection, far_selection], axis=0)[:, 1:]
        block_level, slot = slots(others)
        is_near = lax.broadcasted_iota(jnp.int32, others.shape, 0) < spans
        mine = ((level == 1) & (block_level <= 1)) | ((level == 2) & (block_level == 2) & is_near)
        live = (others != jnp.concatenate([ids(level + 1), ids(level + 2)], axis=0)) & mine
        return plan_of(live, slot, jnp.zeros_like(others), 2 * spans)

    n, split, order = half, SPLIT, ORDER
    own_pieces, z_arrays, served_pieces, downs_of = {}, {}, {}, {}
    ups, owns, others, squares_in, kept, returned = {}, {}, {}, [], [], []
    squares = [jnp.zeros((spans, block_rows), jnp.float32)]
    last, served_plan = [], []

    def downs(q, kv, name):
        low = to(kv, lift, f"lift_{name}")
        far = to(q, far_down, f"far_down_{name}")
        return to(q, near_down, f"near_down_{name}"), far, low

    def pack(c):
        if split[c]:
            (send,) = pack_call(place, queries, keys, values, c, half, (1,), None, last)
            swapped = to(send, swap, f"swap_c{c}")
            q_keep, kv_keep = pack_call(
                place, queries, keys, values, c, half, (0,), note, (*last, send)
            )
            last[:] = [q_keep]
            downs_of[c] = downs(q_keep, kv_keep, f"keep_c{c}")
            served_plan.append(served_lists(*downs_of[c][:2]))
            z_arrays[c] = (swapped,)
            own_pieces[c] = (
                [(q_keep, "top rows"), (swapped, "queries")],
                [(kv_keep, "head"), (swapped, "keys_values")],
            )
        else:
            send, keep = pack_call(place, queries, keys, values, c, half, (1, 0), None, last)
            last[:] = [keep]
            z_arrays[c] = (keep, to(send, swap, f"swap_c{c}"))
            own_pieces[c] = (
                [(array, "queries") for array in z_arrays[c]],
                [(array, "keys_values") for array in z_arrays[c]],
            )

    def join(c):
        if split[c]:
            q_swap, kv_swap = cut_call(*z_arrays[c], last)
            last[:] = [q_swap]
            swaps = downs(q_swap, kv_swap, f"recv_c{c}")
            near, far, low = [
                [(k, kind), (r, "head")]
                for k, r, kind in zip(downs_of[c], swaps, ("top rows", "top rows", "head"))
            ]
        else:
            level_q, level_kv = join_call(*z_arrays[c], last)
            last[:] = [level_q]
            near, far, low = [
                [(array, "first"), (array, "second")] for array in downs(level_q, level_kv, f"c{c}")
            ]
        served_pieces[c] = (near + far, own_pieces[c][1] + low)

    def is_direct(c):
        return DIRECT and c == n - 1

    def serve(c):
        packs = attention_call(
            served_plan[0], *served_pieces[c], False, is_direct(c), 1, per_dev, block_rows, last
        )
        last[:] = [packs[0]]
        if is_direct(c):
            near_same, near_cross, far_same, far_cross = packs
            far = (
                to(far_same, far_up, f"far_up_same_c{c}"),
                to(far_cross, crossed(far_up), f"far_up_cross_c{c}"),
            )
            near = (
                to(near_same, near_up, f"near_up_same_c{c}"),
                to(near_cross, crossed(near_up), f"near_up_cross_c{c}"),
            )
            ups[c] = (*near, *far)
        else:
            near, far = packs
            far = to(far, far_up, f"far_up_c{c}")
            ups[c] = (to(near, near_up, f"near_up_c{c}"), far)

    def attend(c):
        state = attention_call(
            own_plan,
            own_pieces[c][0],
            served_pieces[c][1],
            True,
            is_direct(c),
            1,
            per_dev,
            block_rows,
            last,
        )
        last[:] = [state[1]]
        owns[c] = state[:2]
        if is_direct(c):
            others[c] = to(state[2], swap, f"back_own_c{c}")

    def merge(*chunks):
        if is_direct(chunks[0]):
            c = chunks[0]
            keep, back, squares[0] = own_merge_call(
                valid, squares[0], squares_in[0], owns[c], others[c], ups[c], per_dev, last
            )
            kept.append(keep)
            returned.append(back)
            return
        parts = [(owns[c], *ups[c]) for c in chunks]
        keep, send, squares[0] = merge_call(valid, squares[0], parts, per_dev, last)
        last[:] = [keep]
        kept.append(keep)
        returned.append(to(send, swap, f"back_c{chunks[0]}"))
        if DIRECT and chunks[-1] == n - 2:
            squares_in.append(to(squares[0][per_dev:], swap, "squares_swap"))

    steps = {"p": pack, "j": join, "s": serve, "a": attend, "m": merge}
    for what, *args in order:
        if what == "w":
            tokens = {"plan": own_plan, "served": served_plan and served_plan[0], **sent}
            last.append(tokens[args[0]])
        else:
            steps[what](*args)
    square = squares[0]
    if not DIRECT:
        square = square[:per_dev] + to(square[per_dev:], swap, "squares_swap")
    n_head = lax.axis_size("head")
    hop = 1
    while hop < n_head:
        square = square + lax.ppermute(square, "head", [(i, i ^ hop) for i in range(n_head)])
        hop *= 2
    return finish_call(place, kept, returned, square, norm_gain, per_dev)


def solution(mesh):
    placed = (P("ctx", "head"), P("ctx", "head"), P("ctx", "head"), P("ctx", None), P("head"))
    body = level_shards if mesh.shape["ctx"] == 8 else shards
    return jax.shard_map(
        body, mesh=mesh, in_specs=placed, out_specs=P("ctx", "head"), check_vma=False
    )
```
